32 devices in a mesh: grp: 4 (over y, core), row: 8 (over z, x).
Axes of the slice: x: 2, y: 2, z: 4, core: 2. Of those that a mesh axis runs over, the one named last changes fastest.
Arguments:
- stiffness: bfloat16 [7, 2, 192, 192], replicated, may hold values from -0.4375 to 0.4375
- lame: float32 [768, 7, 2], P(('grp', 'row')), may hold values from 0.3 to 3
- prolong: bfloat16 [768, 24, 192], P(('grp', 'row')), may hold values from -0.4375 to 0.4375
- columns: int32 [768, 7], P(('grp', 'row')), may hold values from -1 to 47, as said below
- ghost_count: int32 [32, 2], P(('grp', 'row')), may hold values from 1 to 12
- ghost_offset: int32 [32, 2], P(('grp', 'row')), may hold values from 0 to 23, as said below
- owner_map: int32 [768, 1], P(('grp', 'row')), may hold values from 0 to 3; in each aligned block of 24 rows (0 to 23, 24 to 47, ...) at most 12 rows name the same one
Outputs:
- coarse_rows: bfloat16 [1536, 24, 168], P(('grp', 'row'))
- coarse_ids: int32 [1536], P(('grp', 'row'))
The draws below stay inside these ranges and needn't reach their ends.
Inputs may be any that keep to these rules, and one draw needn't show every extreme that they name: `columns`: slot 0 of every row names the row's own element; -1 marks an empty slot. ghost_offset + ghost_count <= 24 entry by entry. `owner_map`: at most 12 elements of one device name the same subgroup index.
All inputs are finite; a program needn't handle non-finite values.
Results may differ from the reference program's by a relative error of at most 0.001.
Values may be sent and summed in bfloat16 or wider, within the bound.
No kernel may reach another device: no remote copies, remote signals or barrier semaphores. Data moves between devices by JAX's collectives and lax.ppermute only.
A program may use at most 64 MiB of HBM per device.

```python
import math
import jax
import jax.numpy as jnp
import numpy as np
from jax import lax

FB = 192
CB = 24
NB = 7
ELEM_DEV = 24
GHOSTS = 12
CAP = 12
ELEMENTS = 768
N_GRP = 4
N_ROW = 8


def ghost_plan(key):
    device_total = ELEMENTS // ELEM_DEV
    key_counts, key_offsets, key_chosen = jax.random.split(key, 3)
    counts = jax.random.randint(key_counts, (device_total, 2), 1, GHOSTS + 1)
    chosen = jax.random.randint(key_chosen, (), 0, device_total)
    device_rows = jnp.arange(device_total)[:, None]
    fixed_counts = jnp.array([[GHOSTS, 1]], dtype=jnp.int32)
    counts = jnp.where(device_rows == chosen, fixed_counts, counts)
    offsets = jax.random.randint(key_offsets, (device_total, 2), 0, ELEM_DEV - counts + 1)
    fixed_offsets = jnp.array([[0, ELEM_DEV - 1]], dtype=jnp.int32)
    offsets = jnp.where(device_rows == chosen, fixed_offsets, offsets)
    return (counts.astype(jnp.int32), offsets.astype(jnp.int32))


def draw_ghost_count(key, part):
    counts, offsets = ghost_plan(key)
    return counts


def draw_ghost_offset(key, part):
    counts, offsets = ghost_plan(key)
    return offsets


def draw_columns(key, part):
    key = jax.random.fold_in(key, 5)
    column_span = ELEM_DEV + 2 * GHOSTS
    others = jax.random.randint(key, (ELEMENTS, NB - 1), -1, column_span)
    own_index = (jnp.arange(ELEMENTS) % ELEM_DEV)[:, None]
    result = jnp.concatenate([own_index, others], axis=1)
    result = result.at[0, NB - 1].set(column_span - 1)
    return result.astype(jnp.int32)


def steps_of(key, dims, shards, least, largest):
    gain = 1.0
    for dim, parts in shards:
        heights = jax.random.uniform(jax.random.fold_in(jax.random.fold_in(key, 6), dim), (parts,), jnp.float32, least / len(shards), largest / len(shards))
        gain = gain * jnp.repeat(jnp.exp(heights), dims[dim] // parts).reshape((-1,) + (1,) * (len(dims) - 1 - dim))
    return gain


def shared_out(rng, own, number, rows, amount, top, reach, lean):
    ranking = jax.random.permutation(rng, amount)
    heavy_load, ordinary = portions_of(amount, rows * top, reach, lean, True), portions_of(amount, rows * top, reach, lean, False)
    places = jnp.arange(amount)

    def named(lengths, turn):
        used = int((lengths > 0).sum())
        fixed = max(1, used // 4)
        moved = fixed + (places - fixed + turn * (used - fixed)) % max(1, amount - fixed)
        return jnp.zeros((amount,), jnp.int32).at[ranking[jnp.where(places < fixed, places, moved)]].set(jnp.asarray(lengths, jnp.int32))

    lengths = jnp.where(number % 4 == 0, named(heavy_load, number // 4), named(ordinary, number - number // 4 - 1))
    mixed = jax.random.permutation(jax.random.fold_in(own, 3), amount)
    donor, taker = mixed[0:amount // 2 * 2:2], mixed[1:amount // 2 * 2:2]
    slack = jnp.minimum(lengths[donor] - 1, reach - lengths[taker]) // 2
    slack = jnp.where((donor == ranking[0]) | (taker == ranking[0]) | (lengths[taker] == 0), 0, jnp.maximum(slack, 0))
    moved = jax.random.randint(jax.random.fold_in(own, 4), (amount // 2,), 0, 1 << 20) % (slack + 1)
    lengths = lengths.at[donor].add(-moved).at[taker].add(moved)
    members = jnp.searchsorted(jnp.cumsum(lengths), jnp.arange(rows * top), side="right").astype(jnp.int32)
    grid = members.reshape(top, rows).T
    grid = grid[jax.random.permutation(jax.random.fold_in(own, 1), rows)]
    turn = jax.random.randint(jax.random.fold_in(own, 2), (rows, 1), 0, top)
    return jnp.take_along_axis(grid, (jnp.arange(top)[None, :] + turn) % top, axis=1)


def portions_of(amount, total, most, lean, full):
    portions = [(1 << 20) // math.isqrt(rank ** lean) + 1 for rank in range(1, amount + 1)]
    largest = most if full else min(most, max(-(-total // amount), total * portions[0] // sum(portions)))
    least = 1 if total - largest >= amount - 1 else 0
    given, rest = [largest] + [least] * (amount - 1), total - largest - least * (amount - 1)
    while rest > 0:
        movable = [i for i in range(1, amount) if given[i] < largest] or [i for i in range(1, amount) if given[i] < most]
        whole, left = sum([portions[i] for i in movable]), rest
        for i in movable:
            extra = min(most - given[i], max(1, left * portions[i] // whole), rest)
            given[i] = given[i] + extra
            rest = rest - extra
    return np.array(given)


def gaussian(rng, shape, spread, limit, shards=(), kind=jnp.bfloat16):
    loudness = steps_of(rng, shape, shards, -0.22, 0.18) if shards else 1.0
    values = jax.random.normal(rng, shape, jnp.float32) * spread * loudness
    return jnp.minimum(jnp.maximum(values, -limit), limit).astype(kind)


def setup_inputs(seed: int = 0) -> dict:
    streams_of = jax.random.split(jax.random.key(seed), 8)
    stiffness = gaussian(streams_of[0], (NB, 2, FB, FB), FB ** -0.5, 0.4375)
    lame = jnp.clip(jnp.exp(math.log(3.0) - 2.3025851 * jax.random.uniform(streams_of[1], (ELEMENTS, NB, 2), jnp.float32) ** steps_of(streams_of[1], (ELEMENTS, NB, 2), ((0, 32),), -0.2, 0.2)), 0.3, 3.0)
    prolong = gaussian(streams_of[2], (ELEMENTS, CB, FB), FB ** -0.5, 0.4375, ((0, 32),))
    columns = draw_columns(jax.random.fold_in(streams_of[7], 71), 0)
    ghost_count = draw_ghost_count(jax.random.fold_in(streams_of[7], 71), 0)
    ghost_offset = draw_ghost_offset(jax.random.fold_in(streams_of[7], 71), 0)
    owner_map_keys = jax.random.split(jax.random.fold_in(streams_of[6], 1), ELEMENTS // ELEM_DEV)
    owner_map_turns = jax.random.permutation(jax.random.fold_in(streams_of[6], 3), ELEMENTS // ELEM_DEV)
    owner_map = jax.vmap(lambda own, number: shared_out(jax.random.fold_in(streams_of[6], 2), own, number, ELEM_DEV, N_GRP, 1, CAP, 2))(owner_map_keys, owner_map_turns).reshape((ELEMENTS, 1))
    return {"stiffness": stiffness, "lame": lame, "prolong": prolong, "columns": columns, "ghost_count": ghost_count, "ghost_offset": ghost_offset, "owner_map": owner_map}


def slot_rank(target):
    matching = target[..., :, None] == target[..., None, :]
    places = jnp.arange(target.shape[-1])
    earlier = places[None, :] < places[:, None]
    return jnp.sum(jnp.logical_and(matching, earlier), axis=-1).astype(jnp.int32)


def reference(stiffness, lame, prolong, columns, ghost_count, ghost_offset, owner_map):
    device_total = N_GRP * N_ROW
    stiff_first = stiffness[:, 0].astype(jnp.float32)
    stiff_second = stiffness[:, 1].astype(jnp.float32)

    def one_device(device):
        first = device * ELEM_DEV
        local_lame = lax.dynamic_slice_in_dim(lame, first, ELEM_DEV, 0).astype(jnp.float32)
        local_columns = lax.dynamic_slice_in_dim(columns, first, ELEM_DEV, 0)
        own_prolong = lax.dynamic_slice_in_dim(prolong, first, ELEM_DEV, 0).astype(jnp.float32)
        row_index = device % N_ROW
        below = jnp.clip(device - 1, 0, device_total - 1).astype(jnp.int32)
        above = jnp.clip(device + 1, 0, device_total - 1).astype(jnp.int32)
        below_slot = local_columns - ELEM_DEV
        above_slot = local_columns - ELEM_DEV - GHOSTS
        is_local = (local_columns >= 0) & (local_columns < ELEM_DEV)
        is_below = (below_slot >= 0) & (below_slot < GHOSTS) & (row_index >= 1) & (below_slot < ghost_count[below, 1])
        is_above = (above_slot >= 0) & (row_index <= N_ROW - 2) & (above_slot < ghost_count[above, 0])
        element = jnp.where(is_local, first + local_columns,
                            jnp.where(is_below, below * ELEM_DEV + ghost_offset[below, 1] + below_slot,
                                      above * ELEM_DEV + ghost_offset[above, 0] + above_slot))
        usable = (is_local | is_below | is_above).astype(jnp.float32)
        element = jnp.clip(element, 0, ELEMENTS - 1).astype(jnp.int32)
        chosen = jnp.take(prolong, element, axis=0).astype(jnp.float32) * usable[:, :, None, None]
        part_first = jnp.einsum('eskj,sij->eski', chosen, stiff_first, precision=lax.Precision.HIGHEST)
        part_second = jnp.einsum('eskj,sij->eski', chosen, stiff_second, precision=lax.Precision.HIGHEST)
        applied = local_lame[:, :, 0, None, None] * part_first + local_lame[:, :, 1, None, None] * part_second
        coarse = jnp.einsum('eai,eski->eask', own_prolong, applied, precision=lax.Precision.HIGHEST)
        return coarse.reshape(ELEM_DEV, CB, NB * CB).astype(jnp.bfloat16)

    coarse_all = lax.map(one_device, jnp.arange(device_total, dtype=jnp.int32))
    target = owner_map.reshape(device_total, ELEM_DEV)
    position = slot_rank(target)
    devices = jnp.arange(device_total, dtype=jnp.int32)[:, None]
    destination = ((target * N_ROW + devices % N_ROW) * N_GRP + devices // N_ROW) * CAP + position
    destination = destination.reshape(-1).astype(jnp.int32)
    rows_out = jnp.zeros((device_total * N_GRP * CAP, CB, NB * CB), jnp.bfloat16)
    rows_out = rows_out.at[destination].set(coarse_all.reshape(ELEMENTS, CB, NB * CB))
    ids_out = jnp.full((device_total * N_GRP * CAP,), -1, jnp.int32)
    ids_out = ids_out.at[destination].set(jnp.arange(ELEMENTS, dtype=jnp.int32))
    return (rows_out, ids_out)
```

```python
import functools

import jax
import jax.numpy as jnp
from jax import lax
from jax.experimental import pallas as pl
from jax.experimental.pallas import tpu as pltpu
from jax.sharding import PartitionSpec as P

LANES = 128
VMEM = pl.BlockSpec(memory_space=pltpu.VMEM)
SMEM = pl.BlockSpec(memory_space=pltpu.SMEM)


def in_vmem(value):
    return pltpu.with_memory_space_constraint(value, pltpu.VMEM)


def params():
    return pltpu.CompilerParams(vmem_limit_bytes=24 * 1024 * 1024)


def passed_along(value, axis, by):
    peers = lax.axis_size(axis)
    pairs = [(i, i + by) for i in range(peers) if 0 <= i + by < peers]
    return lax.ppermute(value, axis, pairs)


def pack_kernel(count_ref, offset_ref, prolong_ref, below_ref, above_ref):
    elements = prolong_ref.shape[0]
    for way, out_ref in enumerate((below_ref, above_ref)):
        first = offset_ref[0, way]
        length = count_ref[0, way]

        def block(slot):
            value = prolong_ref[jnp.minimum(first + slot, elements - 1)].astype(jnp.float32)
            return jnp.where(slot < length, value, 0.0)

        for pair in range(out_ref.shape[0]):
            even, odd = block(2 * pair), block(2 * pair + 1)
            tail = jnp.concatenate([even[:, LANES:], odd[:, LANES:]], axis=1)
            out_ref[pair] = jnp.concatenate(
                [even[:, :LANES], odd[:, :LANES], tail], axis=0
            ).astype(jnp.bfloat16)


def left_kernel(lame_ref, stiffness_ref, prolong_ref, left_ref):
    elements, slots, rows, _ = left_ref.shape
    coarse = rows // 2
    own = prolong_ref[...]
    for s in range(slots):
        first = jnp.dot(own, stiffness_ref[s, 0], preferred_element_type=jnp.float32)
        second = jnp.dot(own, stiffness_ref[s, 1], preferred_element_type=jnp.float32)
        for e in range(elements):
            part = slice(e * coarse, (e + 1) * coarse)
            total = lame_ref[s, 0, e] * first[part] + lame_ref[s, 1, e] * second[part]
            high = total.astype(jnp.bfloat16).astype(jnp.float32)
            left_ref[e, s] = jnp.concatenate([high, total - high], axis=0).astype(jnp.bfloat16)


def rows_kernel(columns_ref, owner_ref, prolong_ref, below_ref, above_ref, left_ref, out_ref, table, filled):
    elements, coarse, fine = prolong_ref.shape
    slots = left_ref.shape[1]
    ghosts = 2 * below_ref.shape[0]
    owners = filled.shape[0]
    capacity = out_ref.shape[0] // owners
    half = fine - LANES
    for e in range(elements):
        table[e] = prolong_ref[e].astype(jnp.float32)
    for start, ref in ((elements, below_ref), (elements + ghosts, above_ref)):
        for pair in range(ghosts // 2):
            block = ref[pair].astype(jnp.float32)
            tail = block[2 * coarse :]
            for odd in range(2):
                table[start + 2 * pair + odd] = jnp.concatenate(
                    [block[odd * coarse : (odd + 1) * coarse], tail[:, odd * half : (odd + 1) * half]], axis=1
                )
    table[elements + 2 * ghosts] = jnp.zeros((coarse, fine), jnp.float32)

    lane8 = lax.broadcasted_iota(jnp.int32, (8, LANES), 1)
    empty = jnp.concatenate(
        [jnp.zeros((coarse, LANES), jnp.float32), jnp.where(lane8 >= 120, -1.0, 0.0)], axis=0
    ).astype(jnp.bfloat16)
    for i in range(out_ref.shape[0]):
        out_ref[i] = empty
    for t in range(owners):
        filled[t] = 0

    width = slots * coarse
    lane = lax.broadcasted_iota(jnp.int32, (coarse, width), 1)
    for e in range(elements):
        blocks = []
        for s in range(slots):
            c = columns_ref[e, s]
            blocks.append(table[jnp.where(c < 0, elements + 2 * ghosts, c)])
        right = jnp.concatenate(blocks, axis=0).astype(jnp.bfloat16)
        left = left_ref[e].reshape(slots * 2 * coarse, fine)
        product = lax.dot_general(
            left, right, (((1,), (1,)), ((), ())), preferred_element_type=jnp.float32
        )
        result = None
        for s in range(slots):
            at = 2 * coarse * s
            part = product[at : at + coarse] + product[at + coarse : at + 2 * coarse]
            result = part if s == 0 else jnp.where(lane >= s * coarse, part, result)
        rest = result[:, LANES:]
        tail = jnp.concatenate(
            [rest[0:8], rest[8:16], rest[16:24], jnp.full((8, 8), e, jnp.float32)], axis=1
        )
        target = owner_ref[e]
        position = filled[target]
        filled[target] = position + 1
        out_ref[target * capacity + position] = jnp.concatenate(
            [result[:, :LANES], tail], axis=0
        ).astype(jnp.bfloat16)


def unpack_kernel(elements, capacity, received_ref, rows_ref, ids_ref):
    rest = rows_ref.shape[2] - LANES
    lane = lax.broadcasted_iota(jnp.int32, (8, LANES), 1)
    count = rows_ref.shape[0]
    wide = pl.cdiv(count, LANES)
    local = [jnp.full((8, LANES), -1.0, jnp.float32) for _ in range(wide)]
    for i in range(count):
        block = received_ref[i].astype(jnp.float32)
        tail = block[24:32]
        rows_ref[i] = jnp.concatenate(
            [
                block[0:24],
                jnp.concatenate([tail[:, rest * q : rest * (q + 1)] for q in range(3)], axis=0),
            ],
            axis=1,
        ).astype(jnp.bfloat16)
        local[i // LANES] = jnp.where(lane == i % LANES, tail[:, 127:128], local[i // LANES])
    local = jnp.concatenate(local, axis=1)[0:1, :count].astype(jnp.int32)
    group = lax.broadcasted_iota(jnp.int32, (1, count), 1) // capacity
    first = (group * lax.axis_size("row") + lax.axis_index("row")) * elements
    ids_ref[...] = jnp.where(local >= 0, first + local, -1)


def on_device(stiffness, lame, prolong, columns, ghost_count, ghost_offset, owner_map):
    elements, coarse, fine = prolong.shape
    slots = stiffness.shape[0]
    ghosts = elements // 2
    owners = lax.axis_size("grp")
    capacity = 2 * ((elements + owners - 1) // owners)
    run = pltpu.VMEM((ghosts // 2, 3 * coarse, LANES), jnp.bfloat16)
    to_below, to_above = pl.pallas_call(
        pack_kernel, out_shape=(run, run), in_specs=[SMEM, SMEM, VMEM], out_specs=(VMEM, VMEM),
        compiler_params=params(), name="pack",
    )(ghost_count, ghost_offset, prolong)
    from_below = passed_along(to_above, "row", 1)
    from_above = passed_along(to_below, "row", -1)
    left = pl.pallas_call(
        left_kernel,
        out_shape=pltpu.VMEM((elements, slots, 2 * coarse, fine), jnp.bfloat16),
        in_specs=[SMEM, VMEM, VMEM], out_specs=VMEM,
        compiler_params=params(), name="left",
    )(lame.transpose(1, 2, 0), stiffness, prolong.reshape(elements * coarse, fine))
    packed = pl.pallas_call(
        rows_kernel,
        out_shape=pltpu.VMEM((owners * capacity, 32, LANES), jnp.bfloat16),
        in_specs=[SMEM, SMEM, VMEM, VMEM, VMEM, VMEM], out_specs=VMEM,
        scratch_shapes=[
            pltpu.VMEM((elements + 2 * ghosts + 1, coarse, fine), jnp.float32),
            pltpu.SMEM((owners,), jnp.int32),
        ],
        compiler_params=params(), name="rows",
    )(columns, owner_map[:, 0], prolong, in_vmem(from_below), in_vmem(from_above), in_vmem(left))
    received = lax.all_to_all(packed, "grp", split_axis=0, concat_axis=0, tiled=True)
    coarse_rows, ids = pl.pallas_call(
        functools.partial(unpack_kernel, elements, capacity),
        out_shape=(
            jax.ShapeDtypeStruct((owners * capacity, coarse, slots * coarse), jnp.bfloat16),
            jax.ShapeDtypeStruct((1, owners * capacity), jnp.int32),
        ),
        in_specs=[VMEM], out_specs=(VMEM, VMEM),
        compiler_params=params(), name="unpack",
    )(in_vmem(received))
    return (coarse_rows, ids.reshape(-1))


def solution(mesh):
    split = ("grp", "row")
    return jax.shard_map(
        on_device, mesh=mesh,
        in_specs=(P(), P(split, None, None), P(split, None, None)) + (P(split, None),) * 4,
        out_specs=(P(split, None, None), P(split)), check_vma=False,
    )
```

```python
import functools

import jax
import jax.numpy as jnp
from jax import lax
from jax.experimental import pallas as pl
from jax.experimental.pallas import tpu as pltpu
from jax.sharding import PartitionSpec as P

LANES = 128
VMEM = pl.BlockSpec(memory_space=pltpu.VMEM)
HBM = pl.BlockSpec(memory_space=pltpu.HBM)
SMEM = pl.BlockSpec(memory_space=pltpu.SMEM)


def in_vmem(value):
    return pltpu.with_memory_space_constraint(value, pltpu.VMEM)


def in_smem(value):
    return pltpu.with_memory_space_constraint(value, pltpu.SMEM)


def in_hbm(value):
    return pltpu.with_memory_space_constraint(value, pltpu.HBM)


def params():
    return pltpu.CompilerParams(vmem_limit_bytes=24 * 1024 * 1024)


def passed_along(value, axis, by):
    peers = lax.axis_size(axis)
    pairs = [(i, i + by) for i in range(peers) if 0 <= i + by < peers]
    return lax.ppermute(value, axis, pairs)


def fetch(pairs, sems):
    copies = [pltpu.make_async_copy(src, dst, sems.at[i]) for i, (src, dst) in enumerate(pairs)]
    for copy in copies:
        copy.start()
    return copies


def pack_kernel(count_hbm, offset_hbm, prolong_hbm, below_ref, above_ref, count_ref, offset_ref, prolong_ref, sems):
    copies = fetch(
        [(count_hbm, count_ref), (offset_hbm, offset_ref), (prolong_hbm, prolong_ref)], sems
    )
    for copy in copies:
        copy.wait()
    elements = prolong_ref.shape[0]
    for way, out_ref in enumerate((below_ref, above_ref)):
        first = offset_ref[0, way]
        length = count_ref[0, way]

        def block(slot):
            value = prolong_ref[jnp.minimum(first + slot, elements - 1)].astype(jnp.float32)
            return jnp.where(slot < length, value, 0.0)

        for pair in range(out_ref.shape[0]):
            even, odd = block(2 * pair), block(2 * pair + 1)
            tail = jnp.concatenate([even[:, LANES:], odd[:, LANES:]], axis=1)
            out_ref[pair] = jnp.concatenate(
                [even[:, :LANES], odd[:, :LANES], tail], axis=0
            ).astype(jnp.bfloat16)


def left_kernel(
    lame_hbm, columns_hbm, owner_hbm, stiffness_hbm, prolong_hbm,
    left_ref, prolong_ref, columns_ref, place_ref, start_ref,
    lame_ref, owner_ref, stiffness_ref, filled, sems,
):
    elements, slots, rows, _ = left_ref.shape
    coarse = rows // 2
    owners = filled.shape[0]
    copies = fetch(
        [(prolong_hbm, prolong_ref), (lame_hbm, lame_ref), (owner_hbm, owner_ref), (columns_hbm, columns_ref)]
        + [(stiffness_hbm.at[s], stiffness_ref.at[s]) for s in range(slots)],
        sems,
    )
    for copy in copies[:3]:
        copy.wait()
    for t in range(owners):
        filled[t] = 0
    for e in range(elements):
        filled[owner_ref[0, e]] = filled[owner_ref[0, e]] + 1
    total = jnp.int32(0)
    for t in range(owners):
        start_ref[t] = total
        total = total + filled[t]
        filled[t] = start_ref[t]
    start_ref[owners] = total
    for e in range(elements):
        place_ref[e] = filled[owner_ref[0, e]]
        filled[owner_ref[0, e]] = place_ref[e] + 1

    own = prolong_ref[...]
    for s in range(slots):
        copies[4 + s].wait()
        first = jnp.dot(own, stiffness_ref[s, 0], preferred_element_type=jnp.float32)
        second = jnp.dot(own, stiffness_ref[s, 1], preferred_element_type=jnp.float32)
        for e in range(elements):
            part = slice(e * coarse, (e + 1) * coarse)
            total = lame_ref[s, 0, e] * first[part] + lame_ref[s, 1, e] * second[part]
            high = total.astype(jnp.bfloat16).astype(jnp.float32)
            left_ref[e, s] = jnp.concatenate([high, total - high], axis=0).astype(jnp.bfloat16)
    copies[3].wait()


def rows_kernel(columns_ref, place_ref, start_ref, prolong_ref, below_ref, above_ref, left_ref, out_ref, table):
    elements, slots, rows, fine = left_ref.shape
    coarse = rows // 2
    ghosts = 2 * below_ref.shape[0]
    half = fine - LANES
    owners = start_ref.shape[0] - 1
    for e in range(elements):
        table[e] = prolong_ref[e * coarse : (e + 1) * coarse].astype(jnp.float32)
    for start, ref in ((elements, below_ref), (elements + ghosts, above_ref)):
        for pair in range(ghosts // 2):
            block = ref[pair].astype(jnp.float32)
            tail = block[2 * coarse :]
            for odd in range(2):
                table[start + 2 * pair + odd] = jnp.concatenate(
                    [block[odd * coarse : (odd + 1) * coarse], tail[:, odd * half : (odd + 1) * half]], axis=1
                )
    table[elements + 2 * ghosts] = jnp.zeros((coarse, fine), jnp.float32)

    row8 = lax.broadcasted_iota(jnp.int32, (8, 8), 0)
    lane8 = lax.broadcasted_iota(jnp.int32, (8, 8), 1)
    starts = jnp.zeros((8, 8), jnp.float32)
    for t in range(owners):
        here = jnp.logical_and(row8 == t % 8, lane8 == t // 8)
        starts = jnp.where(here, start_ref[t].astype(jnp.float32), starts)

    width = slots * coarse
    lane = lax.broadcasted_iota(jnp.int32, (coarse, width), 1)
    for e in range(elements):
        blocks = []
        for s in range(slots):
            c = columns_ref[s, e]
            blocks.append(table[jnp.where(c < 0, elements + 2 * ghosts, c)])
        right = jnp.concatenate(blocks, axis=0).astype(jnp.bfloat16)
        left = left_ref[e].reshape(slots * 2 * coarse, fine)
        product = lax.dot_general(
            left, right, (((1,), (1,)), ((), ())), preferred_element_type=jnp.float32
        )
        result = None
        for s in range(slots):
            at = 2 * coarse * s
            part = product[at : at + coarse] + product[at + coarse : at + 2 * coarse]
            result = part if s == 0 else jnp.where(lane >= s * coarse, part, result)
        rest = result[:, LANES:]
        spare = jnp.where(lane8 >= 2, jnp.float32(e), starts)
        tail = jnp.concatenate([rest[0:8], rest[8:16], rest[16:24], spare], axis=1)
        out_ref[place_ref[e]] = jnp.concatenate([result[:, :LANES], tail], axis=0).astype(jnp.bfloat16)


def unpack_kernel(elements, capacity, received_ref, rows_ref, ids_ref):
    rest = rows_ref.shape[2] - LANES
    count = rows_ref.shape[0]
    owners = count // capacity
    me = lax.axis_index("grp")
    row = lax.broadcasted_iota(jnp.int32, (8, LANES), 0)
    lane = lax.broadcasted_iota(jnp.int32, (8, LANES), 1)
    wide = pl.cdiv(count, LANES)
    local = [jnp.full((8, LANES), -1.0, jnp.float32) for _ in range(wide)]

    def start_of(tail, t):
        here = jnp.logical_and(row == t % 8, lane == 120 + t // 8)
        return jnp.sum(jnp.where(here, tail, 0.0)).astype(jnp.int32)

    bounds = []
    for source in range(owners):
        tail = received_ref[source * elements].astype(jnp.float32)[24:32]
        begin = start_of(tail, me)
        end = jnp.where(me == owners - 1, elements, start_of(tail, jnp.minimum(me + 1, owners - 1)))
        bounds.append((begin, end - begin))
    for i in range(count):
        source, slot = i // capacity, i % capacity
        begin, length = bounds[source]
        block = received_ref[source * elements + jnp.minimum(begin + slot, elements - 1)].astype(jnp.float32)
        block = jnp.where(slot < length, block, 0.0)
        tail = block[24:32]
        rows_ref[i] = jnp.concatenate(
            [
                block[0:24],
                jnp.concatenate([tail[:, rest * q : rest * (q + 1)] for q in range(3)], axis=0),
            ],
            axis=1,
        ).astype(jnp.bfloat16)
        here = jnp.logical_and(lane == i % LANES, slot < length)
        local[i // LANES] = jnp.where(here, tail[:, 127:128], local[i // LANES])
    local = jnp.concatenate(local, axis=1)[0:1, :count].astype(jnp.int32)
    group = lax.broadcasted_iota(jnp.int32, (1, count), 1) // capacity
    first = (group * lax.axis_size("row") + lax.axis_index("row")) * elements
    ids_ref[...] = jnp.where(local >= 0, first + local, -1)


def on_device(stiffness, lame, prolong, columns, ghost_count, ghost_offset, owner_map):
    elements, coarse, fine = prolong.shape
    slots = stiffness.shape[0]
    ghosts = elements // 2
    owners = lax.axis_size("grp")
    capacity = 2 * ((elements + owners - 1) // owners)
    run = pltpu.VMEM((ghosts // 2, 3 * coarse, LANES), jnp.bfloat16)
    to_below, to_above = pl.pallas_call(
        pack_kernel, out_shape=(run, run), in_specs=[HBM] * 3, out_specs=(VMEM, VMEM),
        scratch_shapes=[
            pltpu.SMEM(ghost_count.shape, jnp.int32),
            pltpu.SMEM(ghost_offset.shape, jnp.int32),
            pltpu.VMEM(prolong.shape, jnp.bfloat16),
            pltpu.SemaphoreType.DMA((3,)),
        ],
        compiler_params=params(), name="pack",
    )(in_hbm(ghost_count), in_hbm(ghost_offset), in_hbm(prolong))
    from_below = passed_along(to_above, "row", 1)
    from_above = passed_along(to_below, "row", -1)
    left, own, by_slot, place, start = pl.pallas_call(
        left_kernel,
        out_shape=(
            pltpu.VMEM((elements, slots, 2 * coarse, fine), jnp.bfloat16),
            pltpu.VMEM((elements * coarse, fine), jnp.bfloat16),
            pltpu.SMEM((slots, elements), jnp.int32),
            pltpu.SMEM((elements,), jnp.int32),
            pltpu.SMEM((owners + 1,), jnp.int32),
        ),
        in_specs=[HBM] * 5, out_specs=(VMEM, VMEM, SMEM, SMEM, SMEM),
        scratch_shapes=[
            pltpu.SMEM((slots, 2, elements), jnp.float32),
            pltpu.SMEM((1, elements), jnp.int32),
            pltpu.VMEM(stiffness.shape, jnp.bfloat16),
            pltpu.SMEM((owners,), jnp.int32),
            pltpu.SemaphoreType.DMA((4 + slots,)),
        ],
        compiler_params=params(), name="left",
    )(
        in_hbm(lame.transpose(1, 2, 0)), in_hbm(columns.T), in_hbm(owner_map.T),
        in_hbm(stiffness), in_hbm(prolong.reshape(elements * coarse, fine)),
    )
    packed = pl.pallas_call(
        rows_kernel,
        out_shape=pltpu.VMEM((elements, 32, LANES), jnp.bfloat16),
        in_specs=[SMEM, SMEM, SMEM, VMEM, VMEM, VMEM, VMEM], out_specs=VMEM,
        scratch_shapes=[pltpu.VMEM((elements + 2 * ghosts + 1, coarse, fine), jnp.float32)],
        compiler_params=params(), name="rows",
    )(
        in_smem(by_slot), in_smem(place), in_smem(start), in_vmem(own),
        in_vmem(from_below), in_vmem(from_above), in_vmem(left),
    )
    received = lax.all_gather(packed, "grp", axis=0, tiled=True)
    coarse_rows, ids = pl.pallas_call(
        functools.partial(unpack_kernel, elements, capacity),
        out_shape=(
            jax.ShapeDtypeStruct((owners * capacity, coarse, slots * coarse), jnp.bfloat16),
            jax.ShapeDtypeStruct((1, owners * capacity), jnp.int32),
        ),
        in_specs=[VMEM], out_specs=(VMEM, VMEM),
        compiler_params=params(), name="unpack",
    )(in_vmem(received))
    return (coarse_rows, ids.reshape(-1))


def solution(mesh):
    split = ("grp", "row")
    return jax.shard_map(
        on_device, mesh=mesh,
        in_specs=(P(), P(split, None, None), P(split, None, None)) + (P(split, None),) * 4,
        out_specs=(P(split, None, None), P(split)), check_vma=False,
    )
```

```python
import functools

import jax
import jax.numpy as jnp
from jax import lax
from jax.experimental import pallas as pl
from jax.experimental.pallas import tpu as pltpu
from jax.sharding import PartitionSpec as P

LANES = 128
VMEM = pl.BlockSpec(memory_space=pltpu.VMEM)
HBM = pl.BlockSpec(memory_space=pltpu.HBM)
SMEM = pl.BlockSpec(memory_space=pltpu.SMEM)


def in_vmem(value):
    return pltpu.with_memory_space_constraint(value, pltpu.VMEM)


def in_smem(value):
    return pltpu.with_memory_space_constraint(value, pltpu.SMEM)


def in_hbm(value):
    return pltpu.with_memory_space_constraint(value, pltpu.HBM)


def params():
    return pltpu.CompilerParams(vmem_limit_bytes=24 * 1024 * 1024)


def swapped(value, axis, parity):
    peers = lax.axis_size(axis)
    pairs = [(i, i + 1) for i in range(parity, peers - 1, 2)]
    return lax.ppermute(value, axis, pairs + [(j, i) for i, j in pairs])


def fetch(pairs, sems):
    copies = [pltpu.make_async_copy(src, dst, sems.at[i]) for i, (src, dst) in enumerate(pairs)]
    for copy in copies:
        copy.start()
    return copies


def pack_kernel(
    count_hbm, offset_hbm, prolong_hbm, lame_hbm, columns_hbm, owner_hbm, stiffness_hbm,
    odd_ref, even_ref, prolong_ref, lame_ref, columns_ref, owner_ref, stiffness_ref,
    count_ref, offset_ref, sems,
):
    copies = fetch(
        [
            (count_hbm, count_ref), (offset_hbm, offset_ref), (prolong_hbm, prolong_ref), (lame_hbm, lame_ref),
            (columns_hbm, columns_ref), (owner_hbm, owner_ref), (stiffness_hbm, stiffness_ref),
        ],
        sems,
    )
    for copy in copies[:3]:
        copy.wait()
    elements = prolong_ref.shape[0]
    odd_row = lax.rem(lax.axis_index("row"), 2)
    for way, out_ref in ((odd_row, odd_ref), (1 - odd_row, even_ref)):
        first = offset_ref[0, way]
        length = count_ref[0, way]

        def block(slot):
            value = prolong_ref[jnp.minimum(first + slot, elements - 1)].astype(jnp.float32)
            return jnp.where(slot < length, value, 0.0)

        for pair in range(out_ref.shape[0]):
            even, odd = block(2 * pair), block(2 * pair + 1)
            tail = jnp.concatenate([even[:, LANES:], odd[:, LANES:]], axis=1)
            out_ref[pair] = jnp.concatenate(
                [even[:, :LANES], odd[:, :LANES], tail], axis=0
            ).astype(jnp.bfloat16)
    for copy in copies[3:]:
        copy.wait()


def left_kernel(lame_ref, owner_ref, stiffness_ref, prolong_ref, left_ref, place_ref, start_ref, filled):
    elements, slots, rows, _ = left_ref.shape
    coarse = rows // 2
    owners = filled.shape[0]
    for t in range(owners):
        filled[t] = 0
    for e in range(elements):
        filled[owner_ref[0, e]] = filled[owner_ref[0, e]] + 1
    total = jnp.int32(0)
    for t in range(owners):
        start_ref[t] = total
        total = total + filled[t]
        filled[t] = start_ref[t]
    start_ref[owners] = total
    for e in range(elements):
        place_ref[e] = filled[owner_ref[0, e]]
        filled[owner_ref[0, e]] = place_ref[e] + 1

    own = prolong_ref[...]
    for s in range(slots):
        first = jnp.dot(own, stiffness_ref[s, 0], preferred_element_type=jnp.float32)
        second = jnp.dot(own, stiffness_ref[s, 1], preferred_element_type=jnp.float32)
        for e in range(elements):
            part = slice(e * coarse, (e + 1) * coarse)
            total = lame_ref[s, 0, e] * first[part] + lame_ref[s, 1, e] * second[part]
            high = total.astype(jnp.bfloat16).astype(jnp.float32)
            left_ref[e, s] = jnp.concatenate([high, total - high], axis=0).astype(jnp.bfloat16)


def rows_kernel(columns_ref, place_ref, start_ref, prolong_ref, odd_ref, even_ref, left_ref, out_ref, table):
    elements, slots, rows, fine = left_ref.shape
    coarse = rows // 2
    ghosts = 2 * odd_ref.shape[0]
    odd_row = lax.rem(lax.axis_index("row"), 2)
    half = fine - LANES
    owners = start_ref.shape[0] - 1
    for e in range(elements):
        table[e] = prolong_ref[e * coarse : (e + 1) * coarse].astype(jnp.float32)
    for start, ref in ((elements + ghosts * odd_row, odd_ref), (elements + ghosts * (1 - odd_row), even_ref)):
        for pair in range(ghosts // 2):
            block = ref[pair].astype(jnp.float32)
            tail = block[2 * coarse :]
            for odd in range(2):
                table[start + 2 * pair + odd] = jnp.concatenate(
                    [block[odd * coarse : (odd + 1) * coarse], tail[:, odd * half : (odd + 1) * half]], axis=1
                )
    table[elements + 2 * ghosts] = jnp.zeros((coarse, fine), jnp.float32)

    row8 = lax.broadcasted_iota(jnp.int32, (8, 8), 0)
    lane8 = lax.broadcasted_iota(jnp.int32, (8, 8), 1)
    starts = jnp.zeros((8, 8), jnp.float32)
    for t in range(owners):
        here = jnp.logical_and(row8 == t % 8, lane8 == t // 8)
        starts = jnp.where(here, start_ref[t].astype(jnp.float32), starts)

    width = slots * coarse
    lane = lax.broadcasted_iota(jnp.int32, (coarse, width), 1)
    for e in range(elements):
        blocks = []
        for s in range(slots):
            c = columns_ref[s, e]
            blocks.append(table[jnp.where(c < 0, elements + 2 * ghosts, c)])
        right = jnp.concatenate(blocks, axis=0).astype(jnp.bfloat16)
        left = left_ref[e].reshape(slots * 2 * coarse, fine)
        product = lax.dot_general(
            left, right, (((1,), (1,)), ((), ())), preferred_element_type=jnp.float32
        )
        result = None
        for s in range(slots):
            at = 2 * coarse * s
            part = product[at : at + coarse] + product[at + coarse : at + 2 * coarse]
            result = part if s == 0 else jnp.where(lane >= s * coarse, part, result)
        rest = result[:, LANES:]
        spare = jnp.where(lane8 >= 2, jnp.float32(e), starts)
        tail = jnp.concatenate([rest[0:8], rest[8:16], rest[16:24], spare], axis=1)
        out_ref[place_ref[e]] = jnp.concatenate([result[:, :LANES], tail], axis=0).astype(jnp.bfloat16)


def unpack_kernel(elements, capacity, received_ref, rows_ref, ids_ref):
    rest = rows_ref.shape[2] - LANES
    count = rows_ref.shape[0]
    owners = count // capacity
    me = lax.axis_index("grp")
    row = lax.broadcasted_iota(jnp.int32, (8, LANES), 0)
    lane = lax.broadcasted_iota(jnp.int32, (8, LANES), 1)
    wide = pl.cdiv(count, LANES)
    local = [jnp.full((8, LANES), -1.0, jnp.float32) for _ in range(wide)]

    def start_of(tail, t):
        here = jnp.logical_and(row == t % 8, lane == 120 + t // 8)
        return jnp.sum(jnp.where(here, tail, 0.0)).astype(jnp.int32)

    bounds = []
    for source in range(owners):
        tail = received_ref[source * elements].astype(jnp.float32)[24:32]
        begin = start_of(tail, me)
        end = jnp.where(me == owners - 1, elements, start_of(tail, jnp.minimum(me + 1, owners - 1)))
        bounds.append((begin, end - begin))
    for i in range(count):
        source, slot = i // capacity, i % capacity
        begin, length = bounds[source]
        block = received_ref[source * elements + jnp.minimum(begin + slot, elements - 1)].astype(jnp.float32)
        block = jnp.where(slot < length, block, 0.0)
        tail = block[24:32]
        rows_ref[i] = jnp.concatenate(
            [
                block[0:24],
                jnp.concatenate([tail[:, rest * q : rest * (q + 1)] for q in range(3)], axis=0),
            ],
            axis=1,
        ).astype(jnp.bfloat16)
        here = jnp.logical_and(lane == i % LANES, slot < length)
        local[i // LANES] = jnp.where(here, tail[:, 127:128], local[i // LANES])
    local = jnp.concatenate(local, axis=1)[0:1, :count].astype(jnp.int32)
    group = lax.broadcasted_iota(jnp.int32, (1, count), 1) // capacity
    first = (group * lax.axis_size("row") + lax.axis_index("row")) * elements
    ids_ref[...] = jnp.where(local >= 0, first + local, -1)


def on_device(stiffness, lame, prolong, columns, ghost_count, ghost_offset, owner_map):
    elements, coarse, fine = prolong.shape
    slots = stiffness.shape[0]
    ghosts = elements // 2
    owners = lax.axis_size("grp")
    capacity = 2 * ((elements + owners - 1) // owners)
    run = pltpu.VMEM((ghosts // 2, 3 * coarse, LANES), jnp.bfloat16)
    by_odd, by_even, own, lame_slots, by_slot, owner, tables = pl.pallas_call(
        pack_kernel,
        out_shape=(
            run, run,
            pltpu.VMEM(prolong.shape, jnp.bfloat16),
            pltpu.SMEM((slots, 2, elements), jnp.float32),
            pltpu.SMEM((slots, elements), jnp.int32),
            pltpu.SMEM((1, elements), jnp.int32),
            pltpu.VMEM(stiffness.shape, jnp.bfloat16),
        ),
        in_specs=[HBM] * 7, out_specs=(VMEM, VMEM, VMEM, SMEM, SMEM, SMEM, VMEM),
        scratch_shapes=[
            pltpu.SMEM(ghost_count.shape, jnp.int32),
            pltpu.SMEM(ghost_offset.shape, jnp.int32),
            pltpu.SemaphoreType.DMA((7,)),
        ],
        compiler_params=params(), name="pack",
    )(
        in_hbm(ghost_count), in_hbm(ghost_offset), in_hbm(prolong), in_hbm(lame.transpose(1, 2, 0)),
        in_hbm(columns.T), in_hbm(owner_map.T), in_hbm(stiffness),
    )
    from_odd = swapped(by_odd, "row", 1)
    from_even = swapped(by_even, "row", 0)
    own = in_vmem(own.reshape(elements * coarse, fine))
    left, place, start = pl.pallas_call(
        left_kernel,
        out_shape=(
            pltpu.VMEM((elements, slots, 2 * coarse, fine), jnp.bfloat16),
            pltpu.SMEM((elements,), jnp.int32),
            pltpu.SMEM((owners + 1,), jnp.int32),
        ),
        in_specs=[SMEM, SMEM, VMEM, VMEM], out_specs=(VMEM, SMEM, SMEM),
        scratch_shapes=[pltpu.SMEM((owners,), jnp.int32)],
        compiler_params=params(), name="left",
    )(in_smem(lame_slots), in_smem(owner), in_vmem(tables), own)
    packed = pl.pallas_call(
        rows_kernel,
        out_shape=pltpu.VMEM((elements, 32, LANES), jnp.bfloat16),
        in_specs=[SMEM, SMEM, SMEM, VMEM, VMEM, VMEM, VMEM], out_specs=VMEM,
        scratch_shapes=[pltpu.VMEM((elements + 2 * ghosts + 1, coarse, fine), jnp.float32)],
        compiler_params=params(), name="rows",
    )(
        in_smem(by_slot), in_smem(place), in_smem(start), own,
        in_vmem(from_odd), in_vmem(from_even), in_vmem(left),
    )
    received = lax.all_gather(packed, "grp", axis=0, tiled=True)
    coarse_rows, ids = pl.pallas_call(
        functools.partial(unpack_kernel, elements, capacity),
        out_shape=(
            jax.ShapeDtypeStruct((owners * capacity, coarse, slots * coarse), jnp.bfloat16),
            jax.ShapeDtypeStruct((1, owners * capacity), jnp.int32),
        ),
        in_specs=[VMEM], out_specs=(VMEM, VMEM),
        compiler_params=params(), name="unpack",
    )(in_vmem(received))
    return (coarse_rows, ids.reshape(-1))


def solution(mesh):
    split = ("grp", "row")
    return jax.shard_map(
        on_device, mesh=mesh,
        in_specs=(P(), P(split, None, None), P(split, None, None)) + (P(split, None),) * 4,
        out_specs=(P(split, None, None), P(split)), check_vma=False,
    )
```

```python
import functools

import jax
import jax.numpy as jnp
from jax import lax
from jax.experimental import pallas as pl
from jax.experimental.pallas import tpu as pltpu
from jax.sharding import PartitionSpec as P

LANES = 128
VMEM = pl.BlockSpec(memory_space=pltpu.VMEM)
HBM = pl.BlockSpec(memory_space=pltpu.HBM)
SMEM = pl.BlockSpec(memory_space=pltpu.SMEM)


def in_vmem(value):
    return pltpu.with_memory_space_constraint(value, pltpu.VMEM)


def in_smem(value):
    return pltpu.with_memory_space_constraint(value, pltpu.SMEM)


def in_hbm(value):
    return pltpu.with_memory_space_constraint(value, pltpu.HBM)


def params():
    return pltpu.CompilerParams(vmem_limit_bytes=24 * 1024 * 1024)


def swapped(value, axis, parity):
    peers = lax.axis_size(axis)
    pairs = [(i, i + 1) for i in range(parity, peers - 1, 2)]
    return lax.ppermute(value, axis, pairs + [(j, i) for i, j in pairs])


def fetch(pairs, sems):
    copies = [pltpu.make_async_copy(src, dst, sems.at[i]) for i, (src, dst) in enumerate(pairs)]
    for copy in copies:
        copy.start()
    return copies


def pack_kernel(
    count_hbm, offset_hbm, prolong_hbm, odd_ref, even_ref, prolong_ref, count_ref, offset_ref, sems,
):
    copies = fetch(
        [(prolong_hbm, prolong_ref), (count_hbm, count_ref), (offset_hbm, offset_ref)], sems
    )
    for copy in copies:
        copy.wait()
    elements = prolong_ref.shape[0]
    odd_row = lax.rem(lax.axis_index("row"), 2)
    for way, out_ref in ((odd_row, odd_ref), (1 - odd_row, even_ref)):
        first = offset_ref[0, way]
        length = count_ref[0, way]

        def block(slot):
            value = prolong_ref[jnp.minimum(first + slot, elements - 1)].astype(jnp.float32)
            return jnp.where(slot < length, value, 0.0)

        for pair in range(out_ref.shape[0]):
            even, odd = block(2 * pair), block(2 * pair + 1)
            tail = jnp.concatenate([even[:, LANES:], odd[:, LANES:]], axis=1)
            out_ref[pair] = jnp.concatenate(
                [even[:, :LANES], odd[:, :LANES], tail], axis=0
            ).astype(jnp.bfloat16)


def left_kernel(
    lame_hbm, columns_hbm, owner_hbm, stiffness_hbm, prolong_ref,
    left_ref, columns_ref, place_ref, start_ref,
    lame_ref, owner_ref, stiffness_ref, filled, sems,
):
    elements, slots, rows, _ = left_ref.shape
    coarse = rows // 2
    owners = filled.shape[0]
    copies = fetch(
        [(stiffness_hbm.at[s], stiffness_ref.at[s]) for s in range(slots)]
        + [(lame_hbm, lame_ref), (owner_hbm, owner_ref), (columns_hbm, columns_ref)],
        sems,
    )
    copies[slots + 1].wait()
    for t in range(owners):
        filled[t] = 0
    for e in range(elements):
        filled[owner_ref[0, e]] = filled[owner_ref[0, e]] + 1
    total = jnp.int32(0)
    for t in range(owners):
        start_ref[t] = total
        total = total + filled[t]
        filled[t] = start_ref[t]
    start_ref[owners] = total
    for e in range(elements):
        place_ref[e] = filled[owner_ref[0, e]]
        filled[owner_ref[0, e]] = place_ref[e] + 1

    for copy in copies[slots:slots + 1] + copies[slots + 2:]:
        copy.wait()
    own = prolong_ref[...]
    for s in range(slots):
        copies[s].wait()
        first = jnp.dot(own, stiffness_ref[s, 0], preferred_element_type=jnp.float32)
        second = jnp.dot(own, stiffness_ref[s, 1], preferred_element_type=jnp.float32)
        for e in range(elements):
            part = slice(e * coarse, (e + 1) * coarse)
            total = lame_ref[s, 0, e] * first[part] + lame_ref[s, 1, e] * second[part]
            high = total.astype(jnp.bfloat16).astype(jnp.float32)
            left_ref[e, s] = jnp.concatenate([high, total - high], axis=0).astype(jnp.bfloat16)


def rows_kernel(columns_ref, place_ref, start_ref, prolong_ref, odd_ref, even_ref, left_ref, out_ref, table):
    elements, slots, rows, fine = left_ref.shape
    coarse = rows // 2
    ghosts = 2 * odd_ref.shape[0]
    odd_row = lax.rem(lax.axis_index("row"), 2)
    half = fine - LANES
    owners = start_ref.shape[0] - 1
    for e in range(elements):
        table[e] = prolong_ref[e * coarse : (e + 1) * coarse].astype(jnp.float32)
    for start, ref in ((elements + ghosts * odd_row, odd_ref), (elements + ghosts * (1 - odd_row), even_ref)):
        for pair in range(ghosts // 2):
            block = ref[pair].astype(jnp.float32)
            tail = block[2 * coarse :]
            for odd in range(2):
                table[start + 2 * pair + odd] = jnp.concatenate(
                    [block[odd * coarse : (odd + 1) * coarse], tail[:, odd * half : (odd + 1) * half]], axis=1
                )
    table[elements + 2 * ghosts] = jnp.zeros((coarse, fine), jnp.float32)

    row8 = lax.broadcasted_iota(jnp.int32, (8, 8), 0)
    lane8 = lax.broadcasted_iota(jnp.int32, (8, 8), 1)
    starts = jnp.zeros((8, 8), jnp.float32)
    for t in range(owners):
        here = jnp.logical_and(row8 == t % 8, lane8 == t // 8)
        starts = jnp.where(here, start_ref[t].astype(jnp.float32), starts)

    width = slots * coarse
    lane = lax.broadcasted_iota(jnp.int32, (coarse, width), 1)
    for e in range(elements):
        blocks = []
        for s in range(slots):
            c = columns_ref[s, e]
            blocks.append(table[jnp.where(c < 0, elements + 2 * ghosts, c)])
        right = jnp.concatenate(blocks, axis=0).astype(jnp.bfloat16)
        left = left_ref[e].reshape(slots * 2 * coarse, fine)
        product = lax.dot_general(
            left, right, (((1,), (1,)), ((), ())), preferred_element_type=jnp.float32
        )
        result = None
        for s in range(slots):
            at = 2 * coarse * s
            part = product[at : at + coarse] + product[at + coarse : at + 2 * coarse]
            result = part if s == 0 else jnp.where(lane >= s * coarse, part, result)
        rest = result[:, LANES:]
        spare = jnp.where(lane8 >= 2, jnp.float32(e), starts)
        tail = jnp.concatenate([rest[0:8], rest[8:16], rest[16:24], spare], axis=1)
        out_ref[place_ref[e]] = jnp.concatenate([result[:, :LANES], tail], axis=0).astype(jnp.bfloat16)


def unpack_kernel(elements, capacity, received_ref, rows_ref, ids_ref):
    rest = rows_ref.shape[2] - LANES
    count = rows_ref.shape[0]
    owners = count // capacity
    me = lax.axis_index("grp")
    row = lax.broadcasted_iota(jnp.int32, (8, LANES), 0)
    lane = lax.broadcasted_iota(jnp.int32, (8, LANES), 1)
    wide = pl.cdiv(count, LANES)
    local = [jnp.full((8, LANES), -1.0, jnp.float32) for _ in range(wide)]

    def start_of(tail, t):
        here = jnp.logical_and(row == t % 8, lane == 120 + t // 8)
        return jnp.sum(jnp.where(here, tail, 0.0)).astype(jnp.int32)

    bounds = []
    for source in range(owners):
        tail = received_ref[source * elements].astype(jnp.float32)[24:32]
        begin = start_of(tail, me)
        end = jnp.where(me == owners - 1, elements, start_of(tail, jnp.minimum(me + 1, owners - 1)))
        bounds.append((begin, end - begin))
    for i in range(count):
        source, slot = i // capacity, i % capacity
        begin, length = bounds[source]
        block = received_ref[source * elements + jnp.minimum(begin + slot, elements - 1)].astype(jnp.float32)
        block = jnp.where(slot < length, block, 0.0)
        tail = block[24:32]
        rows_ref[i] = jnp.concatenate(
            [
                block[0:24],
                jnp.concatenate([tail[:, rest * q : rest * (q + 1)] for q in range(3)], axis=0),
            ],
            axis=1,
        ).astype(jnp.bfloat16)
        here = jnp.logical_and(lane == i % LANES, slot < length)
        local[i // LANES] = jnp.where(here, tail[:, 127:128], local[i // LANES])
    local = jnp.concatenate(local, axis=1)[0:1, :count].astype(jnp.int32)
    group = lax.broadcasted_iota(jnp.int32, (1, count), 1) // capacity
    first = (group * lax.axis_size("row") + lax.axis_index("row")) * elements
    ids_ref[...] = jnp.where(local >= 0, first + local, -1)


def on_device(stiffness, lame, prolong, columns, ghost_count, ghost_offset, owner_map):
    elements, coarse, fine = prolong.shape
    slots = stiffness.shape[0]
    ghosts = elements // 2
    owners = lax.axis_size("grp")
    capacity = 2 * ((elements + owners - 1) // owners)
    run = pltpu.VMEM((ghosts // 2, 3 * coarse, LANES), jnp.bfloat16)
    by_odd, by_even, own = pl.pallas_call(
        pack_kernel,
        out_shape=(run, run, pltpu.VMEM(prolong.shape, jnp.bfloat16)),
        in_specs=[HBM] * 3, out_specs=(VMEM, VMEM, VMEM),
        scratch_shapes=[
            pltpu.SMEM(ghost_count.shape, jnp.int32),
            pltpu.SMEM(ghost_offset.shape, jnp.int32),
            pltpu.SemaphoreType.DMA((3,)),
        ],
        compiler_params=params(), name="pack",
    )(in_hbm(ghost_count), in_hbm(ghost_offset), in_hbm(prolong))
    from_even = swapped(by_even, "row", 0)
    from_odd = swapped(by_odd, "row", 1)
    own = in_vmem(own.reshape(elements * coarse, fine))
    left, by_slot, place, start = pl.pallas_call(
        left_kernel,
        out_shape=(
            pltpu.VMEM((elements, slots, 2 * coarse, fine), jnp.bfloat16),
            pltpu.SMEM((slots, elements), jnp.int32),
            pltpu.SMEM((elements,), jnp.int32),
            pltpu.SMEM((owners + 1,), jnp.int32),
        ),
        in_specs=[HBM] * 4 + [VMEM], out_specs=(VMEM, SMEM, SMEM, SMEM),
        scratch_shapes=[
            pltpu.SMEM((slots, 2, elements), jnp.float32),
            pltpu.SMEM((1, elements), jnp.int32),
            pltpu.VMEM(stiffness.shape, jnp.bfloat16),
            pltpu.SMEM((owners,), jnp.int32),
            pltpu.SemaphoreType.DMA((slots + 3,)),
        ],
        compiler_params=params(), name="left",
    )(in_hbm(lame.transpose(1, 2, 0)), in_hbm(columns.T), in_hbm(owner_map.T), in_hbm(stiffness), own)
    packed = pl.pallas_call(
        rows_kernel,
        out_shape=pltpu.VMEM((elements, 32, LANES), jnp.bfloat16),
        in_specs=[SMEM, SMEM, SMEM, VMEM, VMEM, VMEM, VMEM], out_specs=VMEM,
        scratch_shapes=[pltpu.VMEM((elements + 2 * ghosts + 1, coarse, fine), jnp.float32)],
        compiler_params=params(), name="rows",
    )(
        in_smem(by_slot), in_smem(place), in_smem(start), own,
        in_vmem(from_odd), in_vmem(from_even), in_vmem(left),
    )
    received = lax.all_gather(packed, "grp", axis=0, tiled=True)
    coarse_rows, ids = pl.pallas_call(
        functools.partial(unpack_kernel, elements, capacity),
        out_shape=(
            jax.ShapeDtypeStruct((owners * capacity, coarse, slots * coarse), jnp.bfloat16),
            jax.ShapeDtypeStruct((1, owners * capacity), jnp.int32),
        ),
        in_specs=[VMEM], out_specs=(VMEM, VMEM),
        compiler_params=params(), name="unpack",
    )(in_vmem(received))
    return (coarse_rows, ids.reshape(-1))


def solution(mesh):
    split = ("grp", "row")
    return jax.shard_map(
        on_device, mesh=mesh,
        in_specs=(P(), P(split, None, None), P(split, None, None)) + (P(split, None),) * 4,
        out_specs=(P(split, None, None), P(split)), check_vma=False,
    )
```

```python
import functools

import jax
import jax.numpy as jnp
from jax import lax
from jax.experimental import pallas as pl
from jax.experimental.pallas import tpu as pltpu
from jax.sharding import PartitionSpec as P

LANES = 128
VMEM = pl.BlockSpec(memory_space=pltpu.VMEM)
HBM = pl.BlockSpec(memory_space=pltpu.HBM)
SMEM = pl.BlockSpec(memory_space=pltpu.SMEM)


def in_vmem(value):
    return pltpu.with_memory_space_constraint(value, pltpu.VMEM)


def in_smem(value):
    return pltpu.with_memory_space_constraint(value, pltpu.SMEM)


def in_hbm(value):
    return pltpu.with_memory_space_constraint(value, pltpu.HBM)


def params():
    return pltpu.CompilerParams(vmem_limit_bytes=24 * 1024 * 1024)


def swapped(value, axis, parity):
    peers = lax.axis_size(axis)
    pairs = [(i, i + 1) for i in range(parity, peers - 1, 2)]
    return lax.ppermute(value, axis, pairs + [(j, i) for i, j in pairs])


def fetch(pairs, sems):
    copies = [pltpu.make_async_copy(src, dst, sems.at[i]) for i, (src, dst) in enumerate(pairs)]
    for copy in copies:
        copy.start()
    return copies


def pack_kernel(
    count_hbm, offset_hbm, prolong_hbm, lame_hbm, columns_hbm, owner_hbm,
    odd_ref, even_ref, prolong_ref, lame_ref, columns_ref, owner_ref,
    count_ref, offset_ref, sems,
):
    copies = fetch(
        [
            (prolong_hbm, prolong_ref), (count_hbm, count_ref), (offset_hbm, offset_ref),
            (lame_hbm, lame_ref), (columns_hbm, columns_ref), (owner_hbm, owner_ref),
        ],
        sems,
    )
    for copy in copies:
        copy.wait()
    elements = prolong_ref.shape[0]
    odd_row = lax.rem(lax.axis_index("row"), 2)
    for way, out_ref in ((odd_row, odd_ref), (1 - odd_row, even_ref)):
        first = offset_ref[0, way]
        length = count_ref[0, way]

        def block(slot):
            value = prolong_ref[jnp.minimum(first + slot, elements - 1)].astype(jnp.float32)
            return jnp.where(slot < length, value, 0.0)

        for pair in range(out_ref.shape[0]):
            even, odd = block(2 * pair), block(2 * pair + 1)
            tail = jnp.concatenate([even[:, LANES:], odd[:, LANES:]], axis=1)
            out_ref[pair] = jnp.concatenate(
                [even[:, :LANES], odd[:, :LANES], tail], axis=0
            ).astype(jnp.bfloat16)


def left_kernel(
    lame_ref, owner_ref, stiffness_hbm, prolong_ref, left_ref, place_ref, start_ref, stiffness_ref, filled, sems,
):
    elements, slots, rows, _ = left_ref.shape
    coarse = rows // 2
    owners = filled.shape[0]
    copies = fetch([(stiffness_hbm.at[s], stiffness_ref.at[s]) for s in range(slots)], sems)
    for t in range(owners):
        filled[t] = 0
    for e in range(elements):
        filled[owner_ref[0, e]] = filled[owner_ref[0, e]] + 1
    total = jnp.int32(0)
    for t in range(owners):
        start_ref[t] = total
        total = total + filled[t]
        filled[t] = start_ref[t]
    start_ref[owners] = total
    for e in range(elements):
        place_ref[e] = filled[owner_ref[0, e]]
        filled[owner_ref[0, e]] = place_ref[e] + 1

    own = prolong_ref[...]
    for s in range(slots):
        copies[s].wait()
        first = jnp.dot(own, stiffness_ref[s, 0], preferred_element_type=jnp.float32)
        second = jnp.dot(own, stiffness_ref[s, 1], preferred_element_type=jnp.float32)
        for e in range(elements):
            part = slice(e * coarse, (e + 1) * coarse)
            total = lame_ref[s, 0, e] * first[part] + lame_ref[s, 1, e] * second[part]
            high = total.astype(jnp.bfloat16).astype(jnp.float32)
            left_ref[e, s] = jnp.concatenate([high, total - high], axis=0).astype(jnp.bfloat16)


def rows_kernel(columns_ref, place_ref, start_ref, prolong_ref, even_ref, odd_ref, left_ref, out_ref, table):
    elements, slots, rows, fine = left_ref.shape
    coarse = rows // 2
    ghosts = 2 * odd_ref.shape[0]
    odd_row = lax.rem(lax.axis_index("row"), 2)
    half = fine - LANES
    owners = start_ref.shape[0] - 1
    for e in range(elements):
        table[e] = prolong_ref[e * coarse : (e + 1) * coarse].astype(jnp.float32)
    for start, ref in ((elements + ghosts * (1 - odd_row), even_ref), (elements + ghosts * odd_row, odd_ref)):
        for pair in range(ghosts // 2):
            block = ref[pair].astype(jnp.float32)
            tail = block[2 * coarse :]
            for odd in range(2):
                table[start + 2 * pair + odd] = jnp.concatenate(
                    [block[odd * coarse : (odd + 1) * coarse], tail[:, odd * half : (odd + 1) * half]], axis=1
                )
    table[elements + 2 * ghosts] = jnp.zeros((coarse, fine), jnp.float32)

    row8 = lax.broadcasted_iota(jnp.int32, (8, 8), 0)
    lane8 = lax.broadcasted_iota(jnp.int32, (8, 8), 1)
    starts = jnp.zeros((8, 8), jnp.float32)
    for t in range(owners):
        here = jnp.logical_and(row8 == t % 8, lane8 == t // 8)
        starts = jnp.where(here, start_ref[t].astype(jnp.float32), starts)

    width = slots * coarse
    lane = lax.broadcasted_iota(jnp.int32, (coarse, width), 1)
    for e in range(elements):
        blocks = []
        for s in range(slots):
            c = columns_ref[s, e]
            blocks.append(table[jnp.where(c < 0, elements + 2 * ghosts, c)])
        right = jnp.concatenate(blocks, axis=0).astype(jnp.bfloat16)
        left = left_ref[e].reshape(slots * 2 * coarse, fine)
        product = lax.dot_general(
            left, right, (((1,), (1,)), ((), ())), preferred_element_type=jnp.float32
        )
        result = None
        for s in range(slots):
            at = 2 * coarse * s
            part = product[at : at + coarse] + product[at + coarse : at + 2 * coarse]
            result = part if s == 0 else jnp.where(lane >= s * coarse, part, result)
        rest = result[:, LANES:]
        spare = jnp.where(lane8 >= 2, jnp.float32(e), starts)
        tail = jnp.concatenate([rest[0:8], rest[8:16], rest[16:24], spare], axis=1)
        out_ref[place_ref[e]] = jnp.concatenate([result[:, :LANES], tail], axis=0).astype(jnp.bfloat16)


def unpack_kernel(elements, capacity, received_ref, rows_hbm, ids_ref, rows_ref, sems):
    rest = rows_ref.shape[2] - LANES
    count = rows_ref.shape[0]
    owners = count // capacity
    me = lax.axis_index("grp")
    row = lax.broadcasted_iota(jnp.int32, (8, LANES), 0)
    lane = lax.broadcasted_iota(jnp.int32, (8, LANES), 1)
    wide = pl.cdiv(count, LANES)
    local = [jnp.full((8, LANES), -1.0, jnp.float32) for _ in range(wide)]

    def start_of(tail, t):
        here = jnp.logical_and(row == t % 8, lane == 120 + t // 8)
        return jnp.sum(jnp.where(here, tail, 0.0)).astype(jnp.int32)

    bounds = []
    for source in range(owners):
        tail = received_ref[source * elements].astype(jnp.float32)[24:32]
        begin = start_of(tail, me)
        end = jnp.where(me == owners - 1, elements, start_of(tail, jnp.minimum(me + 1, owners - 1)))
        bounds.append((begin, end - begin))
    copies = []
    for i in range(count):
        source, slot = i // capacity, i % capacity
        begin, length = bounds[source]
        block = received_ref[source * elements + jnp.minimum(begin + slot, elements - 1)].astype(jnp.float32)
        block = jnp.where(slot < length, block, 0.0)
        tail = block[24:32]
        rows_ref[i] = jnp.concatenate(
            [
                block[0:24],
                jnp.concatenate([tail[:, rest * q : rest * (q + 1)] for q in range(3)], axis=0),
            ],
            axis=1,
        ).astype(jnp.bfloat16)
        here = jnp.logical_and(lane == i % LANES, slot < length)
        local[i // LANES] = jnp.where(here, tail[:, 127:128], local[i // LANES])
        if slot == capacity - 1:
            part = pl.ds(source * capacity, capacity)
            copies.append(pltpu.make_async_copy(rows_ref.at[part], rows_hbm.at[part], sems.at[source]))
            copies[-1].start()
    local = jnp.concatenate(local, axis=1)[0:1, :count].astype(jnp.int32)
    group = lax.broadcasted_iota(jnp.int32, (1, count), 1) // capacity
    first = (group * lax.axis_size("row") + lax.axis_index("row")) * elements
    ids_ref[...] = jnp.where(local >= 0, first + local, -1)
    for copy in copies:
        copy.wait()


def on_device(stiffness, lame, prolong, columns, ghost_count, ghost_offset, owner_map):
    elements, coarse, fine = prolong.shape
    slots = stiffness.shape[0]
    ghosts = elements // 2
    owners = lax.axis_size("grp")
    capacity = 2 * ((elements + owners - 1) // owners)
    run = pltpu.VMEM((ghosts // 2, 3 * coarse, LANES), jnp.bfloat16)
    by_odd, by_even, own, lame_slots, by_slot, owner = pl.pallas_call(
        pack_kernel,
        out_shape=(
            run, run,
            pltpu.VMEM(prolong.shape, jnp.bfloat16),
            pltpu.SMEM((slots, 2, elements), jnp.float32),
            pltpu.SMEM((slots, elements), jnp.int32),
            pltpu.SMEM((1, elements), jnp.int32),
        ),
        in_specs=[HBM] * 6, out_specs=(VMEM,) * 3 + (SMEM,) * 3,
        scratch_shapes=[
            pltpu.SMEM(ghost_count.shape, jnp.int32),
            pltpu.SMEM(ghost_offset.shape, jnp.int32),
            pltpu.SemaphoreType.DMA((6,)),
        ],
        compiler_params=params(), name="pack",
    )(
        in_hbm(ghost_count), in_hbm(ghost_offset), in_hbm(prolong),
        in_hbm(lame.transpose(1, 2, 0)), in_hbm(columns.T), in_hbm(owner_map.T),
    )
    from_even = swapped(by_even, "row", 0)
    from_odd = swapped(by_odd, "row", 1)
    own = in_vmem(own.reshape(elements * coarse, fine))
    left, place, start = pl.pallas_call(
        left_kernel,
        out_shape=(
            pltpu.VMEM((elements, slots, 2 * coarse, fine), jnp.bfloat16),
            pltpu.SMEM((elements,), jnp.int32),
            pltpu.SMEM((owners + 1,), jnp.int32),
        ),
        in_specs=[SMEM, SMEM, HBM, VMEM], out_specs=(VMEM, SMEM, SMEM),
        scratch_shapes=[
            pltpu.VMEM(stiffness.shape, jnp.bfloat16),
            pltpu.SMEM((owners,), jnp.int32),
            pltpu.SemaphoreType.DMA((slots,)),
        ],
        compiler_params=params(), name="left",
    )(in_smem(lame_slots), in_smem(owner), in_hbm(stiffness), own)
    packed = pl.pallas_call(
        rows_kernel,
        out_shape=pltpu.VMEM((elements, 32, LANES), jnp.bfloat16),
        in_specs=[SMEM, SMEM, SMEM, VMEM, VMEM, VMEM, VMEM], out_specs=VMEM,
        scratch_shapes=[pltpu.VMEM((elements + 2 * ghosts + 1, coarse, fine), jnp.float32)],
        compiler_params=params(), name="rows",
    )(
        in_smem(by_slot), in_smem(place), in_smem(start), own,
        in_vmem(from_even), in_vmem(from_odd), in_vmem(left),
    )
    received = lax.all_gather(packed, "grp", axis=0, tiled=True)
    coarse_rows, ids = pl.pallas_call(
        functools.partial(unpack_kernel, elements, capacity),
        out_shape=(
            jax.ShapeDtypeStruct((owners * capacity, coarse, slots * coarse), jnp.bfloat16),
            jax.ShapeDtypeStruct((1, owners * capacity), jnp.int32),
        ),
        in_specs=[VMEM], out_specs=(HBM, VMEM),
        scratch_shapes=[
            pltpu.VMEM((owners * capacity, coarse, slots * coarse), jnp.bfloat16),
            pltpu.SemaphoreType.DMA((owners,)),
        ],
        compiler_params=params(), name="unpack",
    )(in_vmem(received))
    return (coarse_rows, ids.reshape(-1))


def solution(mesh):
    split = ("grp", "row")
    return jax.shard_map(
        on_device, mesh=mesh,
        in_specs=(P(), P(split, None, None), P(split, None, None)) + (P(split, None),) * 4,
        out_specs=(P(split, None, None), P(split)), check_vma=False,
    )
```

```python
import functools

import jax
import jax.numpy as jnp
from jax import lax
from jax.experimental import pallas as pl
from jax.experimental.pallas import tpu as pltpu
from jax.sharding import PartitionSpec as P

LANES = 128
VMEM = pl.BlockSpec(memory_space=pltpu.VMEM)
HBM = pl.BlockSpec(memory_space=pltpu.HBM)
SMEM = pl.BlockSpec(memory_space=pltpu.SMEM)


def in_vmem(value):
    return pltpu.with_memory_space_constraint(value, pltpu.VMEM)


def in_smem(value):
    return pltpu.with_memory_space_constraint(value, pltpu.SMEM)


def in_hbm(value):
    return pltpu.with_memory_space_constraint(value, pltpu.HBM)


def params():
    return pltpu.CompilerParams(vmem_limit_bytes=24 * 1024 * 1024)


def swapped(value, axis, parity):
    peers = lax.axis_size(axis)
    pairs = [(i, i + 1) for i in range(parity, peers - 1, 2)]
    return lax.ppermute(value, axis, pairs + [(j, i) for i, j in pairs])


def fetch(pairs, sems):
    copies = [pltpu.make_async_copy(src, dst, sems.at[i]) for i, (src, dst) in enumerate(pairs)]
    for copy in copies:
        copy.start()
    return copies


def pack_kernel(
    count_hbm, offset_hbm, prolong_hbm, lame_hbm, columns_hbm, owner_hbm,
    odd_ref, even_ref, prolong_ref, lame_ref, columns_ref, owner_ref,
    count_ref, offset_ref, sems,
):
    copies = fetch(
        [
            (prolong_hbm, prolong_ref), (count_hbm, count_ref), (offset_hbm, offset_ref),
            (lame_hbm, lame_ref), (columns_hbm, columns_ref), (owner_hbm, owner_ref),
        ],
        sems,
    )
    for copy in copies:
        copy.wait()
    elements = prolong_ref.shape[0]
    odd_row = lax.rem(lax.axis_index("row"), 2)
    for way, out_ref in ((odd_row, odd_ref), (1 - odd_row, even_ref)):
        first = offset_ref[0, way]
        length = count_ref[0, way]

        def block(slot):
            value = prolong_ref[jnp.minimum(first + slot, elements - 1)].astype(jnp.float32)
            return jnp.where(slot < length, value, 0.0)

        for pair in range(out_ref.shape[0]):
            even, odd = block(2 * pair), block(2 * pair + 1)
            tail = jnp.concatenate([even[:, LANES:], odd[:, LANES:]], axis=1)
            out_ref[pair] = jnp.concatenate(
                [even[:, :LANES], odd[:, :LANES], tail], axis=0
            ).astype(jnp.bfloat16)


def left_kernel(
    capacity, lame_ref, owner_ref, stiffness_hbm, prolong_ref, left_ref, order_ref, stiffness_ref, filled, sems,
):
    elements, slots, rows, _ = left_ref.shape
    coarse = rows // 2
    copies = fetch([(stiffness_hbm, stiffness_ref)], sems)
    me = lax.axis_index("grp")
    for t in range(filled.shape[0]):
        filled[t] = 0
    for i in range(order_ref.shape[0]):
        order_ref[i] = elements
    for e in range(elements):
        away = lax.bitwise_xor(owner_ref[0, e], me)
        position = filled[away]
        filled[away] = position + 1
        order_ref[away * capacity + position] = e

    copies[0].wait()
    own = prolong_ref[...]
    for s in range(slots):
        first = jnp.dot(own, stiffness_ref[s, 0], preferred_element_type=jnp.float32)
        second = jnp.dot(own, stiffness_ref[s, 1], preferred_element_type=jnp.float32)
        for e in range(elements):
            part = slice(e * coarse, (e + 1) * coarse)
            total = lame_ref[s, 0, e] * first[part] + lame_ref[s, 1, e] * second[part]
            high = total.astype(jnp.bfloat16).astype(jnp.float32)
            left_ref[e, s] = jnp.concatenate([high, total - high], axis=0).astype(jnp.bfloat16)


def rows_kernel(columns_ref, order_ref, prolong_ref, even_ref, odd_ref, left_ref, *refs):
    sends, (table, packed) = refs[:-2], refs[-2:]
    elements, slots, rows, fine = left_ref.shape
    coarse = rows // 2
    ghosts = 2 * odd_ref.shape[0]
    odd_row = lax.rem(lax.axis_index("row"), 2)
    half = fine - LANES
    capacity = sends[0].shape[0]
    for e in range(elements):
        table[e] = prolong_ref[e * coarse : (e + 1) * coarse].astype(jnp.float32)
    for start, ref in ((elements + ghosts * (1 - odd_row), even_ref), (elements + ghosts * odd_row, odd_ref)):
        for pair in range(ghosts // 2):
            block = ref[pair].astype(jnp.float32)
            tail = block[2 * coarse :]
            for odd in range(2):
                table[start + 2 * pair + odd] = jnp.concatenate(
                    [block[odd * coarse : (odd + 1) * coarse], tail[:, odd * half : (odd + 1) * half]], axis=1
                )
    table[elements + 2 * ghosts] = jnp.zeros((coarse, fine), jnp.float32)

    lane8 = lax.broadcasted_iota(jnp.int32, (8, LANES), 1)
    packed[elements] = jnp.concatenate(
        [jnp.zeros((coarse, LANES), jnp.float32), jnp.where(lane8 >= 120, -1.0, 0.0)], axis=0
    ).astype(jnp.bfloat16)

    width = slots * coarse
    lane = lax.broadcasted_iota(jnp.int32, (coarse, width), 1)
    for e in range(elements):
        blocks = []
        for s in range(slots):
            c = columns_ref[s, e]
            blocks.append(table[jnp.where(c < 0, elements + 2 * ghosts, c)])
        right = jnp.concatenate(blocks, axis=0).astype(jnp.bfloat16)
        left = left_ref[e].reshape(slots * 2 * coarse, fine)
        product = lax.dot_general(
            left, right, (((1,), (1,)), ((), ())), preferred_element_type=jnp.float32
        )
        result = None
        for s in range(slots):
            at = 2 * coarse * s
            part = product[at : at + coarse] + product[at + coarse : at + 2 * coarse]
            result = part if s == 0 else jnp.where(lane >= s * coarse, part, result)
        rest = result[:, LANES:]
        spare = jnp.full((8, 8), e, jnp.float32)
        tail = jnp.concatenate([rest[0:8], rest[8:16], rest[16:24], spare], axis=1)
        packed[e] = jnp.concatenate([result[:, :LANES], tail], axis=0).astype(jnp.bfloat16)
    for k, send in enumerate(sends):
        for p in range(capacity):
            send[p] = packed[order_ref[k * capacity + p]]


def unpack_kernel(elements, away, *refs):
    received, (rows_ref, ids_ref) = refs[:-2], refs[-2:]
    capacity = received[0].shape[0]
    rest = rows_ref.shape[2] - LANES
    count = rows_ref.shape[0]
    wide = pl.cdiv(count, LANES) * LANES
    me = lax.axis_index("grp")
    lane = lax.broadcasted_iota(jnp.int32, (8, wide), 1)
    local = jnp.full((8, wide), -1.0, jnp.float32)
    for k, ref in zip(away, received):
        first = lax.bitwise_xor(me, k) * capacity
        for p in range(capacity):
            block = ref[p].astype(jnp.float32)
            tail = block[24:32]
            rows_ref[first + p] = jnp.concatenate(
                [
                    block[0:24],
                    jnp.concatenate([tail[:, rest * q : rest * (q + 1)] for q in range(3)], axis=0),
                ],
                axis=1,
            ).astype(jnp.bfloat16)
            local = jnp.where(lane == first + p, tail[:, 127:128], local)
    local = local[0:1, :count].astype(jnp.int32)
    group = lax.broadcasted_iota(jnp.int32, (1, count), 1) // capacity
    first = (group * lax.axis_size("row") + lax.axis_index("row")) * elements
    ids_ref[...] = jnp.where(local >= 0, first + local, -1)


def on_device(stiffness, lame, prolong, columns, ghost_count, ghost_offset, owner_map):
    elements, coarse, fine = prolong.shape
    slots = stiffness.shape[0]
    ghosts = elements // 2
    owners = lax.axis_size("grp")
    capacity = 2 * ((elements + owners - 1) // owners)
    run = pltpu.VMEM((ghosts // 2, 3 * coarse, LANES), jnp.bfloat16)
    by_odd, by_even, own, lame_slots, by_slot, owner = pl.pallas_call(
        pack_kernel,
        out_shape=(
            run, run,
            pltpu.VMEM(prolong.shape, jnp.bfloat16),
            pltpu.SMEM((slots, 2, elements), jnp.float32),
            pltpu.SMEM((slots, elements), jnp.int32),
            pltpu.SMEM((1, elements), jnp.int32),
        ),
        in_specs=[HBM] * 6, out_specs=(VMEM,) * 3 + (SMEM,) * 3,
        scratch_shapes=[
            pltpu.SMEM(ghost_count.shape, jnp.int32),
            pltpu.SMEM(ghost_offset.shape, jnp.int32),
            pltpu.SemaphoreType.DMA((6,)),
        ],
        compiler_params=params(), name="pack",
    )(
        in_hbm(ghost_count), in_hbm(ghost_offset), in_hbm(prolong),
        in_hbm(lame.transpose(1, 2, 0)), in_hbm(columns.T), in_hbm(owner_map.T),
    )
    from_even = swapped(by_even, "row", 0)
    from_odd = swapped(by_odd, "row", 1)
    own = in_vmem(own.reshape(elements * coarse, fine))
    left, order = pl.pallas_call(
        functools.partial(left_kernel, capacity),
        out_shape=(
            pltpu.VMEM((elements, slots, 2 * coarse, fine), jnp.bfloat16),
            pltpu.SMEM((owners * capacity,), jnp.int32),
        ),
        in_specs=[SMEM, SMEM, HBM, VMEM], out_specs=(VMEM, SMEM),
        scratch_shapes=[
            pltpu.VMEM(stiffness.shape, jnp.bfloat16),
            pltpu.SMEM((owners,), jnp.int32),
            pltpu.SemaphoreType.DMA((1,)),
        ],
        compiler_params=params(), name="left",
    )(in_smem(lame_slots), in_smem(owner), in_hbm(stiffness), own)
    sends = pl.pallas_call(
        rows_kernel,
        out_shape=[pltpu.VMEM((capacity, 32, LANES), jnp.bfloat16)] * owners,
        in_specs=[SMEM, SMEM, VMEM, VMEM, VMEM, VMEM], out_specs=[VMEM] * owners,
        scratch_shapes=[
            pltpu.VMEM((elements + 2 * ghosts + 1, coarse, fine), jnp.float32),
            pltpu.VMEM((elements + 1, 32, LANES), jnp.bfloat16),
        ],
        compiler_params=params(), name="rows",
    )(
        in_smem(by_slot), in_smem(order), own,
        in_vmem(from_even), in_vmem(from_odd), in_vmem(left),
    )
    arrival = [*range(2, owners), 1]
    received = {0: sends[0]}
    for k in arrival:
        received[k] = lax.ppermute(sends[k], "grp", [(i, i ^ k) for i in range(owners)])
    coarse_rows, ids = pl.pallas_call(
        functools.partial(unpack_kernel, elements, (*arrival, 0)),
        out_shape=(
            jax.ShapeDtypeStruct((owners * capacity, coarse, slots * coarse), jnp.bfloat16),
            jax.ShapeDtypeStruct((1, owners * capacity), jnp.int32),
        ),
        in_specs=[VMEM] * owners, out_specs=(VMEM, VMEM),
        compiler_params=params(), name="unpack",
    )(*[in_vmem(received[k]) for k in (*arrival, 0)])
    return (coarse_rows, ids.reshape(-1))


def solution(mesh):
    split = ("grp", "row")
    return jax.shard_map(
        on_device, mesh=mesh,
        in_specs=(P(), P(split, None, None), P(split, None, None)) + (P(split, None),) * 4,
        out_specs=(P(split, None, None), P(split)), check_vma=False,
    )
```

```python
import functools

import jax
import jax.numpy as jnp
from jax import lax
from jax.experimental import pallas as pl
from jax.experimental.pallas import tpu as pltpu
from jax.sharding import PartitionSpec as P

LANES = 128
VMEM = pl.BlockSpec(memory_space=pltpu.VMEM)
HBM = pl.BlockSpec(memory_space=pltpu.HBM)
SMEM = pl.BlockSpec(memory_space=pltpu.SMEM)


def in_vmem(value):
    return pltpu.with_memory_space_constraint(value, pltpu.VMEM)


def in_smem(value):
    return pltpu.with_memory_space_constraint(value, pltpu.SMEM)


def in_hbm(value):
    return pltpu.with_memory_space_constraint(value, pltpu.HBM)


def params():
    return pltpu.CompilerParams(vmem_limit_bytes=24 * 1024 * 1024)


def swapped(value, axis, parity):
    peers = lax.axis_size(axis)
    pairs = [(i, i + 1) for i in range(parity, peers - 1, 2)]
    return lax.ppermute(value, axis, pairs + [(j, i) for i, j in pairs])


def fetch(pairs, sems):
    copies = [pltpu.make_async_copy(src, dst, sems.at[i]) for i, (src, dst) in enumerate(pairs)]
    for copy in copies:
        copy.start()
    return copies


def pack_kernel(
    count_hbm, offset_hbm, prolong_hbm, lame_hbm, columns_hbm, owner_hbm,
    odd_ref, even_ref, prolong_ref, lame_ref, columns_ref, owner_ref,
    count_ref, offset_ref, sems,
):
    copies = fetch(
        [
            (prolong_hbm, prolong_ref), (count_hbm, count_ref), (offset_hbm, offset_ref),
            (lame_hbm, lame_ref), (columns_hbm, columns_ref), (owner_hbm, owner_ref),
        ],
        sems,
    )
    for copy in copies:
        copy.wait()
    elements = prolong_ref.shape[0]
    odd_row = lax.rem(lax.axis_index("row"), 2)
    for way, out_ref in ((odd_row, odd_ref), (1 - odd_row, even_ref)):
        first = offset_ref[0, way]
        length = count_ref[0, way]

        def block(slot):
            value = prolong_ref[jnp.minimum(first + slot, elements - 1)].astype(jnp.float32)
            return jnp.where(slot < length, value, 0.0)

        for pair in range(out_ref.shape[0]):
            even, odd = block(2 * pair), block(2 * pair + 1)
            tail = jnp.concatenate([even[:, LANES:], odd[:, LANES:]], axis=1)
            out_ref[pair] = jnp.concatenate(
                [even[:, :LANES], odd[:, :LANES], tail], axis=0
            ).astype(jnp.bfloat16)


def left_kernel(
    capacity, lame_ref, owner_ref, stiffness_hbm, prolong_ref, left_ref, order_ref, stiffness_ref, filled, sems,
):
    elements, slots, rows, _ = left_ref.shape
    coarse = rows // 2
    copies = fetch([(stiffness_hbm, stiffness_ref)], sems)
    me = lax.axis_index("grp")
    for t in range(filled.shape[0]):
        filled[t] = 0
    for i in range(order_ref.shape[0]):
        order_ref[i] = elements
    for e in range(elements):
        away = lax.bitwise_xor(owner_ref[0, e], me)
        position = filled[away]
        filled[away] = position + 1
        order_ref[away * capacity + position] = e

    copies[0].wait()
    own = prolong_ref[...]
    for s in range(slots):
        first = jnp.dot(own, stiffness_ref[s, 0], preferred_element_type=jnp.float32)
        second = jnp.dot(own, stiffness_ref[s, 1], preferred_element_type=jnp.float32)
        for e in range(elements):
            part = slice(e * coarse, (e + 1) * coarse)
            total = lame_ref[s, 0, e] * first[part] + lame_ref[s, 1, e] * second[part]
            high = total.astype(jnp.bfloat16).astype(jnp.float32)
            left_ref[e, s] = jnp.concatenate([high, total - high], axis=0).astype(jnp.bfloat16)


def rows_kernel(columns_ref, order_ref, prolong_ref, even_ref, odd_ref, left_ref, *refs):
    sends, (table, packed) = refs[:-2], refs[-2:]
    elements, slots, rows, fine = left_ref.shape
    coarse = rows // 2
    ghosts = 2 * odd_ref.shape[0]
    odd_row = lax.rem(lax.axis_index("row"), 2)
    half = fine - LANES
    capacity = sends[0].shape[0]
    for e in range(elements):
        table[e] = prolong_ref[e * coarse : (e + 1) * coarse].astype(jnp.float32)
    for start, ref in ((elements + ghosts * (1 - odd_row), even_ref), (elements + ghosts * odd_row, odd_ref)):
        for pair in range(ghosts // 2):
            block = ref[pair].astype(jnp.float32)
            tail = block[2 * coarse :]
            for odd in range(2):
                table[start + 2 * pair + odd] = jnp.concatenate(
                    [block[odd * coarse : (odd + 1) * coarse], tail[:, odd * half : (odd + 1) * half]], axis=1
                )
    table[elements + 2 * ghosts] = jnp.zeros((coarse, fine), jnp.float32)

    lane8 = lax.broadcasted_iota(jnp.int32, (8, LANES), 1)
    packed[elements] = jnp.concatenate(
        [jnp.zeros((coarse, LANES), jnp.float32), jnp.where(lane8 >= 120, -1.0, 0.0)], axis=0
    ).astype(jnp.bfloat16)

    width = slots * coarse
    lane = lax.broadcasted_iota(jnp.int32, (coarse, width), 1)
    for e in range(elements):
        blocks = []
        for s in range(slots):
            c = columns_ref[s, e]
            blocks.append(table[jnp.where(c < 0, elements + 2 * ghosts, c)])
        right = jnp.concatenate(blocks, axis=0).astype(jnp.bfloat16)
        left = left_ref[e].reshape(slots * 2 * coarse, fine)
        product = lax.dot_general(
            left, right, (((1,), (1,)), ((), ())), preferred_element_type=jnp.float32
        )
        result = None
        for s in range(slots):
            at = 2 * coarse * s
            part = product[at : at + coarse] + product[at + coarse : at + 2 * coarse]
            result = part if s == 0 else jnp.where(lane >= s * coarse, part, result)
        rest = result[:, LANES:]
        spare = jnp.full((8, 8), e, jnp.float32)
        tail = jnp.concatenate([rest[0:8], rest[8:16], rest[16:24], spare], axis=1)
        packed[e] = jnp.concatenate([result[:, :LANES], tail], axis=0).astype(jnp.bfloat16)
    for k, send in enumerate(sends):
        for p in range(capacity):
            send[p] = packed[order_ref[k * capacity + p]]


def unpack_kernel(elements, away, *refs):
    received, (rows_ref, ids_ref) = refs[:-2], refs[-2:]
    capacity = received[0].shape[0]
    rest = rows_ref.shape[2] - LANES
    count = rows_ref.shape[0]
    wide = pl.cdiv(count, LANES) * LANES
    me = lax.axis_index("grp")
    lane = lax.broadcasted_iota(jnp.int32, (8, wide), 1)
    local = jnp.full((8, wide), -1.0, jnp.float32)
    for k, ref in zip(away, received):
        first = lax.bitwise_xor(me, k) * capacity
        for p in range(capacity):
            block = ref[p].astype(jnp.float32)
            tail = block[24:32]
            rows_ref[first + p] = jnp.concatenate(
                [
                    block[0:24],
                    jnp.concatenate([tail[:, rest * q : rest * (q + 1)] for q in range(3)], axis=0),
                ],
                axis=1,
            ).astype(jnp.bfloat16)
            local = jnp.where(lane == first + p, tail[:, 127:128], local)
    local = local[0:1, :count].astype(jnp.int32)
    group = lax.broadcasted_iota(jnp.int32, (1, count), 1) // capacity
    first = (group * lax.axis_size("row") + lax.axis_index("row")) * elements
    ids_ref[...] = jnp.where(local >= 0, first + local, -1)


def on_device(stiffness, lame, prolong, columns, ghost_count, ghost_offset, owner_map):
    elements, coarse, fine = prolong.shape
    slots = stiffness.shape[0]
    ghosts = elements // 2
    owners = lax.axis_size("grp")
    capacity = 2 * ((elements + owners - 1) // owners)
    run = pltpu.VMEM((ghosts // 2, 3 * coarse, LANES), jnp.bfloat16)
    by_odd, by_even, own, lame_slots, by_slot, owner = pl.pallas_call(
        pack_kernel,
        out_shape=(
            run, run,
            pltpu.VMEM(prolong.shape, jnp.bfloat16),
            pltpu.SMEM((slots, 2, elements), jnp.float32),
            pltpu.SMEM((slots, elements), jnp.int32),
            pltpu.SMEM((1, elements), jnp.int32),
        ),
        in_specs=[HBM] * 6, out_specs=(VMEM,) * 3 + (SMEM,) * 3,
        scratch_shapes=[
            pltpu.SMEM(ghost_count.shape, jnp.int32),
            pltpu.SMEM(ghost_offset.shape, jnp.int32),
            pltpu.SemaphoreType.DMA((6,)),
        ],
        compiler_params=params(), name="pack",
    )(
        in_hbm(ghost_count), in_hbm(ghost_offset), in_hbm(prolong),
        in_hbm(lame.transpose(1, 2, 0)), in_hbm(columns.T), in_hbm(owner_map.T),
    )
    from_even = swapped(by_even, "row", 0)
    from_odd = swapped(by_odd, "row", 1)
    own = in_vmem(own.reshape(elements * coarse, fine))
    left, order = pl.pallas_call(
        functools.partial(left_kernel, capacity),
        out_shape=(
            pltpu.VMEM((elements, slots, 2 * coarse, fine), jnp.bfloat16),
            pltpu.SMEM((owners * capacity,), jnp.int32),
        ),
        in_specs=[SMEM, SMEM, HBM, VMEM], out_specs=(VMEM, SMEM),
        scratch_shapes=[
            pltpu.VMEM(stiffness.shape, jnp.bfloat16),
            pltpu.SMEM((owners,), jnp.int32),
            pltpu.SemaphoreType.DMA((1,)),
        ],
        compiler_params=params(), name="left",
    )(in_smem(lame_slots), in_smem(owner), in_hbm(stiffness), own)
    sends = pl.pallas_call(
        rows_kernel,
        out_shape=[pltpu.VMEM((capacity, 32, LANES), jnp.bfloat16)] * owners,
        in_specs=[SMEM, SMEM, VMEM, VMEM, VMEM, VMEM], out_specs=[VMEM] * owners,
        scratch_shapes=[
            pltpu.VMEM((elements + 2 * ghosts + 1, coarse, fine), jnp.float32),
            pltpu.VMEM((elements + 1, 32, LANES), jnp.bfloat16),
        ],
        compiler_params=params(), name="rows",
    )(
        in_smem(by_slot), in_smem(order), own,
        in_vmem(from_even), in_vmem(from_odd), in_vmem(left),
    )
    arrival = range(owners - 1, 0, -1)
    received = {0: sends[0]}
    for k in arrival:
        received[k] = lax.ppermute(sends[k], "grp", [(i, i ^ k) for i in range(owners)])
    coarse_rows, ids = pl.pallas_call(
        functools.partial(unpack_kernel, elements, (*arrival, 0)),
        out_shape=(
            jax.ShapeDtypeStruct((owners * capacity, coarse, slots * coarse), jnp.bfloat16),
            jax.ShapeDtypeStruct((1, owners * capacity), jnp.int32),
        ),
        in_specs=[VMEM] * owners, out_specs=(VMEM, VMEM),
        compiler_params=params(), name="unpack",
    )(*[in_vmem(received[k]) for k in (*arrival, 0)])
    return (coarse_rows, ids.reshape(-1))


def solution(mesh):
    split = ("grp", "row")
    return jax.shard_map(
        on_device, mesh=mesh,
        in_specs=(P(), P(split, None, None), P(split, None, None)) + (P(split, None),) * 4,
        out_specs=(P(split, None, None), P(split)), check_vma=False,
    )
```

```python
import functools

import jax
import jax.numpy as jnp
from jax import lax
from jax.experimental import pallas as pl
from jax.experimental.pallas import tpu as pltpu
from jax.sharding import PartitionSpec as P

LANES = 128
VMEM = pl.BlockSpec(memory_space=pltpu.VMEM)
HBM = pl.BlockSpec(memory_space=pltpu.HBM)
SMEM = pl.BlockSpec(memory_space=pltpu.SMEM)


def in_vmem(value):
    return pltpu.with_memory_space_constraint(value, pltpu.VMEM)


def in_smem(value):
    return pltpu.with_memory_space_constraint(value, pltpu.SMEM)


def in_hbm(value):
    return pltpu.with_memory_space_constraint(value, pltpu.HBM)


def params():
    return pltpu.CompilerParams(vmem_limit_bytes=24 * 1024 * 1024)


def swapped(value, axis, parity):
    peers = lax.axis_size(axis)
    pairs = [(i, i + 1) for i in range(parity, peers - 1, 2)]
    return lax.ppermute(value, axis, pairs + [(j, i) for i, j in pairs])


def exchanges(owners):
    same, cross = range(2, owners, 2), range(3, owners, 2)
    return (
        [(k, (1,)) for k in same] + [(k, (0, 1)) for k in cross] + [(k, (0,)) for k in same] + [(1, (0, 1))]
    )


def fetch(pairs, sems):
    copies = [pltpu.make_async_copy(src, dst, sems.at[i]) for i, (src, dst) in enumerate(pairs)]
    for copy in copies:
        copy.start()
    return copies


def pack_kernel(
    count_hbm, offset_hbm, prolong_hbm, lame_hbm, columns_hbm, owner_hbm,
    odd_ref, even_ref, prolong_ref, lame_ref, columns_ref, owner_ref,
    count_ref, offset_ref, sems,
):
    copies = fetch(
        [
            (prolong_hbm, prolong_ref), (count_hbm, count_ref), (offset_hbm, offset_ref),
            (lame_hbm, lame_ref), (columns_hbm, columns_ref), (owner_hbm, owner_ref),
        ],
        sems,
    )
    for copy in copies:
        copy.wait()
    elements = prolong_ref.shape[0]
    odd_row = lax.rem(lax.axis_index("row"), 2)
    for way, out_ref in ((odd_row, odd_ref), (1 - odd_row, even_ref)):
        first = offset_ref[0, way]
        length = count_ref[0, way]

        def block(slot):
            value = prolong_ref[jnp.minimum(first + slot, elements - 1)].astype(jnp.float32)
            return jnp.where(slot < length, value, 0.0)

        for pair in range(out_ref.shape[0]):
            even, odd = block(2 * pair), block(2 * pair + 1)
            tail = jnp.concatenate([even[:, LANES:], odd[:, LANES:]], axis=1)
            out_ref[pair] = jnp.concatenate(
                [even[:, :LANES], odd[:, :LANES], tail], axis=0
            ).astype(jnp.bfloat16)


def left_kernel(
    capacity, lame_ref, owner_ref, stiffness_hbm, prolong_ref, left_ref, order_ref, table_ref,
    stiffness_ref, filled, sems,
):
    elements, slots, rows, _ = left_ref.shape
    coarse = rows // 2
    copies = fetch([(stiffness_hbm, stiffness_ref)], sems)
    me = lax.axis_index("grp")
    for t in range(filled.shape[0]):
        filled[t] = 0
    for i in range(order_ref.shape[0]):
        order_ref[i] = elements
    for e in range(elements):
        away = lax.bitwise_xor(owner_ref[0, e], me)
        position = filled[away]
        filled[away] = position + 1
        order_ref[away * capacity + position] = e

    for e in range(elements):
        table_ref[e] = prolong_ref[e * coarse : (e + 1) * coarse].astype(jnp.float32)
    table_ref[table_ref.shape[0] - 1] = jnp.zeros(table_ref.shape[1:], jnp.float32)
    copies[0].wait()
    own = prolong_ref[...]
    for s in range(slots):
        first = jnp.dot(own, stiffness_ref[s, 0], preferred_element_type=jnp.float32)
        second = jnp.dot(own, stiffness_ref[s, 1], preferred_element_type=jnp.float32)
        for e in range(elements):
            part = slice(e * coarse, (e + 1) * coarse)
            total = lame_ref[s, 0, e] * first[part] + lame_ref[s, 1, e] * second[part]
            high = total.astype(jnp.bfloat16).astype(jnp.float32)
            left_ref[e, s] = jnp.concatenate([high, total - high], axis=0).astype(jnp.bfloat16)


def rows_kernel(away, columns_ref, order_ref, even_ref, odd_ref, left_ref, _, *refs):
    sends, (table, packed) = refs[:-2], refs[-2:]
    elements, slots, rows, fine = left_ref.shape
    coarse = rows // 2
    ghosts = 2 * odd_ref.shape[0]
    odd_row = lax.rem(lax.axis_index("row"), 2)
    half = fine - LANES
    capacity = sends[0].shape[0]
    for start, ref in ((elements + ghosts * (1 - odd_row), even_ref), (elements + ghosts * odd_row, odd_ref)):
        for pair in range(ghosts // 2):
            block = ref[pair].astype(jnp.float32)
            tail = block[2 * coarse :]
            for odd in range(2):
                table[start + 2 * pair + odd] = jnp.concatenate(
                    [block[odd * coarse : (odd + 1) * coarse], tail[:, odd * half : (odd + 1) * half]], axis=1
                )

    lane8 = lax.broadcasted_iota(jnp.int32, (8, LANES), 1)
    packed[elements] = jnp.concatenate(
        [jnp.zeros((coarse, LANES), jnp.float32), jnp.where(lane8 >= 120, -1.0, 0.0)], axis=0
    ).astype(jnp.bfloat16)

    width = slots * coarse
    lane = lax.broadcasted_iota(jnp.int32, (coarse, width), 1)
    for e in range(elements):
        blocks = []
        for s in range(slots):
            c = columns_ref[s, e]
            blocks.append(table[jnp.where(c < 0, elements + 2 * ghosts, c)])
        right = jnp.concatenate(blocks, axis=0).astype(jnp.bfloat16)
        left = left_ref[e].reshape(slots * 2 * coarse, fine)
        product = lax.dot_general(
            left, right, (((1,), (1,)), ((), ())), preferred_element_type=jnp.float32
        )
        result = None
        for s in range(slots):
            at = 2 * coarse * s
            part = product[at : at + coarse] + product[at + coarse : at + 2 * coarse]
            result = part if s == 0 else jnp.where(lane >= s * coarse, part, result)
        rest = result[:, LANES:]
        spare = jnp.full((8, 8), e, jnp.float32)
        tail = jnp.concatenate([rest[0:8], rest[8:16], rest[16:24], spare], axis=1)
        packed[e] = jnp.concatenate([result[:, :LANES], tail], axis=0).astype(jnp.bfloat16)
    for k, send in zip(away, sends):
        for p in range(capacity):
            send[p] = packed[order_ref[k * capacity + p]]


def unpack_kernel(elements, away, *refs):
    received, (rows_ref, ids_ref) = refs[:-2], refs[-2:]
    capacity = received[0].shape[0]
    rest = rows_ref.shape[2] - LANES
    count = rows_ref.shape[0]
    wide = pl.cdiv(count, LANES) * LANES
    me = lax.axis_index("grp")
    lane = lax.broadcasted_iota(jnp.int32, (8, wide), 1)
    local = jnp.full((8, wide), -1.0, jnp.float32)
    for k in sorted(set(away)):
        first = lax.bitwise_xor(me, k) * capacity
        for p in range(capacity):
            block = sum(ref[p].astype(jnp.float32) for way, ref in zip(away, received) if way == k)
            tail = block[24:32]
            rows_ref[first + p] = jnp.concatenate(
                [
                    block[0:24],
                    jnp.concatenate([tail[:, rest * q : rest * (q + 1)] for q in range(3)], axis=0),
                ],
                axis=1,
            ).astype(jnp.bfloat16)
            local = jnp.where(lane == first + p, tail[:, 127:128], local)
    local = local[0:1, :count].astype(jnp.int32)
    group = lax.broadcasted_iota(jnp.int32, (1, count), 1) // capacity
    first = (group * lax.axis_size("row") + lax.axis_index("row")) * elements
    ids_ref[...] = jnp.where(local >= 0, first + local, -1)


def on_device(stiffness, lame, prolong, columns, ghost_count, ghost_offset, owner_map):
    elements, coarse, fine = prolong.shape
    slots = stiffness.shape[0]
    ghosts = elements // 2
    owners = lax.axis_size("grp")
    capacity = 2 * ((elements + owners - 1) // owners)
    run = pltpu.VMEM((ghosts // 2, 3 * coarse, LANES), jnp.bfloat16)
    by_odd, by_even, own, lame_slots, by_slot, owner = pl.pallas_call(
        pack_kernel,
        out_shape=(
            run, run,
            pltpu.VMEM(prolong.shape, jnp.bfloat16),
            pltpu.SMEM((slots, 2, elements), jnp.float32),
            pltpu.SMEM((slots, elements), jnp.int32),
            pltpu.SMEM((1, elements), jnp.int32),
        ),
        in_specs=[HBM] * 6, out_specs=(VMEM,) * 3 + (SMEM,) * 3,
        scratch_shapes=[
            pltpu.SMEM(ghost_count.shape, jnp.int32),
            pltpu.SMEM(ghost_offset.shape, jnp.int32),
            pltpu.SemaphoreType.DMA((6,)),
        ],
        compiler_params=params(), name="pack",
    )(
        in_hbm(ghost_count), in_hbm(ghost_offset), in_hbm(prolong),
        in_hbm(lame.transpose(1, 2, 0)), in_hbm(columns.T), in_hbm(owner_map.T),
    )
    from_even = swapped(by_even, "row", 0)
    from_odd = swapped(by_odd, "row", 1)
    own = in_vmem(own.reshape(elements * coarse, fine))
    table = pltpu.VMEM((elements + 2 * ghosts + 1, coarse, fine), jnp.float32)
    left, order, local = pl.pallas_call(
        functools.partial(left_kernel, capacity),
        out_shape=(
            pltpu.VMEM((elements, slots, 2 * coarse, fine), jnp.bfloat16),
            pltpu.SMEM((owners * capacity,), jnp.int32),
            table,
        ),
        in_specs=[SMEM, SMEM, HBM, VMEM], out_specs=(VMEM, SMEM, VMEM),
        scratch_shapes=[
            pltpu.VMEM(stiffness.shape, jnp.bfloat16),
            pltpu.SMEM((owners,), jnp.int32),
            pltpu.SemaphoreType.DMA((1,)),
        ],
        compiler_params=params(), name="left",
    )(in_smem(lame_slots), in_smem(owner), in_hbm(stiffness), own)
    steps = exchanges(owners)
    away = [k for k, _ in steps] + [0]
    *sends, own_rows, _ = pl.pallas_call(
        functools.partial(rows_kernel, away),
        out_shape=[pltpu.VMEM((capacity, 32, LANES), jnp.bfloat16)] * len(away) + [table],
        in_specs=[SMEM, SMEM, VMEM, VMEM, VMEM, VMEM], out_specs=[VMEM] * (len(away) + 1),
        scratch_shapes=[pltpu.VMEM((elements + 1, 32, LANES), jnp.bfloat16)],
        input_output_aliases={5: len(away)},
        compiler_params=params(), name="rows",
    )(
        in_smem(by_slot), in_smem(order),
        in_vmem(from_even), in_vmem(from_odd), in_vmem(left), in_vmem(local),
    )
    received = [
        lax.ppermute(send, "grp", [(i, i ^ k) for i in range(owners) if i % 2 in parities])
        for send, (k, parities) in zip(sends, steps)
    ]
    coarse_rows, ids = pl.pallas_call(
        functools.partial(unpack_kernel, elements, away),
        out_shape=(
            jax.ShapeDtypeStruct((owners * capacity, coarse, slots * coarse), jnp.bfloat16),
            jax.ShapeDtypeStruct((1, owners * capacity), jnp.int32),
        ),
        in_specs=[VMEM] * len(away), out_specs=(VMEM, VMEM),
        compiler_params=params(), name="unpack",
    )(*[in_vmem(value) for value in received], in_vmem(own_rows))
    return (coarse_rows, ids.reshape(-1))


def solution(mesh):
    split = ("grp", "row")
    return jax.shard_map(
        on_device, mesh=mesh,
        in_specs=(P(), P(split, None, None), P(split, None, None)) + (P(split, None),) * 4,
        out_specs=(P(split, None, None), P(split)), check_vma=False,
    )
```

```python
import functools

import jax
import jax.numpy as jnp
from jax import lax
from jax.experimental import pallas as pl
from jax.experimental.pallas import tpu as pltpu
from jax.sharding import PartitionSpec as P

LANES = 128
VMEM = pl.BlockSpec(memory_space=pltpu.VMEM)
HBM = pl.BlockSpec(memory_space=pltpu.HBM)
SMEM = pl.BlockSpec(memory_space=pltpu.SMEM)


def in_vmem(value):
    return pltpu.with_memory_space_constraint(value, pltpu.VMEM)


def in_smem(value):
    return pltpu.with_memory_space_constraint(value, pltpu.SMEM)


def in_hbm(value):
    return pltpu.with_memory_space_constraint(value, pltpu.HBM)


def params():
    return pltpu.CompilerParams(vmem_limit_bytes=24 * 1024 * 1024)


def swapped(value, axis, parity):
    peers = lax.axis_size(axis)
    pairs = [(i, i + 1) for i in range(parity, peers - 1, 2)]
    alone = set(range(peers)) - {i for pair in pairs for i in pair}
    return lax.ppermute(value, axis, pairs + [(j, i) for i, j in pairs] + [(i, i) for i in sorted(alone)])


def fetch(pairs, sems):
    copies = [pltpu.make_async_copy(src, dst, sems.at[i]) for i, (src, dst) in enumerate(pairs)]
    for copy in copies:
        copy.start()
    return copies


def pack_kernel(
    count_hbm, offset_hbm, prolong_hbm, lame_hbm, columns_hbm, owner_hbm,
    odd_ref, even_ref, prolong_ref, lame_ref, columns_ref, owner_ref,
    count_ref, offset_ref, sems,
):
    copies = fetch(
        [
            (prolong_hbm, prolong_ref), (count_hbm, count_ref), (offset_hbm, offset_ref),
            (lame_hbm, lame_ref), (columns_hbm, columns_ref), (owner_hbm, owner_ref),
        ],
        sems,
    )
    for copy in copies:
        copy.wait()
    elements = prolong_ref.shape[0]
    odd_row = lax.rem(lax.axis_index("row"), 2)
    for way, out_ref in ((odd_row, odd_ref), (1 - odd_row, even_ref)):
        first = offset_ref[0, way]
        length = count_ref[0, way]

        def block(slot):
            value = prolong_ref[jnp.minimum(first + slot, elements - 1)].astype(jnp.float32)
            return jnp.where(slot < length, value, 0.0)

        for pair in range(out_ref.shape[0]):
            even, odd = block(2 * pair), block(2 * pair + 1)
            tail = jnp.concatenate([even[:, LANES:], odd[:, LANES:]], axis=1)
            out_ref[pair] = jnp.concatenate(
                [even[:, :LANES], odd[:, :LANES], tail], axis=0
            ).astype(jnp.bfloat16)


def left_kernel(
    capacity, lame_ref, owner_ref, stiffness_hbm, prolong_ref, left_ref, order_ref, stiffness_ref, filled, sems,
):
    elements, slots, rows, _ = left_ref.shape
    coarse = rows // 2
    copies = fetch([(stiffness_hbm, stiffness_ref)], sems)
    me = lax.axis_index("grp")
    for t in range(filled.shape[0]):
        filled[t] = 0
    for i in range(order_ref.shape[0]):
        order_ref[i] = elements
    for e in range(elements):
        away = lax.bitwise_xor(owner_ref[0, e], me)
        position = filled[away]
        filled[away] = position + 1
        order_ref[away * capacity + position] = e

    copies[0].wait()
    own = prolong_ref[...]
    for s in range(slots):
        first = jnp.dot(own, stiffness_ref[s, 0], preferred_element_type=jnp.float32)
        second = jnp.dot(own, stiffness_ref[s, 1], preferred_element_type=jnp.float32)
        for e in range(elements):
            part = slice(e * coarse, (e + 1) * coarse)
            total = lame_ref[s, 0, e] * first[part] + lame_ref[s, 1, e] * second[part]
            high = total.astype(jnp.bfloat16).astype(jnp.float32)
            left_ref[e, s] = jnp.concatenate([high, total - high], axis=0).astype(jnp.bfloat16)


def rows_kernel(columns_ref, order_ref, prolong_ref, even_ref, odd_ref, left_ref, *refs):
    sends, (table, packed) = refs[:-2], refs[-2:]
    elements, slots, rows, fine = left_ref.shape
    coarse = rows // 2
    ghosts = 2 * odd_ref.shape[0]
    row, last = lax.axis_index("row"), lax.axis_size("row") - 1
    half = fine - LANES
    capacity = sends[0].shape[0]
    for e in range(elements):
        table[e] = prolong_ref[e * coarse : (e + 1) * coarse].astype(jnp.float32)
    for parity, ref in enumerate((even_ref, odd_ref)):
        from_above = lax.rem(row, 2) == parity
        start = jnp.where(from_above, elements + ghosts, elements)
        has_partner = jnp.where(from_above, row < last, row > 0)
        for pair in range(ghosts // 2):
            block = jnp.where(has_partner, ref[pair].astype(jnp.float32), 0.0)
            tail = block[2 * coarse :]
            for odd in range(2):
                table[start + 2 * pair + odd] = jnp.concatenate(
                    [block[odd * coarse : (odd + 1) * coarse], tail[:, odd * half : (odd + 1) * half]], axis=1
                )
    table[elements + 2 * ghosts] = jnp.zeros((coarse, fine), jnp.float32)

    lane8 = lax.broadcasted_iota(jnp.int32, (8, LANES), 1)
    packed[elements] = jnp.concatenate(
        [jnp.zeros((coarse, LANES), jnp.float32), jnp.where(lane8 >= 120, -1.0, 0.0)], axis=0
    ).astype(jnp.bfloat16)

    width = slots * coarse
    lane = lax.broadcasted_iota(jnp.int32, (coarse, width), 1)
    for e in range(elements):
        blocks = []
        for s in range(slots):
            c = columns_ref[s, e]
            blocks.append(table[jnp.where(c < 0, elements + 2 * ghosts, c)])
        right = jnp.concatenate(blocks, axis=0).astype(jnp.bfloat16)
        left = left_ref[e].reshape(slots * 2 * coarse, fine)
        product = lax.dot_general(
            left, right, (((1,), (1,)), ((), ())), preferred_element_type=jnp.float32
        )
        result = None
        for s in range(slots):
            at = 2 * coarse * s
            part = product[at : at + coarse] + product[at + coarse : at + 2 * coarse]
            result = part if s == 0 else jnp.where(lane >= s * coarse, part, result)
        rest = result[:, LANES:]
        spare = jnp.full((8, 8), e, jnp.float32)
        tail = jnp.concatenate([rest[0:8], rest[8:16], rest[16:24], spare], axis=1)
        packed[e] = jnp.concatenate([result[:, :LANES], tail], axis=0).astype(jnp.bfloat16)
    for k, send in enumerate(sends):
        for p in range(capacity):
            send[p] = packed[order_ref[k * capacity + p]]


def unpack_kernel(elements, away, *refs):
    received, (rows_ref, ids_ref) = refs[:-2], refs[-2:]
    capacity = received[0].shape[0]
    rest = rows_ref.shape[2] - LANES
    count = rows_ref.shape[0]
    wide = pl.cdiv(count, LANES) * LANES
    me = lax.axis_index("grp")
    lane = lax.broadcasted_iota(jnp.int32, (8, wide), 1)
    local = jnp.full((8, wide), -1.0, jnp.float32)
    for k, ref in zip(away, received):
        first = lax.bitwise_xor(me, k) * capacity
        for p in range(capacity):
            block = ref[p].astype(jnp.float32)
            tail = block[24:32]
            rows_ref[first + p] = jnp.concatenate(
                [
                    block[0:24],
                    jnp.concatenate([tail[:, rest * q : rest * (q + 1)] for q in range(3)], axis=0),
                ],
                axis=1,
            ).astype(jnp.bfloat16)
            local = jnp.where(lane == first + p, tail[:, 127:128], local)
    local = local[0:1, :count].astype(jnp.int32)
    group = lax.broadcasted_iota(jnp.int32, (1, count), 1) // capacity
    first = (group * lax.axis_size("row") + lax.axis_index("row")) * elements
    ids_ref[...] = jnp.where(local >= 0, first + local, -1)


def on_device(stiffness, lame, prolong, columns, ghost_count, ghost_offset, owner_map):
    elements, coarse, fine = prolong.shape
    slots = stiffness.shape[0]
    ghosts = elements // 2
    owners = lax.axis_size("grp")
    capacity = 2 * ((elements + owners - 1) // owners)
    run = pltpu.VMEM((ghosts // 2, 3 * coarse, LANES), jnp.bfloat16)
    by_odd, by_even, own, lame_slots, by_slot, owner = pl.pallas_call(
        pack_kernel,
        out_shape=(
            run, run,
            pltpu.VMEM(prolong.shape, jnp.bfloat16),
            pltpu.SMEM((slots, 2, elements), jnp.float32),
            pltpu.SMEM((slots, elements), jnp.int32),
            pltpu.SMEM((1, elements), jnp.int32),
        ),
        in_specs=[HBM] * 6, out_specs=(VMEM,) * 3 + (SMEM,) * 3,
        scratch_shapes=[
            pltpu.SMEM(ghost_count.shape, jnp.int32),
            pltpu.SMEM(ghost_offset.shape, jnp.int32),
            pltpu.SemaphoreType.DMA((6,)),
        ],
        compiler_params=params(), name="pack",
    )(
        in_hbm(ghost_count), in_hbm(ghost_offset), in_hbm(prolong),
        in_hbm(lame.transpose(1, 2, 0)), in_hbm(columns.T), in_hbm(owner_map.T),
    )
    from_even = swapped(by_even, "row", 0)
    from_odd = swapped(by_odd, "row", 1)
    own = in_vmem(own.reshape(elements * coarse, fine))
    left, order = pl.pallas_call(
        functools.partial(left_kernel, capacity),
        out_shape=(
            pltpu.VMEM((elements, slots, 2 * coarse, fine), jnp.bfloat16),
            pltpu.SMEM((owners * capacity,), jnp.int32),
        ),
        in_specs=[SMEM, SMEM, HBM, VMEM], out_specs=(VMEM, SMEM),
        scratch_shapes=[
            pltpu.VMEM(stiffness.shape, jnp.bfloat16),
            pltpu.SMEM((owners,), jnp.int32),
            pltpu.SemaphoreType.DMA((1,)),
        ],
        compiler_params=params(), name="left",
    )(in_smem(lame_slots), in_smem(owner), in_hbm(stiffness), own)
    sends = pl.pallas_call(
        rows_kernel,
        out_shape=[pltpu.VMEM((capacity, 32, LANES), jnp.bfloat16)] * owners,
        in_specs=[SMEM, SMEM, VMEM, VMEM, VMEM, VMEM], out_specs=[VMEM] * owners,
        scratch_shapes=[
            pltpu.VMEM((elements + 2 * ghosts + 1, coarse, fine), jnp.float32),
            pltpu.VMEM((elements + 1, 32, LANES), jnp.bfloat16),
        ],
        compiler_params=params(), name="rows",
    )(
        in_smem(by_slot), in_smem(order), own,
        in_vmem(from_even), in_vmem(from_odd), in_vmem(left),
    )
    arrival = [*range(2, owners), 1]
    received = {0: sends[0]}
    for k in arrival:
        received[k] = lax.ppermute(sends[k], "grp", [(i, i ^ k) for i in range(owners)])
    coarse_rows, ids = pl.pallas_call(
        functools.partial(unpack_kernel, elements, (*arrival, 0)),
        out_shape=(
            jax.ShapeDtypeStruct((owners * capacity, coarse, slots * coarse), jnp.bfloat16),
            jax.ShapeDtypeStruct((1, owners * capacity), jnp.int32),
        ),
        in_specs=[VMEM] * owners, out_specs=(VMEM, VMEM),
        compiler_params=params(), name="unpack",
    )(*[in_vmem(received[k]) for k in (*arrival, 0)])
    return (coarse_rows, ids.reshape(-1))


def solution(mesh):
    split = ("grp", "row")
    return jax.shard_map(
        on_device, mesh=mesh,
        in_specs=(P(), P(split, None, None), P(split, None, None)) + (P(split, None),) * 4,
        out_specs=(P(split, None, None), P(split)), check_vma=False,
    )
```

```python
import functools

import jax
import jax.numpy as jnp
from jax import lax
from jax.experimental import pallas as pl
from jax.experimental.pallas import tpu as pltpu
from jax.sharding import PartitionSpec as P

LANES = 128
VMEM = pl.BlockSpec(memory_space=pltpu.VMEM)
HBM = pl.BlockSpec(memory_space=pltpu.HBM)
SMEM = pl.BlockSpec(memory_space=pltpu.SMEM)


def in_vmem(value):
    return pltpu.with_memory_space_constraint(value, pltpu.VMEM)


def in_smem(value):
    return pltpu.with_memory_space_constraint(value, pltpu.SMEM)


def in_hbm(value):
    return pltpu.with_memory_space_constraint(value, pltpu.HBM)


def params():
    return pltpu.CompilerParams(vmem_limit_bytes=24 * 1024 * 1024)


def swapped(value, axis, parity):
    peers = lax.axis_size(axis)
    pairs = [(i, i + 1) for i in range(parity, peers - 1, 2)]
    alone = sorted(set(range(peers)) - {i for pair in pairs for i in pair})
    pairs += [(i, j) for i, j in zip(alone[::2], alone[1::2])]
    return lax.ppermute(value, axis, pairs + [(j, i) for i, j in pairs])


def fetch(pairs, sems):
    copies = [pltpu.make_async_copy(src, dst, sems.at[i]) for i, (src, dst) in enumerate(pairs)]
    for copy in copies:
        copy.start()
    return copies


def pack_kernel(
    count_hbm, offset_hbm, prolong_hbm, lame_hbm, columns_hbm, owner_hbm,
    odd_ref, even_ref, prolong_ref, lame_ref, columns_ref, owner_ref,
    count_ref, offset_ref, sems,
):
    copies = fetch(
        [
            (prolong_hbm, prolong_ref), (count_hbm, count_ref), (offset_hbm, offset_ref),
            (lame_hbm, lame_ref), (columns_hbm, columns_ref), (owner_hbm, owner_ref),
        ],
        sems,
    )
    for copy in copies:
        copy.wait()
    elements = prolong_ref.shape[0]
    odd_row = lax.rem(lax.axis_index("row"), 2)
    for way, out_ref in ((odd_row, odd_ref), (1 - odd_row, even_ref)):
        first = offset_ref[0, way]
        length = count_ref[0, way]

        def block(slot):
            value = prolong_ref[jnp.minimum(first + slot, elements - 1)].astype(jnp.float32)
            return jnp.where(slot < length, value, 0.0)

        for pair in range(out_ref.shape[0]):
            even, odd = block(2 * pair), block(2 * pair + 1)
            tail = jnp.concatenate([even[:, LANES:], odd[:, LANES:]], axis=1)
            out_ref[pair] = jnp.concatenate(
                [even[:, :LANES], odd[:, :LANES], tail], axis=0
            ).astype(jnp.bfloat16)


def left_kernel(
    capacity, lame_ref, owner_ref, stiffness_hbm, prolong_ref, left_ref, order_ref, stiffness_ref, filled, sems,
):
    elements, slots, rows, _ = left_ref.shape
    coarse = rows // 2
    copies = fetch([(stiffness_hbm, stiffness_ref)], sems)
    me = lax.axis_index("grp")
    for t in range(filled.shape[0]):
        filled[t] = 0
    for i in range(order_ref.shape[0]):
        order_ref[i] = elements
    for e in range(elements):
        away = lax.bitwise_xor(owner_ref[0, e], me)
        position = filled[away]
        filled[away] = position + 1
        order_ref[away * capacity + position] = e

    copies[0].wait()
    own = prolong_ref[...]
    for s in range(slots):
        first = jnp.dot(own, stiffness_ref[s, 0], preferred_element_type=jnp.float32)
        second = jnp.dot(own, stiffness_ref[s, 1], preferred_element_type=jnp.float32)
        for e in range(elements):
            part = slice(e * coarse, (e + 1) * coarse)
            total = lame_ref[s, 0, e] * first[part] + lame_ref[s, 1, e] * second[part]
            high = total.astype(jnp.bfloat16).astype(jnp.float32)
            left_ref[e, s] = jnp.concatenate([high, total - high], axis=0).astype(jnp.bfloat16)


def rows_kernel(columns_ref, order_ref, prolong_ref, even_ref, odd_ref, left_ref, *refs):
    sends, (table, packed) = refs[:-2], refs[-2:]
    elements, slots, rows, fine = left_ref.shape
    coarse = rows // 2
    ghosts = 2 * odd_ref.shape[0]
    row, last = lax.axis_index("row"), lax.axis_size("row") - 1
    half = fine - LANES
    capacity = sends[0].shape[0]
    for e in range(elements):
        table[e] = prolong_ref[e * coarse : (e + 1) * coarse].astype(jnp.float32)
    for parity, ref in enumerate((even_ref, odd_ref)):
        from_above = lax.rem(row, 2) == parity
        start = jnp.where(from_above, elements + ghosts, elements)
        has_partner = jnp.where(from_above, row < last, row > 0)
        for pair in range(ghosts // 2):
            block = jnp.where(has_partner, ref[pair].astype(jnp.float32), 0.0)
            tail = block[2 * coarse :]
            for odd in range(2):
                table[start + 2 * pair + odd] = jnp.concatenate(
                    [block[odd * coarse : (odd + 1) * coarse], tail[:, odd * half : (odd + 1) * half]], axis=1
                )
    table[elements + 2 * ghosts] = jnp.zeros((coarse, fine), jnp.float32)

    lane8 = lax.broadcasted_iota(jnp.int32, (8, LANES), 1)
    packed[elements] = jnp.concatenate(
        [jnp.zeros((coarse, LANES), jnp.float32), jnp.where(lane8 >= 120, -1.0, 0.0)], axis=0
    ).astype(jnp.bfloat16)

    width = slots * coarse
    lane = lax.broadcasted_iota(jnp.int32, (coarse, width), 1)
    for e in range(elements):
        blocks = []
        for s in range(slots):
            c = columns_ref[s, e]
            blocks.append(table[jnp.where(c < 0, elements + 2 * ghosts, c)])
        right = jnp.concatenate(blocks, axis=0).astype(jnp.bfloat16)
        left = left_ref[e].reshape(slots * 2 * coarse, fine)
        product = lax.dot_general(
            left, right, (((1,), (1,)), ((), ())), preferred_element_type=jnp.float32
        )
        result = None
        for s in range(slots):
            at = 2 * coarse * s
            part = product[at : at + coarse] + product[at + coarse : at + 2 * coarse]
            result = part if s == 0 else jnp.where(lane >= s * coarse, part, result)
        rest = result[:, LANES:]
        spare = jnp.full((8, 8), e, jnp.float32)
        tail = jnp.concatenate([rest[0:8], rest[8:16], rest[16:24], spare], axis=1)
        packed[e] = jnp.concatenate([result[:, :LANES], tail], axis=0).astype(jnp.bfloat16)
    for k, send in enumerate(sends):
        for p in range(capacity):
            send[p] = packed[order_ref[k * capacity + p]]


def unpack_kernel(elements, away, *refs):
    received, (rows_ref, ids_ref) = refs[:-2], refs[-2:]
    capacity = received[0].shape[0]
    rest = rows_ref.shape[2] - LANES
    count = rows_ref.shape[0]
    wide = pl.cdiv(count, LANES) * LANES
    me = lax.axis_index("grp")
    lane = lax.broadcasted_iota(jnp.int32, (8, wide), 1)
    local = jnp.full((8, wide), -1.0, jnp.float32)
    for k, ref in zip(away, received):
        first = lax.bitwise_xor(me, k) * capacity
        for p in range(capacity):
            block = ref[p].astype(jnp.float32)
            tail = block[24:32]
            rows_ref[first + p] = jnp.concatenate(
                [
                    block[0:24],
                    jnp.concatenate([tail[:, rest * q : rest * (q + 1)] for q in range(3)], axis=0),
                ],
                axis=1,
            ).astype(jnp.bfloat16)
            local = jnp.where(lane == first + p, tail[:, 127:128], local)
    local = local[0:1, :count].astype(jnp.int32)
    group = lax.broadcasted_iota(jnp.int32, (1, count), 1) // capacity
    first = (group * lax.axis_size("row") + lax.axis_index("row")) * elements
    ids_ref[...] = jnp.where(local >= 0, first + local, -1)


def on_device(stiffness, lame, prolong, columns, ghost_count, ghost_offset, owner_map):
    elements, coarse, fine = prolong.shape
    slots = stiffness.shape[0]
    ghosts = elements // 2
    owners = lax.axis_size("grp")
    capacity = 2 * ((elements + owners - 1) // owners)
    run = pltpu.VMEM((ghosts // 2, 3 * coarse, LANES), jnp.bfloat16)
    by_odd, by_even, own, lame_slots, by_slot, owner = pl.pallas_call(
        pack_kernel,
        out_shape=(
            run, run,
            pltpu.VMEM(prolong.shape, jnp.bfloat16),
            pltpu.SMEM((slots, 2, elements), jnp.float32),
            pltpu.SMEM((slots, elements), jnp.int32),
            pltpu.SMEM((1, elements), jnp.int32),
        ),
        in_specs=[HBM] * 6, out_specs=(VMEM,) * 3 + (SMEM,) * 3,
        scratch_shapes=[
            pltpu.SMEM(ghost_count.shape, jnp.int32),
            pltpu.SMEM(ghost_offset.shape, jnp.int32),
            pltpu.SemaphoreType.DMA((6,)),
        ],
        compiler_params=params(), name="pack",
    )(
        in_hbm(ghost_count), in_hbm(ghost_offset), in_hbm(prolong),
        in_hbm(lame.transpose(1, 2, 0)), in_hbm(columns.T), in_hbm(owner_map.T),
    )
    from_even = swapped(by_even, "row", 0)
    from_odd = swapped(by_odd, "row", 1)
    own = in_vmem(own.reshape(elements * coarse, fine))
    left, order = pl.pallas_call(
        functools.partial(left_kernel, capacity),
        out_shape=(
            pltpu.VMEM((elements, slots, 2 * coarse, fine), jnp.bfloat16),
            pltpu.SMEM((owners * capacity,), jnp.int32),
        ),
        in_specs=[SMEM, SMEM, HBM, VMEM], out_specs=(VMEM, SMEM),
        scratch_shapes=[
            pltpu.VMEM(stiffness.shape, jnp.bfloat16),
            pltpu.SMEM((owners,), jnp.int32),
            pltpu.SemaphoreType.DMA((1,)),
        ],
        compiler_params=params(), name="left",
    )(in_smem(lame_slots), in_smem(owner), in_hbm(stiffness), own)
    sends = pl.pallas_call(
        rows_kernel,
        out_shape=[pltpu.VMEM((capacity, 32, LANES), jnp.bfloat16)] * owners,
        in_specs=[SMEM, SMEM, VMEM, VMEM, VMEM, VMEM], out_specs=[VMEM] * owners,
        scratch_shapes=[
            pltpu.VMEM((elements + 2 * ghosts + 1, coarse, fine), jnp.float32),
            pltpu.VMEM((elements + 1, 32, LANES), jnp.bfloat16),
        ],
        compiler_params=params(), name="rows",
    )(
        in_smem(by_slot), in_smem(order), own,
        in_vmem(from_even), in_vmem(from_odd), in_vmem(left),
    )
    arrival = [*range(2, owners), 1]
    received = {0: sends[0]}
    for k in arrival:
        received[k] = lax.ppermute(sends[k], "grp", [(i, i ^ k) for i in range(owners)])
    coarse_rows, ids = pl.pallas_call(
        functools.partial(unpack_kernel, elements, (*arrival, 0)),
        out_shape=(
            jax.ShapeDtypeStruct((owners * capacity, coarse, slots * coarse), jnp.bfloat16),
            jax.ShapeDtypeStruct((1, owners * capacity), jnp.int32),
        ),
        in_specs=[VMEM] * owners, out_specs=(VMEM, VMEM),
        compiler_params=params(), name="unpack",
    )(*[in_vmem(received[k]) for k in (*arrival, 0)])
    return (coarse_rows, ids.reshape(-1))


def solution(mesh):
    split = ("grp", "row")
    return jax.shard_map(
        on_device, mesh=mesh,
        in_specs=(P(), P(split, None, None), P(split, None, None)) + (P(split, None),) * 4,
        out_specs=(P(split, None, None), P(split)), check_vma=False,
    )
```

```python
import functools

import jax
import jax.numpy as jnp
from jax import lax
from jax.experimental import pallas as pl
from jax.experimental.pallas import tpu as pltpu
from jax.sharding import PartitionSpec as P

LANES = 128
VMEM = pl.BlockSpec(memory_space=pltpu.VMEM)
HBM = pl.BlockSpec(memory_space=pltpu.HBM)
SMEM = pl.BlockSpec(memory_space=pltpu.SMEM)


def in_vmem(value):
    return pltpu.with_memory_space_constraint(value, pltpu.VMEM)


def in_smem(value):
    return pltpu.with_memory_space_constraint(value, pltpu.SMEM)


def in_hbm(value):
    return pltpu.with_memory_space_constraint(value, pltpu.HBM)


def params():
    return pltpu.CompilerParams(vmem_limit_bytes=24 * 1024 * 1024)


def swapped(value, parity):
    rows = lax.axis_size("row")
    pairs = []
    for group in range(lax.axis_size("grp")):
        for row in range(rows):
            other = row + 1 if row % 2 == parity else row - 1
            there = (group, other) if 0 <= other < rows else (group ^ 1, row)
            pairs.append((group * rows + row, there[0] * rows + there[1]))
    return lax.ppermute(value, ("grp", "row"), pairs)


def fetch(pairs, sems):
    copies = [pltpu.make_async_copy(src, dst, sems.at[i]) for i, (src, dst) in enumerate(pairs)]
    for copy in copies:
        copy.start()
    return copies


def pack_kernel(
    count_hbm, offset_hbm, prolong_hbm, lame_hbm, columns_hbm, owner_hbm,
    odd_ref, even_ref, prolong_ref, lame_ref, columns_ref, owner_ref,
    count_ref, offset_ref, sems,
):
    copies = fetch(
        [
            (prolong_hbm, prolong_ref), (count_hbm, count_ref), (offset_hbm, offset_ref),
            (lame_hbm, lame_ref), (columns_hbm, columns_ref), (owner_hbm, owner_ref),
        ],
        sems,
    )
    for copy in copies:
        copy.wait()
    elements = prolong_ref.shape[0]
    odd_row = lax.rem(lax.axis_index("row"), 2)
    for way, out_ref in ((odd_row, odd_ref), (1 - odd_row, even_ref)):
        first = offset_ref[0, way]
        length = count_ref[0, way]

        def block(slot):
            value = prolong_ref[jnp.minimum(first + slot, elements - 1)].astype(jnp.float32)
            return jnp.where(slot < length, value, 0.0)

        for pair in range(out_ref.shape[0]):
            even, odd = block(2 * pair), block(2 * pair + 1)
            tail = jnp.concatenate([even[:, LANES:], odd[:, LANES:]], axis=1)
            out_ref[pair] = jnp.concatenate(
                [even[:, :LANES], odd[:, :LANES], tail], axis=0
            ).astype(jnp.bfloat16)


def left_kernel(
    capacity, lame_ref, owner_ref, stiffness_hbm, prolong_ref, left_ref, order_ref, stiffness_ref, filled, sems,
):
    elements, slots, rows, _ = left_ref.shape
    coarse = rows // 2
    copies = fetch([(stiffness_hbm, stiffness_ref)], sems)
    me = lax.axis_index("grp")
    for t in range(filled.shape[0]):
        filled[t] = 0
    for i in range(order_ref.shape[0]):
        order_ref[i] = elements
    for e in range(elements):
        away = lax.bitwise_xor(owner_ref[0, e], me)
        position = filled[away]
        filled[away] = position + 1
        order_ref[away * capacity + position] = e

    copies[0].wait()
    own = prolong_ref[...]
    for s in range(slots):
        first = jnp.dot(own, stiffness_ref[s, 0], preferred_element_type=jnp.float32)
        second = jnp.dot(own, stiffness_ref[s, 1], preferred_element_type=jnp.float32)
        for e in range(elements):
            part = slice(e * coarse, (e + 1) * coarse)
            total = lame_ref[s, 0, e] * first[part] + lame_ref[s, 1, e] * second[part]
            high = total.astype(jnp.bfloat16).astype(jnp.float32)
            left_ref[e, s] = jnp.concatenate([high, total - high], axis=0).astype(jnp.bfloat16)


def rows_kernel(columns_ref, order_ref, prolong_ref, even_ref, odd_ref, left_ref, *refs):
    sends, (table, packed) = refs[:-2], refs[-2:]
    elements, slots, rows, fine = left_ref.shape
    coarse = rows // 2
    ghosts = 2 * odd_ref.shape[0]
    row, last = lax.axis_index("row"), lax.axis_size("row") - 1
    half = fine - LANES
    capacity = sends[0].shape[0]
    for e in range(elements):
        table[e] = prolong_ref[e * coarse : (e + 1) * coarse].astype(jnp.float32)
    for parity, ref in enumerate((even_ref, odd_ref)):
        from_above = lax.rem(row, 2) == parity
        start = jnp.where(from_above, elements + ghosts, elements)
        has_partner = jnp.where(from_above, row < last, row > 0)
        for pair in range(ghosts // 2):
            block = jnp.where(has_partner, ref[pair].astype(jnp.float32), 0.0)
            tail = block[2 * coarse :]
            for odd in range(2):
                table[start + 2 * pair + odd] = jnp.concatenate(
                    [block[odd * coarse : (odd + 1) * coarse], tail[:, odd * half : (odd + 1) * half]], axis=1
                )
    table[elements + 2 * ghosts] = jnp.zeros((coarse, fine), jnp.float32)

    lane8 = lax.broadcasted_iota(jnp.int32, (8, LANES), 1)
    packed[elements] = jnp.concatenate(
        [jnp.zeros((coarse, LANES), jnp.float32), jnp.where(lane8 >= 120, -1.0, 0.0)], axis=0
    ).astype(jnp.bfloat16)

    width = slots * coarse
    lane = lax.broadcasted_iota(jnp.int32, (coarse, width), 1)
    for e in range(elements):
        blocks = []
        for s in range(slots):
            c = columns_ref[s, e]
            blocks.append(table[jnp.where(c < 0, elements + 2 * ghosts, c)])
        right = jnp.concatenate(blocks, axis=0).astype(jnp.bfloat16)
        left = left_ref[e].reshape(slots * 2 * coarse, fine)
        product = lax.dot_general(
            left, right, (((1,), (1,)), ((), ())), preferred_element_type=jnp.float32
        )
        result = None
        for s in range(slots):
            at = 2 * coarse * s
            part = product[at : at + coarse] + product[at + coarse : at + 2 * coarse]
            result = part if s == 0 else jnp.where(lane >= s * coarse, part, result)
        rest = result[:, LANES:]
        spare = jnp.full((8, 8), e, jnp.float32)
        tail = jnp.concatenate([rest[0:8], rest[8:16], rest[16:24], spare], axis=1)
        packed[e] = jnp.concatenate([result[:, :LANES], tail], axis=0).astype(jnp.bfloat16)
    for k, send in enumerate(sends):
        for p in range(capacity):
            send[p] = packed[order_ref[k * capacity + p]]


def unpack_kernel(elements, away, *refs):
    received, (rows_ref, ids_ref) = refs[:-2], refs[-2:]
    capacity = received[0].shape[0]
    rest = rows_ref.shape[2] - LANES
    count = rows_ref.shape[0]
    wide = pl.cdiv(count, LANES) * LANES
    me = lax.axis_index("grp")
    lane = lax.broadcasted_iota(jnp.int32, (8, wide), 1)
    local = jnp.full((8, wide), -1.0, jnp.float32)
    for k, ref in zip(away, received):
        first = lax.bitwise_xor(me, k) * capacity
        for p in range(capacity):
            block = ref[p].astype(jnp.float32)
            tail = block[24:32]
            rows_ref[first + p] = jnp.concatenate(
                [
                    block[0:24],
                    jnp.concatenate([tail[:, rest * q : rest * (q + 1)] for q in range(3)], axis=0),
                ],
                axis=1,
            ).astype(jnp.bfloat16)
            local = jnp.where(lane == first + p, tail[:, 127:128], local)
    local = local[0:1, :count].astype(jnp.int32)
    group = lax.broadcasted_iota(jnp.int32, (1, count), 1) // capacity
    first = (group * lax.axis_size("row") + lax.axis_index("row")) * elements
    ids_ref[...] = jnp.where(local >= 0, first + local, -1)


def on_device(stiffness, lame, prolong, columns, ghost_count, ghost_offset, owner_map):
    elements, coarse, fine = prolong.shape
    slots = stiffness.shape[0]
    ghosts = elements // 2
    owners = lax.axis_size("grp")
    capacity = 2 * ((elements + owners - 1) // owners)
    run = pltpu.VMEM((ghosts // 2, 3 * coarse, LANES), jnp.bfloat16)
    by_odd, by_even, own, lame_slots, by_slot, owner = pl.pallas_call(
        pack_kernel,
        out_shape=(
            run, run,
            pltpu.VMEM(prolong.shape, jnp.bfloat16),
            pltpu.SMEM((slots, 2, elements), jnp.float32),
            pltpu.SMEM((slots, elements), jnp.int32),
            pltpu.SMEM((1, elements), jnp.int32),
        ),
        in_specs=[HBM] * 6, out_specs=(VMEM,) * 3 + (SMEM,) * 3,
        scratch_shapes=[
            pltpu.SMEM(ghost_count.shape, jnp.int32),
            pltpu.SMEM(ghost_offset.shape, jnp.int32),
            pltpu.SemaphoreType.DMA((6,)),
        ],
        compiler_params=params(), name="pack",
    )(
        in_hbm(ghost_count), in_hbm(ghost_offset), in_hbm(prolong),
        in_hbm(lame.transpose(1, 2, 0)), in_hbm(columns.T), in_hbm(owner_map.T),
    )
    from_even = swapped(by_even, 0)
    from_odd = swapped(by_odd, 1)
    own = in_vmem(own.reshape(elements * coarse, fine))
    left, order = pl.pallas_call(
        functools.partial(left_kernel, capacity),
        out_shape=(
            pltpu.VMEM((elements, slots, 2 * coarse, fine), jnp.bfloat16),
            pltpu.SMEM((owners * capacity,), jnp.int32),
        ),
        in_specs=[SMEM, SMEM, HBM, VMEM], out_specs=(VMEM, SMEM),
        scratch_shapes=[
            pltpu.VMEM(stiffness.shape, jnp.bfloat16),
            pltpu.SMEM((owners,), jnp.int32),
            pltpu.SemaphoreType.DMA((1,)),
        ],
        compiler_params=params(), name="left",
    )(in_smem(lame_slots), in_smem(owner), in_hbm(stiffness), own)
    sends = pl.pallas_call(
        rows_kernel,
        out_shape=[pltpu.VMEM((capacity, 32, LANES), jnp.bfloat16)] * owners,
        in_specs=[SMEM, SMEM, VMEM, VMEM, VMEM, VMEM], out_specs=[VMEM] * owners,
        scratch_shapes=[
            pltpu.VMEM((elements + 2 * ghosts + 1, coarse, fine), jnp.float32),
            pltpu.VMEM((elements + 1, 32, LANES), jnp.bfloat16),
        ],
        compiler_params=params(), name="rows",
    )(
        in_smem(by_slot), in_smem(order), own,
        in_vmem(from_even), in_vmem(from_odd), in_vmem(left),
    )
    arrival = [*range(2, owners), 1]
    received = {0: sends[0]}
    for k in arrival:
        received[k] = lax.ppermute(sends[k], "grp", [(i, i ^ k) for i in range(owners)])
    coarse_rows, ids = pl.pallas_call(
        functools.partial(unpack_kernel, elements, (*arrival, 0)),
        out_shape=(
            jax.ShapeDtypeStruct((owners * capacity, coarse, slots * coarse), jnp.bfloat16),
            jax.ShapeDtypeStruct((1, owners * capacity), jnp.int32),
        ),
        in_specs=[VMEM] * owners, out_specs=(VMEM, VMEM),
        compiler_params=params(), name="unpack",
    )(*[in_vmem(received[k]) for k in (*arrival, 0)])
    return (coarse_rows, ids.reshape(-1))


def solution(mesh):
    split = ("grp", "row")
    return jax.shard_map(
        on_device, mesh=mesh,
        in_specs=(P(), P(split, None, None), P(split, None, None)) + (P(split, None),) * 4,
        out_specs=(P(split, None, None), P(split)), check_vma=False,
    )
```

```python
import functools

import jax
import jax.numpy as jnp
from jax import lax
from jax.experimental import pallas as pl
from jax.experimental.pallas import tpu as pltpu
from jax.sharding import PartitionSpec as P

LANES = 128
VMEM = pl.BlockSpec(memory_space=pltpu.VMEM)
HBM = pl.BlockSpec(memory_space=pltpu.HBM)
SMEM = pl.BlockSpec(memory_space=pltpu.SMEM)


def in_vmem(value):
    return pltpu.with_memory_space_constraint(value, pltpu.VMEM)


def in_smem(value):
    return pltpu.with_memory_space_constraint(value, pltpu.SMEM)


def in_hbm(value):
    return pltpu.with_memory_space_constraint(value, pltpu.HBM)


def params():
    return pltpu.CompilerParams(vmem_limit_bytes=24 * 1024 * 1024)


def swapped(value, parity):
    rows = lax.axis_size("row")
    pairs = []
    for group in range(lax.axis_size("grp")):
        for row in range(rows):
            other = row + 1 if row % 2 == parity else row - 1
            there = (group, other) if 0 <= other < rows else (group ^ 1, row)
            pairs.append((group * rows + row, there[0] * rows + there[1]))
    return lax.ppermute(value, ("grp", "row"), pairs)


def fetch(pairs, sems):
    copies = [pltpu.make_async_copy(src, dst, sems.at[i]) for i, (src, dst) in enumerate(pairs)]
    for copy in copies:
        copy.start()
    return copies


def pack_kernel(
    count_hbm, offset_hbm, prolong_hbm, lame_hbm, columns_hbm, owner_hbm,
    odd_ref, even_ref, prolong_ref, lame_ref, columns_ref, owner_ref,
    count_ref, offset_ref, sems,
):
    copies = fetch(
        [
            (prolong_hbm, prolong_ref), (count_hbm, count_ref), (offset_hbm, offset_ref),
            (lame_hbm, lame_ref), (columns_hbm, columns_ref), (owner_hbm, owner_ref),
        ],
        sems,
    )
    for copy in copies:
        copy.wait()
    elements = prolong_ref.shape[0]
    odd_row = lax.rem(lax.axis_index("row"), 2)
    for way, out_ref in ((odd_row, odd_ref), (1 - odd_row, even_ref)):
        first = offset_ref[0, way]
        length = count_ref[0, way]

        def block(slot):
            value = prolong_ref[jnp.minimum(first + slot, elements - 1)].astype(jnp.float32)
            return jnp.where(slot < length, value, 0.0)

        for pair in range(out_ref.shape[0]):
            even, odd = block(2 * pair), block(2 * pair + 1)
            tail = jnp.concatenate([even[:, LANES:], odd[:, LANES:]], axis=1)
            out_ref[pair] = jnp.concatenate(
                [even[:, :LANES], odd[:, :LANES], tail], axis=0
            ).astype(jnp.bfloat16)


def left_kernel(
    capacity, lame_ref, owner_ref, stiffness_hbm, prolong_ref, left_ref, order_ref, stiffness_ref, filled, sems,
):
    elements, slots, rows, _ = left_ref.shape
    coarse = rows // 2
    copies = fetch([(stiffness_hbm, stiffness_ref)], sems)
    me = lax.axis_index("grp")
    for t in range(filled.shape[0]):
        filled[t] = 0
    for i in range(order_ref.shape[0]):
        order_ref[i] = elements
    for e in range(elements):
        away = lax.bitwise_xor(owner_ref[0, e], me)
        position = filled[away]
        filled[away] = position + 1
        order_ref[away * capacity + position] = e

    copies[0].wait()
    own = prolong_ref[...]
    for s in range(slots):
        first = jnp.dot(own, stiffness_ref[s, 0], preferred_element_type=jnp.float32)
        second = jnp.dot(own, stiffness_ref[s, 1], preferred_element_type=jnp.float32)
        for e in range(elements):
            part = slice(e * coarse, (e + 1) * coarse)
            total = lame_ref[s, 0, e] * first[part] + lame_ref[s, 1, e] * second[part]
            high = total.astype(jnp.bfloat16).astype(jnp.float32)
            left_ref[e, s] = jnp.concatenate([high, total - high], axis=0).astype(jnp.bfloat16)


def rows_kernel(columns_ref, order_ref, prolong_ref, even_ref, odd_ref, left_ref, *refs):
    sends, (table, packed) = refs[:-2], refs[-2:]
    elements, slots, rows, fine = left_ref.shape
    coarse = rows // 2
    ghosts = 2 * odd_ref.shape[0]
    row, last = lax.axis_index("row"), lax.axis_size("row") - 1
    half = fine - LANES
    capacity = sends[0].shape[0]
    for e in range(elements):
        table[e] = prolong_ref[e * coarse : (e + 1) * coarse].astype(jnp.float32)
    for parity, ref in enumerate((even_ref, odd_ref)):
        from_above = lax.rem(row, 2) == parity
        start = jnp.where(from_above, elements + ghosts, elements)
        has_partner = jnp.where(from_above, row < last, row > 0)
        for pair in range(ghosts // 2):
            block = jnp.where(has_partner, ref[pair].astype(jnp.float32), 0.0)
            tail = block[2 * coarse :]
            for odd in range(2):
                table[start + 2 * pair + odd] = jnp.concatenate(
                    [block[odd * coarse : (odd + 1) * coarse], tail[:, odd * half : (odd + 1) * half]], axis=1
                )
    table[elements + 2 * ghosts] = jnp.zeros((coarse, fine), jnp.float32)

    lane8 = lax.broadcasted_iota(jnp.int32, (8, LANES), 1)
    packed[elements] = jnp.concatenate(
        [jnp.zeros((coarse, LANES), jnp.float32), jnp.where(lane8 >= 120, -1.0, 0.0)], axis=0
    ).astype(jnp.bfloat16)

    width = slots * coarse
    lane = lax.broadcasted_iota(jnp.int32, (coarse, width), 1)
    for e in range(elements):
        blocks = []
        for s in range(slots):
            c = columns_ref[s, e]
            blocks.append(table[jnp.where(c < 0, elements + 2 * ghosts, c)])
        right = jnp.concatenate(blocks, axis=0).astype(jnp.bfloat16)
        left = left_ref[e].reshape(slots * 2 * coarse, fine)
        product = lax.dot_general(
            left, right, (((1,), (1,)), ((), ())), preferred_element_type=jnp.float32
        )
        result = None
        for s in range(slots):
            at = 2 * coarse * s
            part = product[at : at + coarse] + product[at + coarse : at + 2 * coarse]
            result = part if s == 0 else jnp.where(lane >= s * coarse, part, result)
        rest = result[:, LANES:]
        spare = jnp.full((8, 8), e, jnp.float32)
        tail = jnp.concatenate([rest[0:8], rest[8:16], rest[16:24], spare], axis=1)
        packed[e] = jnp.concatenate([result[:, :LANES], tail], axis=0).astype(jnp.bfloat16)
    for k, send in enumerate(sends):
        for p in range(capacity):
            send[p] = packed[order_ref[k * capacity + p]]


def unpack_kernel(elements, away, last, *refs):
    received, refs = refs[: len(away)], refs[len(away) :]
    if last:
        _, before_ref, rows_hbm, ids_hbm, rows_ref, ids_ref, sems = refs
        local = before_ref[...]
    else:
        rows_hbm, after_ref, rows_ref, sems = refs
        local = jnp.full(after_ref.shape, -1.0, jnp.float32)
    capacity = received[0].shape[0]
    rest = rows_ref.shape[2] - LANES
    me = lax.axis_index("grp")
    lane = lax.broadcasted_iota(jnp.int32, local.shape, 1)
    for k, ref in zip(away, received):
        first = lax.bitwise_xor(me, k) * capacity
        for p in range(capacity):
            local = jnp.where(lane == first + p, ref[p].astype(jnp.float32)[24:32, 127:128], local)
    copies = []
    if last:
        count = ids_ref.shape[1]
        owned = local[0:1, :count].astype(jnp.int32)
        group = lax.broadcasted_iota(jnp.int32, (1, count), 1) // capacity
        start = (group * lax.axis_size("row") + lax.axis_index("row")) * elements
        ids_ref[...] = jnp.where(owned >= 0, start + owned, -1)
        copies.append(pltpu.make_async_copy(ids_ref, ids_hbm, sems.at[len(away)]))
        copies[-1].start()
    else:
        after_ref[...] = local
    for i, (k, ref) in enumerate(zip(away, received)):
        for p in range(capacity):
            block = ref[p].astype(jnp.float32)
            tail = block[24:32]
            rows_ref[i * capacity + p] = jnp.concatenate(
                [
                    block[0:24],
                    jnp.concatenate([tail[:, rest * q : rest * (q + 1)] for q in range(3)], axis=0),
                ],
                axis=1,
            ).astype(jnp.bfloat16)
        first = lax.bitwise_xor(me, k) * capacity
        copies.append(
            pltpu.make_async_copy(
                rows_ref.at[pl.ds(i * capacity, capacity)], rows_hbm.at[pl.ds(first, capacity)], sems.at[i]
            )
        )
        copies[-1].start()
    for copy in copies:
        copy.wait()


def on_device(stiffness, lame, prolong, columns, ghost_count, ghost_offset, owner_map):
    elements, coarse, fine = prolong.shape
    slots = stiffness.shape[0]
    ghosts = elements // 2
    owners = lax.axis_size("grp")
    capacity = 2 * ((elements + owners - 1) // owners)
    run = pltpu.VMEM((ghosts // 2, 3 * coarse, LANES), jnp.bfloat16)
    by_odd, by_even, own, lame_slots, by_slot, owner = pl.pallas_call(
        pack_kernel,
        out_shape=(
            run, run,
            pltpu.VMEM(prolong.shape, jnp.bfloat16),
            pltpu.SMEM((slots, 2, elements), jnp.float32),
            pltpu.SMEM((slots, elements), jnp.int32),
            pltpu.SMEM((1, elements), jnp.int32),
        ),
        in_specs=[HBM] * 6, out_specs=(VMEM,) * 3 + (SMEM,) * 3,
        scratch_shapes=[
            pltpu.SMEM(ghost_count.shape, jnp.int32),
            pltpu.SMEM(ghost_offset.shape, jnp.int32),
            pltpu.SemaphoreType.DMA((6,)),
        ],
        compiler_params=params(), name="pack",
    )(
        in_hbm(ghost_count), in_hbm(ghost_offset), in_hbm(prolong),
        in_hbm(lame.transpose(1, 2, 0)), in_hbm(columns.T), in_hbm(owner_map.T),
    )
    from_even = swapped(by_even, 0)
    from_odd = swapped(by_odd, 1)
    own = in_vmem(own.reshape(elements * coarse, fine))
    left, order = pl.pallas_call(
        functools.partial(left_kernel, capacity),
        out_shape=(
            pltpu.VMEM((elements, slots, 2 * coarse, fine), jnp.bfloat16),
            pltpu.SMEM((owners * capacity,), jnp.int32),
        ),
        in_specs=[SMEM, SMEM, HBM, VMEM], out_specs=(VMEM, SMEM),
        scratch_shapes=[
            pltpu.VMEM(stiffness.shape, jnp.bfloat16),
            pltpu.SMEM((owners,), jnp.int32),
            pltpu.SemaphoreType.DMA((1,)),
        ],
        compiler_params=params(), name="left",
    )(in_smem(lame_slots), in_smem(owner), in_hbm(stiffness), own)
    sends = pl.pallas_call(
        rows_kernel,
        out_shape=[pltpu.VMEM((capacity, 32, LANES), jnp.bfloat16)] * owners,
        in_specs=[SMEM, SMEM, VMEM, VMEM, VMEM, VMEM], out_specs=[VMEM] * owners,
        scratch_shapes=[
            pltpu.VMEM((elements + 2 * ghosts + 1, coarse, fine), jnp.float32),
            pltpu.VMEM((elements + 1, 32, LANES), jnp.bfloat16),
        ],
        compiler_params=params(), name="rows",
    )(
        in_smem(by_slot), in_smem(order), own,
        in_vmem(from_even), in_vmem(from_odd), in_vmem(left),
    )
    received = {0: sends[0]}
    for k in [*range(2, owners), 1]:
        received[k] = lax.ppermute(sends[k], "grp", [(i, i ^ k) for i in range(owners)])
    received = {k: in_vmem(value) for k, value in received.items()}
    rows = jax.ShapeDtypeStruct((owners * capacity, coarse, slots * coarse), jnp.bfloat16)
    wide = pl.cdiv(owners * capacity, LANES) * LANES

    def scratch(blocks):
        return pltpu.VMEM((blocks * capacity, coarse, slots * coarse), jnp.bfloat16)

    early, late = [*range(2, owners - 1), 0], [owners - 1, 1]
    partial, local = pl.pallas_call(
        functools.partial(unpack_kernel, elements, early, False),
        out_shape=(pltpu.HBM(rows.shape, rows.dtype), pltpu.VMEM((8, wide), jnp.float32)),
        in_specs=[VMEM] * len(early), out_specs=(HBM, VMEM),
        scratch_shapes=[scratch(len(early)), pltpu.SemaphoreType.DMA((len(early),))],
        compiler_params=params(), name="unpack_early",
    )(*[received[k] for k in early])
    coarse_rows, ids = pl.pallas_call(
        functools.partial(unpack_kernel, elements, late, True),
        out_shape=(rows, jax.ShapeDtypeStruct((1, owners * capacity), jnp.int32)),
        in_specs=[VMEM] * len(late) + [HBM, VMEM], out_specs=(HBM, HBM),
        scratch_shapes=[
            scratch(len(late)),
            pltpu.VMEM((1, owners * capacity), jnp.int32),
            pltpu.SemaphoreType.DMA((len(late) + 1,)),
        ],
        input_output_aliases={len(late): 0},
        compiler_params=params(), name="unpack_late",
    )(*[received[k] for k in late], in_hbm(partial), in_vmem(local))
    return (coarse_rows, ids.reshape(-1))


def solution(mesh):
    split = ("grp", "row")
    return jax.shard_map(
        on_device, mesh=mesh,
        in_specs=(P(), P(split, None, None), P(split, None, None)) + (P(split, None),) * 4,
        out_specs=(P(split, None, None), P(split)), check_vma=False,
    )
```

```python
import functools

import jax
import jax.numpy as jnp
from jax import lax
from jax.experimental import pallas as pl
from jax.experimental.pallas import tpu as pltpu
from jax.sharding import PartitionSpec as P

LANES = 128
VMEM = pl.BlockSpec(memory_space=pltpu.VMEM)
HBM = pl.BlockSpec(memory_space=pltpu.HBM)
SMEM = pl.BlockSpec(memory_space=pltpu.SMEM)


def in_vmem(value):
    return pltpu.with_memory_space_constraint(value, pltpu.VMEM)


def in_smem(value):
    return pltpu.with_memory_space_constraint(value, pltpu.SMEM)


def in_hbm(value):
    return pltpu.with_memory_space_constraint(value, pltpu.HBM)


def params():
    return pltpu.CompilerParams(vmem_limit_bytes=24 * 1024 * 1024)


def swapped(value, parity):
    rows = lax.axis_size("row")
    pairs = []
    for group in range(lax.axis_size("grp")):
        for row in range(rows):
            other = row + 1 if row % 2 == parity else row - 1
            there = (group, other) if 0 <= other < rows else (group ^ 1, row)
            pairs.append((group * rows + row, there[0] * rows + there[1]))
    return lax.ppermute(value, ("grp", "row"), pairs)


def fetch(pairs, sems):
    copies = [pltpu.make_async_copy(src, dst, sems.at[i]) for i, (src, dst) in enumerate(pairs)]
    for copy in copies:
        copy.start()
    return copies


def pack_kernel(
    count_hbm, offset_hbm, prolong_hbm, odd_ref, even_ref, prolong_ref, count_ref, offset_ref, sems,
):
    for copy in fetch([(prolong_hbm, prolong_ref), (count_hbm, count_ref), (offset_hbm, offset_ref)], sems):
        copy.wait()
    elements = prolong_ref.shape[0]
    odd_row = lax.rem(lax.axis_index("row"), 2)
    for way, out_ref in ((odd_row, odd_ref), (1 - odd_row, even_ref)):
        first = offset_ref[0, way]
        length = count_ref[0, way]

        def block(slot):
            value = prolong_ref[jnp.minimum(first + slot, elements - 1)].astype(jnp.float32)
            return jnp.where(slot < length, value, 0.0)

        for pair in range(out_ref.shape[0]):
            even, odd = block(2 * pair), block(2 * pair + 1)
            tail = jnp.concatenate([even[:, LANES:], odd[:, LANES:]], axis=1)
            out_ref[pair] = jnp.concatenate(
                [even[:, :LANES], odd[:, :LANES], tail], axis=0
            ).astype(jnp.bfloat16)


def left_kernel(
    capacity, lame_hbm, owner_hbm, columns_hbm, stiffness_hbm, prolong_ref, left_ref, order_ref, columns_ref,
    lame_ref, owner_ref, stiffness_ref, filled, sems,
):
    elements, slots, rows, _ = left_ref.shape
    coarse = rows // 2
    copies = fetch(
        [(owner_hbm, owner_ref), (lame_hbm, lame_ref), (columns_hbm, columns_ref), (stiffness_hbm, stiffness_ref)],
        sems,
    )
    copies[0].wait()
    me = lax.axis_index("grp")
    for t in range(filled.shape[0]):
        filled[t] = 0
    for i in range(order_ref.shape[0]):
        order_ref[i] = elements
    for e in range(elements):
        away = lax.bitwise_xor(owner_ref[0, e], me)
        position = filled[away]
        filled[away] = position + 1
        order_ref[away * capacity + position] = e

    for copy in copies[1:]:
        copy.wait()
    own = prolong_ref[...]
    spare = jnp.zeros((rows, left_ref.shape[3] - own.shape[1]), jnp.float32)
    for s in range(slots):
        first = jnp.dot(own, stiffness_ref[s, 0], preferred_element_type=jnp.float32)
        second = jnp.dot(own, stiffness_ref[s, 1], preferred_element_type=jnp.float32)
        for e in range(elements):
            part = slice(e * coarse, (e + 1) * coarse)
            total = lame_ref[s, 0, e] * first[part] + lame_ref[s, 1, e] * second[part]
            high = total.astype(jnp.bfloat16).astype(jnp.float32)
            both = jnp.concatenate([high, total - high], axis=0)
            left_ref[e, s] = jnp.concatenate([both, spare], axis=1).astype(jnp.bfloat16)


def rows_kernel(columns_ref, order_ref, prolong_ref, even_ref, odd_ref, left_ref, *refs):
    sends, (table, packed) = refs[:-2], refs[-2:]
    elements, slots, rows, depth = left_ref.shape
    coarse, fine = rows // 2, prolong_ref.shape[1]
    spare = jnp.zeros((coarse, depth - fine), jnp.float32)
    ghosts = 2 * odd_ref.shape[0]
    row, last = lax.axis_index("row"), lax.axis_size("row") - 1
    half = fine - LANES
    capacity = sends[0].shape[0]
    for e in range(elements):
        own = prolong_ref[e * coarse : (e + 1) * coarse].astype(jnp.float32)
        table[e] = jnp.concatenate([own, spare], axis=1)
    for parity, ref in enumerate((even_ref, odd_ref)):
        from_above = lax.rem(row, 2) == parity
        start = jnp.where(from_above, elements + ghosts, elements)
        has_partner = jnp.where(from_above, row < last, row > 0)
        for pair in range(ghosts // 2):
            block = jnp.where(has_partner, ref[pair].astype(jnp.float32), 0.0)
            tail = block[2 * coarse :]
            for odd in range(2):
                table[start + 2 * pair + odd] = jnp.concatenate(
                    [block[odd * coarse : (odd + 1) * coarse], tail[:, odd * half : (odd + 1) * half], spare], axis=1
                )
    table[elements + 2 * ghosts] = jnp.zeros((coarse, depth), jnp.float32)

    lane8 = lax.broadcasted_iota(jnp.int32, (8, LANES), 1)
    packed[elements] = jnp.concatenate(
        [jnp.zeros((coarse, LANES), jnp.float32), jnp.where(lane8 >= 120, -1.0, 0.0)], axis=0
    ).astype(jnp.bfloat16)

    width = slots * coarse
    lane = lax.broadcasted_iota(jnp.int32, (coarse, width), 1)
    for e in range(elements):
        blocks = []
        for s in range(slots):
            c = columns_ref[s, e]
            blocks.append(table[jnp.where(c < 0, elements + 2 * ghosts, c)])
        right = jnp.concatenate(blocks, axis=0).astype(jnp.bfloat16)
        left = left_ref[e].reshape(slots * 2 * coarse, depth)
        product = lax.dot_general(
            left, right, (((1,), (1,)), ((), ())), preferred_element_type=jnp.float32
        )
        result = None
        for s in range(slots):
            at = 2 * coarse * s
            part = product[at : at + coarse] + product[at + coarse : at + 2 * coarse]
            result = part if s == 0 else jnp.where(lane >= s * coarse, part, result)
        rest = result[:, LANES:]
        spare = jnp.full((8, 8), e, jnp.float32)
        tail = jnp.concatenate([rest[0:8], rest[8:16], rest[16:24], spare], axis=1)
        packed[e] = jnp.concatenate([result[:, :LANES], tail], axis=0).astype(jnp.bfloat16)
    for k, send in enumerate(sends):
        for p in range(capacity):
            send[p] = packed[order_ref[k * capacity + p]]


def unpack_kernel(elements, away, last, *refs):
    received, refs = refs[: len(away)], refs[len(away) :]
    if last:
        _, before_ref, rows_hbm, ids_hbm, rows_ref, ids_ref, sems = refs
        local = before_ref[...]
    else:
        rows_hbm, after_ref, rows_ref, sems = refs
        local = jnp.full(after_ref.shape, -1.0, jnp.float32)
    capacity = received[0].shape[0]
    rest = rows_ref.shape[2] - LANES
    me = lax.axis_index("grp")
    lane = lax.broadcasted_iota(jnp.int32, local.shape, 1)
    for k, ref in zip(away, received):
        first = lax.bitwise_xor(me, k) * capacity
        for p in range(capacity):
            local = jnp.where(lane == first + p, ref[p].astype(jnp.float32)[24:32, 127:128], local)
    copies = []
    if last:
        count = ids_ref.shape[1]
        owned = local[0:1, :count].astype(jnp.int32)
        group = lax.broadcasted_iota(jnp.int32, (1, count), 1) // capacity
        start = (group * lax.axis_size("row") + lax.axis_index("row")) * elements
        ids_ref[...] = jnp.where(owned >= 0, start + owned, -1)
        copies.append(pltpu.make_async_copy(ids_ref, ids_hbm, sems.at[len(away)]))
        copies[-1].start()
    else:
        after_ref[...] = local
    for i, (k, ref) in enumerate(zip(away, received)):
        for p in range(capacity):
            block = ref[p].astype(jnp.float32)
            tail = block[24:32]
            rows_ref[i * capacity + p] = jnp.concatenate(
                [
                    block[0:24],
                    jnp.concatenate([tail[:, rest * q : rest * (q + 1)] for q in range(3)], axis=0),
                ],
                axis=1,
            ).astype(jnp.bfloat16)
        first = lax.bitwise_xor(me, k) * capacity
        copies.append(
            pltpu.make_async_copy(
                rows_ref.at[pl.ds(i * capacity, capacity)], rows_hbm.at[pl.ds(first, capacity)], sems.at[i]
            )
        )
        copies[-1].start()
    for copy in copies:
        copy.wait()


def on_device(stiffness, lame, prolong, columns, ghost_count, ghost_offset, owner_map):
    elements, coarse, fine = prolong.shape
    slots = stiffness.shape[0]
    ghosts = elements // 2
    owners = lax.axis_size("grp")
    capacity = 2 * ((elements + owners - 1) // owners)
    run = pltpu.VMEM((ghosts // 2, 3 * coarse, LANES), jnp.bfloat16)
    depth = pl.cdiv(fine, 2 * LANES) * 2 * LANES
    by_odd, by_even, own = pl.pallas_call(
        pack_kernel,
        out_shape=(run, run, pltpu.VMEM(prolong.shape, jnp.bfloat16)),
        in_specs=[HBM] * 3, out_specs=(VMEM,) * 3,
        scratch_shapes=[
            pltpu.SMEM(ghost_count.shape, jnp.int32),
            pltpu.SMEM(ghost_offset.shape, jnp.int32),
            pltpu.SemaphoreType.DMA((3,)),
        ],
        compiler_params=params(), name="pack",
    )(in_hbm(ghost_count), in_hbm(ghost_offset), in_hbm(prolong))
    from_even = swapped(by_even, 0)
    from_odd = swapped(by_odd, 1)
    own = in_vmem(own.reshape(elements * coarse, fine))
    left, order, by_slot = pl.pallas_call(
        functools.partial(left_kernel, capacity),
        out_shape=(
            pltpu.VMEM((elements, slots, 2 * coarse, depth), jnp.bfloat16),
            pltpu.SMEM((owners * capacity,), jnp.int32),
            pltpu.SMEM((slots, elements), jnp.int32),
        ),
        in_specs=[HBM] * 4 + [VMEM], out_specs=(VMEM, SMEM, SMEM),
        scratch_shapes=[
            pltpu.SMEM((slots, 2, elements), jnp.float32),
            pltpu.SMEM((1, elements), jnp.int32),
            pltpu.VMEM(stiffness.shape, jnp.bfloat16),
            pltpu.SMEM((owners,), jnp.int32),
            pltpu.SemaphoreType.DMA((4,)),
        ],
        compiler_params=params(), name="left",
    )(in_hbm(lame.transpose(1, 2, 0)), in_hbm(owner_map.T), in_hbm(columns.T), in_hbm(stiffness), own)
    sends = pl.pallas_call(
        rows_kernel,
        out_shape=[pltpu.VMEM((capacity, 32, LANES), jnp.bfloat16)] * owners,
        in_specs=[SMEM, SMEM, VMEM, VMEM, VMEM, VMEM], out_specs=[VMEM] * owners,
        scratch_shapes=[
            pltpu.VMEM((elements + 2 * ghosts + 1, coarse, depth), jnp.float32),
            pltpu.VMEM((elements + 1, 32, LANES), jnp.bfloat16),
        ],
        compiler_params=params(), name="rows",
    )(
        in_smem(by_slot), in_smem(order), own,
        in_vmem(from_even), in_vmem(from_odd), in_vmem(left),
    )
    received = {0: sends[0]}
    for k in [*range(2, owners), 1]:
        received[k] = lax.ppermute(sends[k], "grp", [(i, i ^ k) for i in range(owners)])
    received = {k: in_vmem(value) for k, value in received.items()}
    rows = jax.ShapeDtypeStruct((owners * capacity, coarse, slots * coarse), jnp.bfloat16)
    wide = pl.cdiv(owners * capacity, LANES) * LANES

    def scratch(blocks):
        return pltpu.VMEM((blocks * capacity, coarse, slots * coarse), jnp.bfloat16)

    early, late = [*range(2, owners - 1), 0], [owners - 1, 1]
    partial, local = pl.pallas_call(
        functools.partial(unpack_kernel, elements, early, False),
        out_shape=(pltpu.HBM(rows.shape, rows.dtype), pltpu.VMEM((8, wide), jnp.float32)),
        in_specs=[VMEM] * len(early), out_specs=(HBM, VMEM),
        scratch_shapes=[scratch(len(early)), pltpu.SemaphoreType.DMA((len(early),))],
        compiler_params=params(), name="unpack_early",
    )(*[received[k] for k in early])
    coarse_rows, ids = pl.pallas_call(
        functools.partial(unpack_kernel, elements, late, True),
        out_shape=(rows, jax.ShapeDtypeStruct((1, owners * capacity), jnp.int32)),
        in_specs=[VMEM] * len(late) + [HBM, VMEM], out_specs=(HBM, HBM),
        scratch_shapes=[
            scratch(len(late)),
            pltpu.VMEM((1, owners * capacity), jnp.int32),
            pltpu.SemaphoreType.DMA((len(late) + 1,)),
        ],
        input_output_aliases={len(late): 0},
        compiler_params=params(), name="unpack_late",
    )(*[received[k] for k in late], in_hbm(partial), in_vmem(local))
    return (coarse_rows, ids.reshape(-1))


def solution(mesh):
    split = ("grp", "row")
    return jax.shard_map(
        on_device, mesh=mesh,
        in_specs=(P(), P(split, None, None), P(split, None, None)) + (P(split, None),) * 4,
        out_specs=(P(split, None, None), P(split)), check_vma=False,
    )
```

```python
import functools

import jax
import jax.numpy as jnp
from jax import lax
from jax.experimental import pallas as pl
from jax.experimental.pallas import tpu as pltpu
from jax.sharding import PartitionSpec as P

LANES = 128
VMEM = pl.BlockSpec(memory_space=pltpu.VMEM)
HBM = pl.BlockSpec(memory_space=pltpu.HBM)
SMEM = pl.BlockSpec(memory_space=pltpu.SMEM)


def in_vmem(value):
    return pltpu.with_memory_space_constraint(value, pltpu.VMEM)


def in_smem(value):
    return pltpu.with_memory_space_constraint(value, pltpu.SMEM)


def in_hbm(value):
    return pltpu.with_memory_space_constraint(value, pltpu.HBM)


def params():
    return pltpu.CompilerParams(vmem_limit_bytes=24 * 1024 * 1024)


def swapped(value, parity):
    rows = lax.axis_size("row")
    pairs = []
    for group in range(lax.axis_size("grp")):
        for row in range(rows):
            other = row + 1 if row % 2 == parity else row - 1
            there = (group, other) if 0 <= other < rows else (group ^ 1, row)
            pairs.append((group * rows + row, there[0] * rows + there[1]))
    return lax.ppermute(value, ("grp", "row"), pairs)


def fetch(pairs, sems):
    copies = [pltpu.make_async_copy(src, dst, sems.at[i]) for i, (src, dst) in enumerate(pairs)]
    for copy in copies:
        copy.start()
    return copies


def pack_kernel(
    count_hbm, offset_hbm, prolong_hbm, odd_ref, even_ref, prolong_ref, count_ref, offset_ref, sems,
):
    for copy in fetch([(prolong_hbm, prolong_ref), (count_hbm, count_ref), (offset_hbm, offset_ref)], sems):
        copy.wait()
    elements = prolong_ref.shape[0]
    odd_row = lax.rem(lax.axis_index("row"), 2)
    for way, out_ref in ((odd_row, odd_ref), (1 - odd_row, even_ref)):
        first = offset_ref[0, way]
        length = count_ref[0, way]

        def block(slot):
            value = prolong_ref[jnp.minimum(first + slot, elements - 1)].astype(jnp.float32)
            return jnp.where(slot < length, value, 0.0)

        for pair in range(out_ref.shape[0]):
            even, odd = block(2 * pair), block(2 * pair + 1)
            tail = jnp.concatenate([even[:, LANES:], odd[:, LANES:]], axis=1)
            out_ref[pair] = jnp.concatenate(
                [even[:, :LANES], odd[:, :LANES], tail], axis=0
            ).astype(jnp.bfloat16)


def left_kernel(
    capacity, lame_hbm, owner_hbm, columns_hbm, stiffness_hbm, prolong_ref, left_ref, order_ref, columns_ref, table_ref,
    lame_ref, owner_ref, stiffness_ref, filled, sems,
):
    elements, slots, rows, _ = left_ref.shape
    coarse = rows // 2
    copies = fetch(
        [(owner_hbm, owner_ref), (lame_hbm, lame_ref), (columns_hbm, columns_ref), (stiffness_hbm, stiffness_ref)],
        sems,
    )
    copies[0].wait()
    me = lax.axis_index("grp")
    for t in range(filled.shape[0]):
        filled[t] = 0
    for i in range(order_ref.shape[0]):
        order_ref[i] = elements
    for e in range(elements):
        away = lax.bitwise_xor(owner_ref[0, e], me)
        position = filled[away]
        filled[away] = position + 1
        order_ref[away * capacity + position] = e

    for copy in copies[1:]:
        copy.wait()
    own = prolong_ref[...]
    spare = jnp.zeros((rows, left_ref.shape[3] - own.shape[1]), jnp.float32)
    for e in range(elements):
        block = own[e * coarse : (e + 1) * coarse].astype(jnp.float32)
        table_ref[e] = jnp.concatenate([block, spare[:coarse]], axis=1)
    table_ref[table_ref.shape[0] - 1] = jnp.zeros(table_ref.shape[1:], jnp.float32)
    for s in range(slots):
        first = jnp.dot(own, stiffness_ref[s, 0], preferred_element_type=jnp.float32)
        second = jnp.dot(own, stiffness_ref[s, 1], preferred_element_type=jnp.float32)
        for e in range(elements):
            part = slice(e * coarse, (e + 1) * coarse)
            total = lame_ref[s, 0, e] * first[part] + lame_ref[s, 1, e] * second[part]
            high = total.astype(jnp.bfloat16).astype(jnp.float32)
            both = jnp.concatenate([high, total - high], axis=0)
            left_ref[e, s] = jnp.concatenate([both, spare], axis=1).astype(jnp.bfloat16)


def rows_kernel(columns_ref, order_ref, even_ref, odd_ref, left_ref, _, *refs):
    sends, (table, packed) = refs[:-2], refs[-2:]
    elements, slots, rows, depth = left_ref.shape
    coarse = rows // 2
    half = LANES // 2
    spare = jnp.zeros((coarse, depth - LANES - half), jnp.float32)
    ghosts = 2 * odd_ref.shape[0]
    row, last = lax.axis_index("row"), lax.axis_size("row") - 1
    capacity = sends[0].shape[0]
    for parity, ref in enumerate((even_ref, odd_ref)):
        from_above = lax.rem(row, 2) == parity
        start = jnp.where(from_above, elements + ghosts, elements)
        has_partner = jnp.where(from_above, row < last, row > 0)
        for pair in range(ghosts // 2):
            block = jnp.where(has_partner, ref[pair].astype(jnp.float32), 0.0)
            tail = block[2 * coarse :]
            for odd in range(2):
                table[start + 2 * pair + odd] = jnp.concatenate(
                    [block[odd * coarse : (odd + 1) * coarse], tail[:, odd * half : (odd + 1) * half], spare], axis=1
                )

    lane8 = lax.broadcasted_iota(jnp.int32, (8, LANES), 1)
    packed[elements] = jnp.concatenate(
        [jnp.zeros((coarse, LANES), jnp.float32), jnp.where(lane8 >= 120, -1.0, 0.0)], axis=0
    ).astype(jnp.bfloat16)

    width = slots * coarse
    lane = lax.broadcasted_iota(jnp.int32, (coarse, width), 1)
    for e in range(elements):
        blocks = []
        for s in range(slots):
            c = columns_ref[s, e]
            blocks.append(table[jnp.where(c < 0, elements + 2 * ghosts, c)])
        right = jnp.concatenate(blocks, axis=0).astype(jnp.bfloat16)
        left = left_ref[e].reshape(slots * 2 * coarse, depth)
        product = lax.dot_general(
            left, right, (((1,), (1,)), ((), ())), preferred_element_type=jnp.float32
        )
        result = None
        for s in range(slots):
            at = 2 * coarse * s
            part = product[at : at + coarse] + product[at + coarse : at + 2 * coarse]
            result = part if s == 0 else jnp.where(lane >= s * coarse, part, result)
        rest = result[:, LANES:]
        spare = jnp.full((8, 8), e, jnp.float32)
        tail = jnp.concatenate([rest[0:8], rest[8:16], rest[16:24], spare], axis=1)
        packed[e] = jnp.concatenate([result[:, :LANES], tail], axis=0).astype(jnp.bfloat16)
    for k, send in enumerate(sends):
        for p in range(capacity):
            send[p] = packed[order_ref[k * capacity + p]]


def unpack_kernel(elements, away, last, *refs):
    received, refs = refs[: len(away)], refs[len(away) :]
    if last:
        _, before_ref, rows_hbm, ids_hbm, rows_ref, ids_ref, sems = refs
        local = before_ref[...]
    else:
        rows_hbm, after_ref, rows_ref, sems = refs
        local = jnp.full(after_ref.shape, -1.0, jnp.float32)
    capacity = received[0].shape[0]
    rest = rows_ref.shape[2] - LANES
    me = lax.axis_index("grp")
    lane = lax.broadcasted_iota(jnp.int32, local.shape, 1)
    for k, ref in zip(away, received):
        first = lax.bitwise_xor(me, k) * capacity
        for p in range(capacity):
            local = jnp.where(lane == first + p, ref[p].astype(jnp.float32)[24:32, 127:128], local)
    copies = []
    if last:
        count = ids_ref.shape[1]
        owned = local[0:1, :count].astype(jnp.int32)
        group = lax.broadcasted_iota(jnp.int32, (1, count), 1) // capacity
        start = (group * lax.axis_size("row") + lax.axis_index("row")) * elements
        ids_ref[...] = jnp.where(owned >= 0, start + owned, -1)
        copies.append(pltpu.make_async_copy(ids_ref, ids_hbm, sems.at[len(away)]))
        copies[-1].start()
    else:
        after_ref[...] = local
    for i, (k, ref) in enumerate(zip(away, received)):
        for p in range(capacity):
            block = ref[p].astype(jnp.float32)
            tail = block[24:32]
            rows_ref[i * capacity + p] = jnp.concatenate(
                [
                    block[0:24],
                    jnp.concatenate([tail[:, rest * q : rest * (q + 1)] for q in range(3)], axis=0),
                ],
                axis=1,
            ).astype(jnp.bfloat16)
        first = lax.bitwise_xor(me, k) * capacity
        copies.append(
            pltpu.make_async_copy(
                rows_ref.at[pl.ds(i * capacity, capacity)], rows_hbm.at[pl.ds(first, capacity)], sems.at[i]
            )
        )
        copies[-1].start()
    for copy in copies:
        copy.wait()


def on_device(stiffness, lame, prolong, columns, ghost_count, ghost_offset, owner_map):
    elements, coarse, fine = prolong.shape
    slots = stiffness.shape[0]
    ghosts = elements // 2
    owners = lax.axis_size("grp")
    capacity = 2 * ((elements + owners - 1) // owners)
    run = pltpu.VMEM((ghosts // 2, 3 * coarse, LANES), jnp.bfloat16)
    depth = pl.cdiv(fine, 2 * LANES) * 2 * LANES
    by_odd, by_even, own = pl.pallas_call(
        pack_kernel,
        out_shape=(run, run, pltpu.VMEM(prolong.shape, jnp.bfloat16)),
        in_specs=[HBM] * 3, out_specs=(VMEM,) * 3,
        scratch_shapes=[
            pltpu.SMEM(ghost_count.shape, jnp.int32),
            pltpu.SMEM(ghost_offset.shape, jnp.int32),
            pltpu.SemaphoreType.DMA((3,)),
        ],
        compiler_params=params(), name="pack",
    )(in_hbm(ghost_count), in_hbm(ghost_offset), in_hbm(prolong))
    from_even = swapped(by_even, 0)
    from_odd = swapped(by_odd, 1)
    own = in_vmem(own.reshape(elements * coarse, fine))
    table = pltpu.VMEM((elements + 2 * ghosts + 1, coarse, depth), jnp.float32)
    left, order, by_slot, local_table = pl.pallas_call(
        functools.partial(left_kernel, capacity),
        out_shape=(
            pltpu.VMEM((elements, slots, 2 * coarse, depth), jnp.bfloat16),
            pltpu.SMEM((owners * capacity,), jnp.int32),
            pltpu.SMEM((slots, elements), jnp.int32),
            table,
        ),
        in_specs=[HBM] * 4 + [VMEM], out_specs=(VMEM, SMEM, SMEM, VMEM),
        scratch_shapes=[
            pltpu.SMEM((slots, 2, elements), jnp.float32),
            pltpu.SMEM((1, elements), jnp.int32),
            pltpu.VMEM(stiffness.shape, jnp.bfloat16),
            pltpu.SMEM((owners,), jnp.int32),
            pltpu.SemaphoreType.DMA((4,)),
        ],
        compiler_params=params(), name="left",
    )(in_hbm(lame.transpose(1, 2, 0)), in_hbm(owner_map.T), in_hbm(columns.T), in_hbm(stiffness), own)
    *sends, _ = pl.pallas_call(
        rows_kernel,
        out_shape=[pltpu.VMEM((capacity, 32, LANES), jnp.bfloat16)] * owners + [table],
        in_specs=[SMEM, SMEM, VMEM, VMEM, VMEM, VMEM], out_specs=[VMEM] * (owners + 1),
        scratch_shapes=[pltpu.VMEM((elements + 1, 32, LANES), jnp.bfloat16)],
        input_output_aliases={5: owners},
        compiler_params=params(), name="rows",
    )(
        in_smem(by_slot), in_smem(order), in_vmem(from_even), in_vmem(from_odd), in_vmem(left), in_vmem(local_table),
    )
    received = {0: sends[0]}
    for k in [*range(2, owners), 1]:
        received[k] = lax.ppermute(sends[k], "grp", [(i, i ^ k) for i in range(owners)])
    received = {k: in_vmem(value) for k, value in received.items()}
    rows = jax.ShapeDtypeStruct((owners * capacity, coarse, slots * coarse), jnp.bfloat16)
    wide = pl.cdiv(owners * capacity, LANES) * LANES

    def scratch(blocks):
        return pltpu.VMEM((blocks * capacity, coarse, slots * coarse), jnp.bfloat16)

    early, late = [*range(2, owners - 1), 0], [owners - 1, 1]
    partial, local = pl.pallas_call(
        functools.partial(unpack_kernel, elements, early, False),
        out_shape=(pltpu.HBM(rows.shape, rows.dtype), pltpu.VMEM((8, wide), jnp.float32)),
        in_specs=[VMEM] * len(early), out_specs=(HBM, VMEM),
        scratch_shapes=[scratch(len(early)), pltpu.SemaphoreType.DMA((len(early),))],
        compiler_params=params(), name="unpack_early",
    )(*[received[k] for k in early])
    coarse_rows, ids = pl.pallas_call(
        functools.partial(unpack_kernel, elements, late, True),
        out_shape=(rows, jax.ShapeDtypeStruct((1, owners * capacity), jnp.int32)),
        in_specs=[VMEM] * len(late) + [HBM, VMEM], out_specs=(HBM, HBM),
        scratch_shapes=[
            scratch(len(late)),
            pltpu.VMEM((1, owners * capacity), jnp.int32),
            pltpu.SemaphoreType.DMA((len(late) + 1,)),
        ],
        input_output_aliases={len(late): 0},
        compiler_params=params(), name="unpack_late",
    )(*[received[k] for k in late], in_hbm(partial), in_vmem(local))
    return (coarse_rows, ids.reshape(-1))


def solution(mesh):
    split = ("grp", "row")
    return jax.shard_map(
        on_device, mesh=mesh,
        in_specs=(P(), P(split, None, None), P(split, None, None)) + (P(split, None),) * 4,
        out_specs=(P(split, None, None), P(split)), check_vma=False,
    )
```

```python
import functools

import jax
import jax.numpy as jnp
from jax import lax
from jax.experimental import pallas as pl
from jax.experimental.pallas import tpu as pltpu
from jax.sharding import PartitionSpec as P

LANES = 128
VMEM = pl.BlockSpec(memory_space=pltpu.VMEM)
HBM = pl.BlockSpec(memory_space=pltpu.HBM)
SMEM = pl.BlockSpec(memory_space=pltpu.SMEM)


def in_vmem(value):
    return pltpu.with_memory_space_constraint(value, pltpu.VMEM)


def in_smem(value):
    return pltpu.with_memory_space_constraint(value, pltpu.SMEM)


def in_hbm(value):
    return pltpu.with_memory_space_constraint(value, pltpu.HBM)


def params():
    return pltpu.CompilerParams(vmem_limit_bytes=24 * 1024 * 1024)


def swapped(value, parity):
    rows = lax.axis_size("row")
    pairs = []
    for group in range(lax.axis_size("grp")):
        for row in range(rows):
            other = row + 1 if row % 2 == parity else row - 1
            there = (group, other) if 0 <= other < rows else (group ^ 1, row)
            pairs.append((group * rows + row, there[0] * rows + there[1]))
    return lax.ppermute(value, ("grp", "row"), pairs)


def fetch(pairs, sems):
    copies = [pltpu.make_async_copy(src, dst, sems.at[i]) for i, (src, dst) in enumerate(pairs)]
    for copy in copies:
        copy.start()
    return copies


def pack_kernel(
    count_hbm, offset_hbm, prolong_hbm, odd_ref, even_ref, prolong_ref, count_ref, offset_ref, sems,
):
    for copy in fetch([(prolong_hbm, prolong_ref), (count_hbm, count_ref), (offset_hbm, offset_ref)], sems):
        copy.wait()
    elements = prolong_ref.shape[0]
    odd_row = lax.rem(lax.axis_index("row"), 2)
    for way, out_ref in ((odd_row, odd_ref), (1 - odd_row, even_ref)):
        first = offset_ref[0, way]
        length = count_ref[0, way]

        def block(slot):
            value = prolong_ref[jnp.minimum(first + slot, elements - 1)].astype(jnp.float32)
            return jnp.where(slot < length, value, 0.0)

        for pair in range(out_ref.shape[0]):
            even, odd = block(2 * pair), block(2 * pair + 1)
            tail = jnp.concatenate([even[:, LANES:], odd[:, LANES:]], axis=1)
            out_ref[pair] = jnp.concatenate(
                [even[:, :LANES], odd[:, :LANES], tail], axis=0
            ).astype(jnp.bfloat16)


def left_kernel(
    capacity, lame_hbm, owner_hbm, columns_hbm, stiffness_hbm, prolong_ref, left_ref, order_ref, columns_ref, table_ref,
    lame_ref, owner_ref, stiffness_ref, filled, sems,
):
    elements, slots, rows, _ = left_ref.shape
    coarse = rows // 2
    copies = fetch(
        [(owner_hbm, owner_ref), (lame_hbm, lame_ref), (columns_hbm, columns_ref), (stiffness_hbm, stiffness_ref)],
        sems,
    )
    copies[0].wait()
    me = lax.axis_index("grp")
    for t in range(filled.shape[0]):
        filled[t] = 0
    for i in range(order_ref.shape[0]):
        order_ref[i] = elements
    for e in range(elements):
        away = lax.bitwise_xor(owner_ref[0, e], me)
        position = filled[away]
        filled[away] = position + 1
        order_ref[away * capacity + position] = e

    for copy in copies[1:]:
        copy.wait()
    own = prolong_ref[...]
    spare = jnp.zeros((rows, left_ref.shape[3] - own.shape[1]), jnp.float32)
    for e in range(elements):
        block = own[e * coarse : (e + 1) * coarse].astype(jnp.float32)
        table_ref[e] = jnp.concatenate([block, spare[:coarse]], axis=1)
    table_ref[table_ref.shape[0] - 1] = jnp.zeros(table_ref.shape[1:], jnp.float32)
    for s in range(slots):
        first = jnp.dot(own, stiffness_ref[s, 0], preferred_element_type=jnp.float32)
        second = jnp.dot(own, stiffness_ref[s, 1], preferred_element_type=jnp.float32)
        for e in range(elements):
            part = slice(e * coarse, (e + 1) * coarse)
            total = lame_ref[s, 0, e] * first[part] + lame_ref[s, 1, e] * second[part]
            high = total.astype(jnp.bfloat16).astype(jnp.float32)
            both = jnp.concatenate([high, total - high], axis=0)
            left_ref[e, s] = jnp.concatenate([both, spare], axis=1).astype(jnp.bfloat16)


def rows_kernel(columns_ref, order_ref, even_ref, odd_ref, left_ref, _, *refs):
    sends, (table, packed) = refs[:-2], refs[-2:]
    elements, slots, rows, depth = left_ref.shape
    coarse = rows // 2
    half = LANES // 2
    spare = jnp.zeros((coarse, depth - LANES - half), jnp.float32)
    ghosts = 2 * odd_ref.shape[0]
    row, last = lax.axis_index("row"), lax.axis_size("row") - 1
    capacity = sends[0].shape[0]
    for parity, ref in enumerate((even_ref, odd_ref)):
        from_above = lax.rem(row, 2) == parity
        start = jnp.where(from_above, elements + ghosts, elements)
        has_partner = jnp.where(from_above, row < last, row > 0)
        for pair in range(ghosts // 2):
            block = jnp.where(has_partner, ref[pair].astype(jnp.float32), 0.0)
            tail = block[2 * coarse :]
            for odd in range(2):
                table[start + 2 * pair + odd] = jnp.concatenate(
                    [block[odd * coarse : (odd + 1) * coarse], tail[:, odd * half : (odd + 1) * half], spare], axis=1
                )

    lane8 = lax.broadcasted_iota(jnp.int32, (8, LANES), 1)
    packed[elements] = jnp.concatenate(
        [jnp.zeros((coarse, LANES), jnp.float32), jnp.where(lane8 >= 120, -1.0, 0.0)], axis=0
    ).astype(jnp.bfloat16)

    width = slots * coarse
    lane = lax.broadcasted_iota(jnp.int32, (coarse, width), 1)
    for e in range(elements):
        blocks = []
        for s in range(slots):
            c = columns_ref[s, e]
            blocks.append(table[jnp.where(c < 0, elements + 2 * ghosts, c)])
        right = jnp.concatenate(blocks, axis=0).astype(jnp.bfloat16)
        left = left_ref[e].reshape(slots * 2 * coarse, depth)
        product = lax.dot_general(
            left, right, (((1,), (1,)), ((), ())), preferred_element_type=jnp.float32
        )
        sides = []
        for side in (slice(0, LANES), slice(LANES, width)):
            result = None
            for s in range(slots):
                if s * coarse < side.stop and (s + 1) * coarse > side.start:
                    at = 2 * coarse * s
                    part = product[at : at + coarse, side] + product[at + coarse : at + 2 * coarse, side]
                    result = part if result is None else jnp.where(lane[:, side] >= s * coarse, part, result)
            sides.append(result)
        rest = sides[1]
        spare = jnp.full((8, 8), e, jnp.float32)
        tail = jnp.concatenate([rest[0:8], rest[8:16], rest[16:24], spare], axis=1)
        packed[e] = jnp.concatenate([sides[0], tail], axis=0).astype(jnp.bfloat16)
    for k, send in enumerate(sends):
        for p in range(capacity):
            send[p] = packed[order_ref[k * capacity + p]]


def unpack_kernel(elements, away, last, *refs):
    received, refs = refs[: len(away)], refs[len(away) :]
    if last:
        _, before_ref, rows_hbm, ids_hbm, rows_ref, ids_ref, sems = refs
        local = before_ref[...]
    else:
        rows_hbm, after_ref, rows_ref, sems = refs
        local = jnp.full(after_ref.shape, -1.0, jnp.float32)
    capacity = received[0].shape[0]
    rest = rows_ref.shape[2] - LANES
    me = lax.axis_index("grp")
    lane = lax.broadcasted_iota(jnp.int32, local.shape, 1)
    for k, ref in zip(away, received):
        first = lax.bitwise_xor(me, k) * capacity
        for p in range(capacity):
            local = jnp.where(lane == first + p, ref[p].astype(jnp.float32)[24:32, 127:128], local)
    copies = []
    if last:
        count = ids_ref.shape[1]
        owned = local[0:1, :count].astype(jnp.int32)
        group = lax.broadcasted_iota(jnp.int32, (1, count), 1) // capacity
        start = (group * lax.axis_size("row") + lax.axis_index("row")) * elements
        ids_ref[...] = jnp.where(owned >= 0, start + owned, -1)
        copies.append(pltpu.make_async_copy(ids_ref, ids_hbm, sems.at[len(away)]))
        copies[-1].start()
    else:
        after_ref[...] = local
    for i, (k, ref) in enumerate(zip(away, received)):
        for p in range(capacity):
            block = ref[p].astype(jnp.float32)
            tail = block[24:32]
            rows_ref[i * capacity + p] = jnp.concatenate(
                [
                    block[0:24],
                    jnp.concatenate([tail[:, rest * q : rest * (q + 1)] for q in range(3)], axis=0),
                ],
                axis=1,
            ).astype(jnp.bfloat16)
        first = lax.bitwise_xor(me, k) * capacity
        copies.append(
            pltpu.make_async_copy(
                rows_ref.at[pl.ds(i * capacity, capacity)], rows_hbm.at[pl.ds(first, capacity)], sems.at[i]
            )
        )
        copies[-1].start()
    for copy in copies:
        copy.wait()


def on_device(stiffness, lame, prolong, columns, ghost_count, ghost_offset, owner_map):
    elements, coarse, fine = prolong.shape
    slots = stiffness.shape[0]
    ghosts = elements // 2
    owners = lax.axis_size("grp")
    capacity = 2 * ((elements + owners - 1) // owners)
    run = pltpu.VMEM((ghosts // 2, 3 * coarse, LANES), jnp.bfloat16)
    depth = pl.cdiv(fine, 2 * LANES) * 2 * LANES
    by_odd, by_even, own = pl.pallas_call(
        pack_kernel,
        out_shape=(run, run, pltpu.VMEM(prolong.shape, jnp.bfloat16)),
        in_specs=[HBM] * 3, out_specs=(VMEM,) * 3,
        scratch_shapes=[
            pltpu.SMEM(ghost_count.shape, jnp.int32),
            pltpu.SMEM(ghost_offset.shape, jnp.int32),
            pltpu.SemaphoreType.DMA((3,)),
        ],
        compiler_params=params(), name="pack",
    )(in_hbm(ghost_count), in_hbm(ghost_offset), in_hbm(prolong))
    from_even = swapped(by_even, 0)
    from_odd = swapped(by_odd, 1)
    own = in_vmem(own.reshape(elements * coarse, fine))
    table = pltpu.VMEM((elements + 2 * ghosts + 1, coarse, depth), jnp.float32)
    left, order, by_slot, local_table = pl.pallas_call(
        functools.partial(left_kernel, capacity),
        out_shape=(
            pltpu.VMEM((elements, slots, 2 * coarse, depth), jnp.bfloat16),
            pltpu.SMEM((owners * capacity,), jnp.int32),
            pltpu.SMEM((slots, elements), jnp.int32),
            table,
        ),
        in_specs=[HBM] * 4 + [VMEM], out_specs=(VMEM, SMEM, SMEM, VMEM),
        scratch_shapes=[
            pltpu.SMEM((slots, 2, elements), jnp.float32),
            pltpu.SMEM((1, elements), jnp.int32),
            pltpu.VMEM(stiffness.shape, jnp.bfloat16),
            pltpu.SMEM((owners,), jnp.int32),
            pltpu.SemaphoreType.DMA((4,)),
        ],
        compiler_params=params(), name="left",
    )(in_hbm(lame.transpose(1, 2, 0)), in_hbm(owner_map.T), in_hbm(columns.T), in_hbm(stiffness), own)
    *sends, _ = pl.pallas_call(
        rows_kernel,
        out_shape=[pltpu.VMEM((capacity, 32, LANES), jnp.bfloat16)] * owners + [table],
        in_specs=[SMEM, SMEM, VMEM, VMEM, VMEM, VMEM], out_specs=[VMEM] * (owners + 1),
        scratch_shapes=[pltpu.VMEM((elements + 1, 32, LANES), jnp.bfloat16)],
        input_output_aliases={5: owners},
        compiler_params=params(), name="rows",
    )(
        in_smem(by_slot), in_smem(order), in_vmem(from_even), in_vmem(from_odd), in_vmem(left), in_vmem(local_table),
    )
    received = {0: sends[0]}
    for k in [*range(2, owners), 1]:
        received[k] = lax.ppermute(sends[k], "grp", [(i, i ^ k) for i in range(owners)])
    received = {k: in_vmem(value) for k, value in received.items()}
    rows = jax.ShapeDtypeStruct((owners * capacity, coarse, slots * coarse), jnp.bfloat16)
    wide = pl.cdiv(owners * capacity, LANES) * LANES

    def scratch(blocks):
        return pltpu.VMEM((blocks * capacity, coarse, slots * coarse), jnp.bfloat16)

    early, late = [*range(2, owners - 1), 0], [owners - 1, 1]
    partial, local = pl.pallas_call(
        functools.partial(unpack_kernel, elements, early, False),
        out_shape=(pltpu.HBM(rows.shape, rows.dtype), pltpu.VMEM((8, wide), jnp.float32)),
        in_specs=[VMEM] * len(early), out_specs=(HBM, VMEM),
        scratch_shapes=[scratch(len(early)), pltpu.SemaphoreType.DMA((len(early),))],
        compiler_params=params(), name="unpack_early",
    )(*[received[k] for k in early])
    coarse_rows, ids = pl.pallas_call(
        functools.partial(unpack_kernel, elements, late, True),
        out_shape=(rows, jax.ShapeDtypeStruct((1, owners * capacity), jnp.int32)),
        in_specs=[VMEM] * len(late) + [HBM, VMEM], out_specs=(HBM, HBM),
        scratch_shapes=[
            scratch(len(late)),
            pltpu.VMEM((1, owners * capacity), jnp.int32),
            pltpu.SemaphoreType.DMA((len(late) + 1,)),
        ],
        input_output_aliases={len(late): 0},
        compiler_params=params(), name="unpack_late",
    )(*[received[k] for k in late], in_hbm(partial), in_vmem(local))
    return (coarse_rows, ids.reshape(-1))


def solution(mesh):
    split = ("grp", "row")
    return jax.shard_map(
        on_device, mesh=mesh,
        in_specs=(P(), P(split, None, None), P(split, None, None)) + (P(split, None),) * 4,
        out_specs=(P(split, None, None), P(split)), check_vma=False,
    )
```

```python
import functools

import jax
import jax.numpy as jnp
from jax import lax
from jax.experimental import pallas as pl
from jax.experimental.pallas import tpu as pltpu
from jax.sharding import PartitionSpec as P

LANES = 128
VMEM = pl.BlockSpec(memory_space=pltpu.VMEM)
HBM = pl.BlockSpec(memory_space=pltpu.HBM)
SMEM = pl.BlockSpec(memory_space=pltpu.SMEM)


def in_vmem(value):
    return pltpu.with_memory_space_constraint(value, pltpu.VMEM)


def in_smem(value):
    return pltpu.with_memory_space_constraint(value, pltpu.SMEM)


def in_hbm(value):
    return pltpu.with_memory_space_constraint(value, pltpu.HBM)


def params():
    return pltpu.CompilerParams(vmem_limit_bytes=24 * 1024 * 1024)


def swapped(value, parity):
    rows = lax.axis_size("row")
    pairs = []
    for group in range(lax.axis_size("grp")):
        for row in range(rows):
            other = row + 1 if row % 2 == parity else row - 1
            there = (group, other) if 0 <= other < rows else (group ^ 1, row)
            pairs.append((group * rows + row, there[0] * rows + there[1]))
    return lax.ppermute(value, ("grp", "row"), pairs)


def fetch(pairs, sems):
    copies = [pltpu.make_async_copy(src, dst, sems.at[i]) for i, (src, dst) in enumerate(pairs)]
    for copy in copies:
        copy.start()
    return copies


def pack_kernel(
    count_hbm, offset_hbm, prolong_hbm, odd_ref, even_ref, prolong_ref, count_ref, offset_ref, sems,
):
    for copy in fetch([(prolong_hbm, prolong_ref), (count_hbm, count_ref), (offset_hbm, offset_ref)], sems):
        copy.wait()
    elements = prolong_ref.shape[0]
    odd_row = lax.rem(lax.axis_index("row"), 2)
    for way, out_ref in ((odd_row, odd_ref), (1 - odd_row, even_ref)):
        first = offset_ref[0, way]
        length = count_ref[0, way]

        def block(slot):
            value = prolong_ref[jnp.minimum(first + slot, elements - 1)].astype(jnp.float32)
            return jnp.where(slot < length, value, 0.0)

        for pair in range(out_ref.shape[0]):
            even, odd = block(2 * pair), block(2 * pair + 1)
            tail = jnp.concatenate([even[:, LANES:], odd[:, LANES:]], axis=1)
            out_ref[pair] = jnp.concatenate(
                [even[:, :LANES], odd[:, :LANES], tail], axis=0
            ).astype(jnp.bfloat16)


def left_kernel(
    capacity, lame_hbm, owner_hbm, columns_hbm, stiffness_hbm, prolong_ref, left_ref, order_ref, columns_ref,
    lame_ref, owner_ref, stiffness_ref, filled, sems,
):
    elements, slots, rows, _ = left_ref.shape
    coarse = rows // 2
    copies = fetch(
        [(owner_hbm, owner_ref), (lame_hbm, lame_ref), (columns_hbm, columns_ref), (stiffness_hbm, stiffness_ref)],
        sems,
    )
    copies[0].wait()
    me = lax.axis_index("grp")
    for t in range(filled.shape[0]):
        filled[t] = 0
    for i in range(order_ref.shape[0]):
        order_ref[i] = elements
    for e in range(elements):
        away = lax.bitwise_xor(owner_ref[0, e], me)
        position = filled[away]
        filled[away] = position + 1
        order_ref[away * capacity + position] = e

    for copy in copies[1:]:
        copy.wait()
    own = prolong_ref[...]
    spare = jnp.zeros((rows, left_ref.shape[3] - own.shape[1]), jnp.float32)
    for s in range(slots):
        first = jnp.dot(own, stiffness_ref[s, 0], preferred_element_type=jnp.float32)
        second = jnp.dot(own, stiffness_ref[s, 1], preferred_element_type=jnp.float32)
        for e in range(elements):
            part = slice(e * coarse, (e + 1) * coarse)
            total = lame_ref[s, 0, e] * first[part] + lame_ref[s, 1, e] * second[part]
            high = total.astype(jnp.bfloat16).astype(jnp.float32)
            both = jnp.concatenate([high, total - high], axis=0)
            left_ref[e, s] = jnp.concatenate([both, spare], axis=1).astype(jnp.bfloat16)


def rows_kernel(columns_ref, order_ref, prolong_ref, even_ref, odd_ref, left_ref, *refs):
    sends, (table, packed) = refs[:-2], refs[-2:]
    elements, slots, rows, depth = left_ref.shape
    coarse, fine = rows // 2, prolong_ref.shape[1]
    spare = jnp.zeros((coarse, depth - fine), jnp.float32)
    ghosts = 2 * odd_ref.shape[0]
    row, last = lax.axis_index("row"), lax.axis_size("row") - 1
    half = fine - LANES
    capacity = sends[0].shape[0]
    for e in range(elements):
        own = prolong_ref[e * coarse : (e + 1) * coarse].astype(jnp.float32)
        table[e] = jnp.concatenate([own, spare], axis=1)
    for parity, ref in enumerate((even_ref, odd_ref)):
        from_above = lax.rem(row, 2) == parity
        start = jnp.where(from_above, elements + ghosts, elements)
        has_partner = jnp.where(from_above, row < last, row > 0)
        for pair in range(ghosts // 2):
            block = jnp.where(has_partner, ref[pair].astype(jnp.float32), 0.0)
            tail = block[2 * coarse :]
            for odd in range(2):
                table[start + 2 * pair + odd] = jnp.concatenate(
                    [block[odd * coarse : (odd + 1) * coarse], tail[:, odd * half : (odd + 1) * half], spare], axis=1
                )
    table[elements + 2 * ghosts] = jnp.zeros((coarse, depth), jnp.float32)

    lane8 = lax.broadcasted_iota(jnp.int32, (8, LANES), 1)
    packed[elements] = jnp.concatenate(
        [jnp.zeros((coarse, LANES), jnp.float32), jnp.where(lane8 >= 120, -1.0, 0.0)], axis=0
    ).astype(jnp.bfloat16)

    width = slots * coarse
    lane = lax.broadcasted_iota(jnp.int32, (coarse, width), 1)
    for e in range(elements):
        blocks = []
        for s in range(slots):
            c = columns_ref[s, e]
            blocks.append(table[jnp.where(c < 0, elements + 2 * ghosts, c)])
        right = jnp.concatenate(blocks, axis=0).astype(jnp.bfloat16)
        left = left_ref[e].reshape(slots * 2 * coarse, depth)
        product = lax.dot_general(
            left, right, (((1,), (1,)), ((), ())), preferred_element_type=jnp.float32
        )
        result = None
        for s in range(slots):
            at = 2 * coarse * s
            part = product[at : at + coarse] + product[at + coarse : at + 2 * coarse]
            result = part if s == 0 else jnp.where(lane >= s * coarse, part, result)
        rest = result[:, LANES:]
        spare = jnp.full((8, 8), e, jnp.float32)
        tail = jnp.concatenate([rest[0:8], rest[8:16], rest[16:24], spare], axis=1)
        packed[e] = jnp.concatenate([result[:, :LANES], tail], axis=0).astype(jnp.bfloat16)
    for k, send in enumerate(sends):
        for p in range(capacity):
            send[p] = packed[order_ref[k * capacity + p]]


def unpack_kernel(elements, away, last, *refs):
    received, refs = refs[: len(away)], refs[len(away) :]
    if last:
        _, before_ref, rows_hbm, ids_hbm, rows_ref, ids_ref, sems = refs
        local = before_ref[...]
    else:
        rows_hbm, after_ref, rows_ref, sems = refs
        local = jnp.full(after_ref.shape, -1.0, jnp.float32)
    capacity = received[0].shape[0]
    rest = rows_ref.shape[2] - LANES
    me = lax.axis_index("grp")
    lane = lax.broadcasted_iota(jnp.int32, local.shape, 1)
    copies = []
    for i, (k, ref) in enumerate(zip(away, received)):
        for p in range(capacity):
            block = ref[p].astype(jnp.float32)
            tail = block[24:32]
            rows_ref[i * capacity + p] = jnp.concatenate(
                [
                    block[0:24],
                    jnp.concatenate([tail[:, rest * q : rest * (q + 1)] for q in range(3)], axis=0),
                ],
                axis=1,
            ).astype(jnp.bfloat16)
        first = lax.bitwise_xor(me, k) * capacity
        copies.append(
            pltpu.make_async_copy(
                rows_ref.at[pl.ds(i * capacity, capacity)], rows_hbm.at[pl.ds(first, capacity)], sems.at[i]
            )
        )
        copies[-1].start()
    for k, ref in zip(away, received):
        first = lax.bitwise_xor(me, k) * capacity
        for p in range(capacity):
            local = jnp.where(lane == first + p, ref[p].astype(jnp.float32)[24:32, 127:128], local)
    if last:
        count = ids_ref.shape[1]
        owned = local[0:1, :count].astype(jnp.int32)
        group = lax.broadcasted_iota(jnp.int32, (1, count), 1) // capacity
        start = (group * lax.axis_size("row") + lax.axis_index("row")) * elements
        ids_ref[...] = jnp.where(owned >= 0, start + owned, -1)
        copies.append(pltpu.make_async_copy(ids_ref, ids_hbm, sems.at[len(away)]))
        copies[-1].start()
    else:
        after_ref[...] = local
    for copy in copies:
        copy.wait()


def on_device(stiffness, lame, prolong, columns, ghost_count, ghost_offset, owner_map):
    elements, coarse, fine = prolong.shape
    slots = stiffness.shape[0]
    ghosts = elements // 2
    owners = lax.axis_size("grp")
    capacity = 2 * ((elements + owners - 1) // owners)
    run = pltpu.VMEM((ghosts // 2, 3 * coarse, LANES), jnp.bfloat16)
    depth = pl.cdiv(fine, 2 * LANES) * 2 * LANES
    by_odd, by_even, own = pl.pallas_call(
        pack_kernel,
        out_shape=(run, run, pltpu.VMEM(prolong.shape, jnp.bfloat16)),
        in_specs=[HBM] * 3, out_specs=(VMEM,) * 3,
        scratch_shapes=[
            pltpu.SMEM(ghost_count.shape, jnp.int32),
            pltpu.SMEM(ghost_offset.shape, jnp.int32),
            pltpu.SemaphoreType.DMA((3,)),
        ],
        compiler_params=params(), name="pack",
    )(in_hbm(ghost_count), in_hbm(ghost_offset), in_hbm(prolong))
    from_even = swapped(by_even, 0)
    from_odd = swapped(by_odd, 1)
    own = in_vmem(own.reshape(elements * coarse, fine))
    left, order, by_slot = pl.pallas_call(
        functools.partial(left_kernel, capacity),
        out_shape=(
            pltpu.VMEM((elements, slots, 2 * coarse, depth), jnp.bfloat16),
            pltpu.SMEM((owners * capacity,), jnp.int32),
            pltpu.SMEM((slots, elements), jnp.int32),
        ),
        in_specs=[HBM] * 4 + [VMEM], out_specs=(VMEM, SMEM, SMEM),
        scratch_shapes=[
            pltpu.SMEM((slots, 2, elements), jnp.float32),
            pltpu.SMEM((1, elements), jnp.int32),
            pltpu.VMEM(stiffness.shape, jnp.bfloat16),
            pltpu.SMEM((owners,), jnp.int32),
            pltpu.SemaphoreType.DMA((4,)),
        ],
        compiler_params=params(), name="left",
    )(in_hbm(lame.transpose(1, 2, 0)), in_hbm(owner_map.T), in_hbm(columns.T), in_hbm(stiffness), own)
    sends = pl.pallas_call(
        rows_kernel,
        out_shape=[pltpu.VMEM((capacity, 32, LANES), jnp.bfloat16)] * owners,
        in_specs=[SMEM, SMEM, VMEM, VMEM, VMEM, VMEM], out_specs=[VMEM] * owners,
        scratch_shapes=[
            pltpu.VMEM((elements + 2 * ghosts + 1, coarse, depth), jnp.float32),
            pltpu.VMEM((elements + 1, 32, LANES), jnp.bfloat16),
        ],
        compiler_params=params(), name="rows",
    )(
        in_smem(by_slot), in_smem(order), own,
        in_vmem(from_even), in_vmem(from_odd), in_vmem(left),
    )
    received = {0: sends[0]}
    for k in [*range(2, owners), 1]:
        received[k] = lax.ppermute(sends[k], "grp", [(i, i ^ k) for i in range(owners)])
    received = {k: in_vmem(value) for k, value in received.items()}
    rows = jax.ShapeDtypeStruct((owners * capacity, coarse, slots * coarse), jnp.bfloat16)
    wide = pl.cdiv(owners * capacity, LANES) * LANES

    def scratch(blocks):
        return pltpu.VMEM((blocks * capacity, coarse, slots * coarse), jnp.bfloat16)

    early, late = [*range(2, owners - 1), 0], [owners - 1, 1]
    partial, local = pl.pallas_call(
        functools.partial(unpack_kernel, elements, early, False),
        out_shape=(pltpu.HBM(rows.shape, rows.dtype), pltpu.VMEM((8, wide), jnp.float32)),
        in_specs=[VMEM] * len(early), out_specs=(HBM, VMEM),
        scratch_shapes=[scratch(len(early)), pltpu.SemaphoreType.DMA((len(early),))],
        compiler_params=params(), name="unpack_early",
    )(*[received[k] for k in early])
    coarse_rows, ids = pl.pallas_call(
        functools.partial(unpack_kernel, elements, late, True),
        out_shape=(rows, jax.ShapeDtypeStruct((1, owners * capacity), jnp.int32)),
        in_specs=[VMEM] * len(late) + [HBM, VMEM], out_specs=(HBM, HBM),
        scratch_shapes=[
            scratch(len(late)),
            pltpu.VMEM((1, owners * capacity), jnp.int32),
            pltpu.SemaphoreType.DMA((len(late) + 1,)),
        ],
        input_output_aliases={len(late): 0},
        compiler_params=params(), name="unpack_late",
    )(*[received[k] for k in late], in_hbm(partial), in_vmem(local))
    return (coarse_rows, ids.reshape(-1))


def solution(mesh):
    split = ("grp", "row")
    return jax.shard_map(
        on_device, mesh=mesh,
        in_specs=(P(), P(split, None, None), P(split, None, None)) + (P(split, None),) * 4,
        out_specs=(P(split, None, None), P(split)), check_vma=False,
    )
```
